32 devices in a mesh: batch: 4 (over z), seq: 8 (over y, x, core).
Axes of the slice: x: 2, y: 2, z: 4, core: 2. Of those that a mesh axis runs over, the one named last changes fastest.
Arguments:
- tokens: bfloat16 [24, 1024, 960], P('batch', 'seq'), may hold values from -6 to 6
- segment_ids: int32 [24, 1024], P('batch', 'seq'), may hold values from 0 to 5, as said below
- position_ids: int32 [24, 1024], P('batch', 'seq'), may hold values from 0 to 1023, as said below
- cotangent: bfloat16 [24, 1024, 960], P('batch', 'seq'), may hold values from -6 to 6
- query_base: bfloat16 [960, 960], replicated, may hold values from -0.1875 to 0.1875
- key_base: bfloat16 [960, 320], replicated, may hold values from -0.1875 to 0.1875
- value_base: bfloat16 [960, 320], replicated, may hold values from -0.1875 to 0.1875
- output_base: bfloat16 [960, 960], replicated, may hold values from -1.5 to 1.5
- gate_base: bfloat16 [960, 2560], replicated, may hold values from -0.1875 to 0.1875
- upper_base: bfloat16 [960, 2560], replicated, may hold values from -0.1875 to 0.1875
- lower_base: bfloat16 [2560, 960], replicated, may hold values from -0.125 to 0.125
- query_left: bfloat16 [960, 16], replicated, may hold values from -0.1875 to 0.1875
- key_left: bfloat16 [960, 16], replicated, may hold values from -0.1875 to 0.1875
- value_left: bfloat16 [960, 16], replicated, may hold values from -0.1875 to 0.1875
- output_left: bfloat16 [960, 16], replicated, may hold values from -0.1875 to 0.1875
- gate_left: bfloat16 [960, 16], replicated, may hold values from -0.1875 to 0.1875
- upper_left: bfloat16 [960, 16], replicated, may hold values from -0.1875 to 0.1875
- lower_left: bfloat16 [2560, 16], replicated, may hold values from -0.125 to 0.125
- query_right: bfloat16 [16, 960], replicated, may hold values from -0.375 to 0.375
- key_right: bfloat16 [16, 320], replicated, may hold values from -0.375 to 0.375
- value_right: bfloat16 [16, 320], replicated, may hold values from -0.375 to 0.375
- output_right: bfloat16 [16, 960], replicated, may hold values from -0.375 to 0.375
- gate_right: bfloat16 [16, 2560], replicated, may hold values from -0.375 to 0.375
- upper_right: bfloat16 [16, 2560], replicated, may hold values from -0.375 to 0.375
- lower_right: bfloat16 [16, 960], replicated, may hold values from -0.375 to 0.375
- query_magnitude: float32 [960], replicated, may hold values from 0.5 to 2
- key_magnitude: float32 [320], replicated, may hold values from 0.5 to 2
- value_magnitude: float32 [320], replicated, may hold values from 0.5 to 2
- output_magnitude: float32 [960], replicated, may hold values from 0.5 to 2
- gate_magnitude: float32 [2560], replicated, may hold values from 0.5 to 2
- upper_magnitude: float32 [2560], replicated, may hold values from 0.5 to 2
- lower_magnitude: float32 [960], replicated, may hold values from 0.5 to 2
Outputs:
- layer_out: bfloat16 [24, 1024, 960], P('batch', 'seq')
- tokens_grad: bfloat16 [24, 1024, 960], P('batch', 'seq')
- query_left_grad: float32 [960, 16], replicated
- key_left_grad: float32 [960, 16], replicated
- value_left_grad: float32 [960, 16], replicated
- output_left_grad: float32 [960, 16], replicated
- gate_left_grad: float32 [960, 16], replicated
- upper_left_grad: float32 [960, 16], replicated
- lower_left_grad: float32 [2560, 16], replicated
- query_right_grad: float32 [16, 960], replicated
- key_right_grad: float32 [16, 320], replicated
- value_right_grad: float32 [16, 320], replicated
- output_right_grad: float32 [16, 960], replicated
- gate_right_grad: float32 [16, 2560], replicated
- upper_right_grad: float32 [16, 2560], replicated
- lower_right_grad: float32 [16, 960], replicated
- query_magnitude_grad: float32 [960], replicated
- key_magnitude_grad: float32 [320], replicated
- value_magnitude_grad: float32 [320], replicated
- output_magnitude_grad: float32 [960], replicated
- gate_magnitude_grad: float32 [2560], replicated
- upper_magnitude_grad: float32 [2560], replicated
- lower_magnitude_grad: float32 [960], replicated
The draws below stay inside these ranges and needn't reach their ends.
Inputs may be any that keep to these rules, and one draw needn't show every extreme that they name: `segment_ids`: along each row the segment ids start at 0 and never fall; in each aligned group of 6 rows one row, drawn from the seed, is a single segment, and every other row holds exactly six segments. `position_ids`: each token's index within its segment.
All inputs are finite; a program needn't handle non-finite values.
Results may differ from the reference program's by a relative error of at most 0.024.
Values may be sent and summed in bfloat16 or wider, within the bound.
No kernel may reach another device: no remote copies, remote signals or barrier semaphores. Data moves between devices by JAX's collectives and lax.ppermute only.
A program may use at most 512 MiB of HBM per device.

```python
import math
import jax
import jax.numpy as jnp
from jax import lax

D = 960
FF = 2560
HEADS = 15
KV_HEADS = 5
HEAD = 64
RANK = 16
ROWS_DEV = 6
GROUP = 3
LENGTH = 1024
ROWS = 24


def segment_layout(key):
    row_keys = jax.random.split(jax.random.fold_in(key, 1), ROWS)
    cuts = jax.vmap(lambda row_key: jax.random.permutation(row_key, LENGTH - 1)[:5] + 1)(row_keys).astype(jnp.int32)
    offsets = jnp.arange(LENGTH, dtype=jnp.int32)
    boundary = jnp.any(offsets[None, :, None] == cuts[:, None, :], axis=-1)
    chosen = jax.random.randint(jax.random.fold_in(key, 2), (ROWS // ROWS_DEV,), 0, ROWS_DEV)
    whole_row = jnp.arange(ROWS) % ROWS_DEV == jnp.repeat(chosen, ROWS_DEV)
    boundary = boundary & jnp.logical_not(whole_row)[:, None]
    segments = jnp.cumsum(boundary.astype(jnp.int32), axis=1).astype(jnp.int32)
    opening = jnp.where(boundary | (offsets == 0)[None, :], offsets[None, :], 0).astype(jnp.int32)
    latest = lax.cummax(opening, axis=1)
    return (segments, (offsets[None, :] - latest).astype(jnp.int32))


def draw_segment_ids(key, part):
    layout = segment_layout(key)
    return layout[0]


def draw_position_ids(key, part):
    layout = segment_layout(key)
    return layout[1]


def block_levels(key, dims, cuts, least, top_value):
    def one(position, parts):
        heights = jax.random.uniform(jax.random.fold_in(jax.random.fold_in(key, 6), position), (parts,), jnp.float32, least / len(cuts), top_value / len(cuts))
        return jnp.repeat(jnp.exp(heights), dims[position] // parts).reshape((-1,) + (1,) * (len(dims) - position - 1))

    factor_of = one(*cuts[0])
    for cut in cuts[1:]:
        factor_of = factor_of * one(*cut)
    return factor_of


def scatter_about(stream_key, shape, deviation, most, shards=(), held_as=jnp.bfloat16):
    level = block_levels(stream_key, shape, shards, -0.22, 0.18) if shards else 1.0
    array = jax.random.normal(stream_key, shape, jnp.float32) * deviation * level
    return jnp.minimum(jnp.maximum(array, -most), most).astype(held_as)


def setup_inputs(seed: int = 0) -> dict:
    key_list = jax.random.split(jax.random.key(seed), 33)
    return {
        "tokens": scatter_about(key_list[0], (ROWS, LENGTH, D), 1.0, 6.0, ((0, 4), (1, 8))),
        "segment_ids": draw_segment_ids(jax.random.fold_in(key_list[32], 71), 0),
        "position_ids": draw_position_ids(jax.random.fold_in(key_list[32], 71), 0),
        "cotangent": scatter_about(key_list[3], (ROWS, LENGTH, D), 1.0, 6.0, ((0, 4), (1, 8))),
        "query_base": scatter_about(key_list[4], (D, HEADS * HEAD), D ** -0.5, 0.1875),
        "key_base": scatter_about(key_list[5], (D, KV_HEADS * HEAD), D ** -0.5, 0.1875),
        "value_base": scatter_about(key_list[6], (D, KV_HEADS * HEAD), D ** -0.5, 0.1875),
        "output_base": scatter_about(key_list[7], (HEADS * HEAD, D), 16 ** -0.5, 1.5),
        "gate_base": scatter_about(key_list[8], (D, FF), D ** -0.5, 0.1875),
        "upper_base": scatter_about(key_list[9], (D, FF), D ** -0.5, 0.1875),
        "lower_base": scatter_about(key_list[10], (FF, D), FF ** -0.5, 0.125),
        "query_left": scatter_about(key_list[11], (D, RANK), D ** -0.5, 0.1875),
        "key_left": scatter_about(key_list[12], (D, RANK), D ** -0.5, 0.1875),
        "value_left": scatter_about(key_list[13], (D, RANK), D ** -0.5, 0.1875),
        "output_left": scatter_about(key_list[14], (HEADS * HEAD, RANK), (HEADS * HEAD) ** -0.5, 0.1875),
        "gate_left": scatter_about(key_list[15], (D, RANK), D ** -0.5, 0.1875),
        "upper_left": scatter_about(key_list[16], (D, RANK), D ** -0.5, 0.1875),
        "lower_left": scatter_about(key_list[17], (FF, RANK), FF ** -0.5, 0.125),
        "query_right": scatter_about(key_list[18], (RANK, HEADS * HEAD), (16 * RANK) ** -0.5, 0.375),
        "key_right": scatter_about(key_list[19], (RANK, KV_HEADS * HEAD), (16 * RANK) ** -0.5, 0.375),
        "value_right": scatter_about(key_list[20], (RANK, KV_HEADS * HEAD), (16 * RANK) ** -0.5, 0.375),
        "output_right": scatter_about(key_list[21], (RANK, D), (16 * RANK) ** -0.5, 0.375),
        "gate_right": scatter_about(key_list[22], (RANK, FF), (16 * RANK) ** -0.5, 0.375),
        "upper_right": scatter_about(key_list[23], (RANK, FF), (16 * RANK) ** -0.5, 0.375),
        "lower_right": scatter_about(key_list[24], (RANK, D), (16 * RANK) ** -0.5, 0.375),
        "query_magnitude": jnp.clip(jnp.exp(jax.random.uniform(key_list[25], (HEADS * HEAD,), jnp.float32, math.log(0.5), math.log(2.0))), 0.5, 2.0),
        "key_magnitude": jnp.clip(jnp.exp(jax.random.uniform(key_list[26], (KV_HEADS * HEAD,), jnp.float32, math.log(0.5), math.log(2.0))), 0.5, 2.0),
        "value_magnitude": jnp.clip(jnp.exp(jax.random.uniform(key_list[27], (KV_HEADS * HEAD,), jnp.float32, math.log(0.5), math.log(2.0))), 0.5, 2.0),
        "output_magnitude": jnp.clip(jnp.exp(jax.random.uniform(key_list[28], (D,), jnp.float32, math.log(0.5), math.log(2.0))), 0.5, 2.0),
        "gate_magnitude": jnp.clip(jnp.exp(jax.random.uniform(key_list[29], (FF,), jnp.float32, math.log(0.5), math.log(2.0))), 0.5, 2.0),
        "upper_magnitude": jnp.clip(jnp.exp(jax.random.uniform(key_list[30], (FF,), jnp.float32, math.log(0.5), math.log(2.0))), 0.5, 2.0),
        "lower_magnitude": jnp.clip(jnp.exp(jax.random.uniform(key_list[31], (D,), jnp.float32, math.log(0.5), math.log(2.0))), 0.5, 2.0),
    }


HIGHEST = lax.Precision.HIGHEST
EPSILON = 1e-05
ROTARY_BASE = 100000.0
MASKED = -1e+30
ADAPTER_SCALE = 2.0

@jax.custom_vjp
def low(v):
    return lax.optimization_barrier(v.astype(jnp.bfloat16)).astype(jnp.float32)

@jax.custom_vjp
def low_back(v):
    return v

def low_keep(v):
    return (low(v), None)

def low_pass(kept, grad):
    return (grad,)

def back_keep(v):
    return (v, None)

def back_low(kept, grad):
    return (low(grad),)
low.defvjp(low_keep, low_pass)
low_back.defvjp(back_keep, back_low)

def rms_norm(values):
    return values * lax.rsqrt(lax.optimization_barrier(jnp.mean(values * values, axis=-1, keepdims=True)) + EPSILON)

def rotary_tables(positions):
    half_head = HEAD // 2
    frequency = ROTARY_BASE ** (-(jnp.arange(half_head, dtype=jnp.float32) * 2.0 / HEAD))
    phases = positions.astype(jnp.float32)[..., None] * frequency
    phases = jnp.concatenate([phases, phases], axis=-1)
    return (jnp.cos(phases), jnp.sin(phases))

def rotate(values, cosine, sine_table):
    half_head = values.shape[-1] // 2
    turned = jnp.concatenate([-values[..., half_head:], values[..., :half_head]], axis=-1)
    return values * cosine + turned * sine_table

def column_scale(base, left, right, magnitude):
    combined = base + ADAPTER_SCALE * jnp.dot(left, right, precision=HIGHEST)
    return magnitude / jnp.sqrt(lax.optimization_barrier(jnp.sum(combined * combined, axis=0)))

def project(inputs, base, left, right, column):
    inner_low = low(low_back(jnp.dot(inputs, left, precision=HIGHEST)))
    linear = jnp.dot(inputs, base, precision=HIGHEST) + ADAPTER_SCALE * jnp.dot(inner_low, right, precision=HIGHEST)
    return low_back(linear) * column

def layer_row(token_row, segments, positions, bases, lefts, rights, columns):
    length_now = token_row.shape[0]
    cosine, sine_table = rotary_tables(positions)
    cosine = cosine[:, None, :]
    sine_table = sine_table[:, None, :]
    normed = low(rms_norm(token_row))
    queries = project(normed, bases[0], lefts[0], rights[0], columns[0]).reshape(length_now, HEADS, HEAD)
    key_rows = project(normed, bases[1], lefts[1], rights[1], columns[1]).reshape(length_now, KV_HEADS, HEAD)
    value_rows = project(normed, bases[2], lefts[2], rights[2], columns[2]).reshape(length_now, KV_HEADS, HEAD)
    queries = low(rotate(queries, cosine, sine_table)).reshape(length_now, KV_HEADS, GROUP, HEAD)
    key_rows = low(rotate(key_rows, cosine, sine_table))
    value_rows = low(value_rows)
    raw_scores = jnp.einsum('qghd,kgd->ghqk', queries, key_rows, precision=HIGHEST)
    scores = low_back(raw_scores) * HEAD ** (-0.5)
    places = jnp.arange(length_now)
    allowed = (segments[:, None] == segments[None, :]) & (places[:, None] >= places[None, :])
    logits = jnp.where(allowed, scores, MASKED)
    shifted = jnp.exp(logits - lax.optimization_barrier(jnp.max(logits, axis=-1, keepdims=True)))
    probs = low(shifted / lax.optimization_barrier(jnp.sum(shifted, axis=-1, keepdims=True)))
    mixed = jnp.einsum('ghqk,kgd->qghd', probs, value_rows, precision=HIGHEST).reshape(length_now, HEADS * HEAD)
    mixed = low(low_back(mixed))
    middle = token_row + project(mixed, bases[3], lefts[3], rights[3], columns[3])
    normed_two = low(rms_norm(middle))
    gate_rows = project(normed_two, bases[4], lefts[4], rights[4], columns[4])
    upper_rows = project(normed_two, bases[5], lefts[5], rights[5], columns[5])
    activated = low(jax.nn.silu(gate_rows) * upper_rows)
    return middle + project(activated, bases[6], lefts[6], rights[6], columns[6])

def reference(tokens, segment_ids, position_ids, cotangent, query_base, key_base, value_base, output_base, gate_base, upper_base, lower_base, query_left, key_left, value_left, output_left, gate_left, upper_left, lower_left, query_right, key_right, value_right, output_right, gate_right, upper_right, lower_right, query_magnitude, key_magnitude, value_magnitude, output_magnitude, gate_magnitude, upper_magnitude, lower_magnitude):
    bases = [weight.astype(jnp.float32) for weight in (query_base, key_base, value_base, output_base, gate_base, upper_base, lower_base)]
    start_lefts = [weight.astype(jnp.float32) for weight in (query_left, key_left, value_left, output_left, gate_left, upper_left, lower_left)]
    start_rights = [weight.astype(jnp.float32) for weight in (query_right, key_right, value_right, output_right, gate_right, upper_right, lower_right)]
    start_magnitudes = [weight.astype(jnp.float32) for weight in (query_magnitude, key_magnitude, value_magnitude, output_magnitude, gate_magnitude, upper_magnitude, lower_magnitude)]

    def forward(token_all, lefts, rights, magnitudes):
        columns = [column_scale(bases[which], lefts[which], rights[which], magnitudes[which]) for which in range(7)]

        def step(carried, element):
            return (carried, layer_row(element[0], element[1], element[2], bases, lefts, rights, columns))
        return lax.scan(jax.checkpoint(step), jnp.zeros((), jnp.float32), (token_all, segment_ids, position_ids))[1]
    result, pullback = jax.vjp(forward, tokens.astype(jnp.float32), start_lefts, start_rights, start_magnitudes)
    input_grad, left_grads, right_grads, magnitude_grads = pullback(cotangent.astype(jnp.float32))
    return (result.astype(jnp.bfloat16), input_grad.astype(jnp.bfloat16), left_grads[0], left_grads[1], left_grads[2], left_grads[3], left_grads[4], left_grads[5], left_grads[6], right_grads[0], right_grads[1], right_grads[2], right_grads[3], right_grads[4], right_grads[5], right_grads[6], magnitude_grads[0], magnitude_grads[1], magnitude_grads[2], magnitude_grads[3], magnitude_grads[4], magnitude_grads[5], magnitude_grads[6])
```

```python
from functools import partial

import jax
import jax.numpy as jnp
from jax import lax
from jax.experimental import pallas as pl
from jax.experimental.pallas import tpu as pltpu
from jax.sharding import PartitionSpec as P

HEADS = 15
KV_HEADS = 5
HEAD = 64
GROUP = 3
RANK = 16
EPSILON = 1e-05
ROTARY_BASE = 100000.0
MASKED = -1e30
ADAPTER_SCALE = 2.0
HEAD_SCALE = HEAD**-0.5
VMEM_LIMIT = 58 * 2**20

bf16 = jnp.bfloat16
f32 = jnp.float32


def dot_nn(a, b):
    return lax.dot_general(a, b, (((1,), (0,)), ((), ())), preferred_element_type=f32)


def dot_tn(a, b):
    return lax.dot_general(a, b, (((0,), (0,)), ((), ())), preferred_element_type=f32)


def dot_nt(a, b):
    return lax.dot_general(a, b, (((1,), (1,)), ((), ())), preferred_element_type=f32)


def full(shape):
    zeros = (0,) * len(shape)
    return pl.BlockSpec(shape, lambda *_: zeros)


def lead(shape, index):
    place = (index,) + (0,) * len(shape)
    return pl.BlockSpec((None,) + shape, lambda *_: place)


def smem():
    return pl.BlockSpec(memory_space=pltpu.SMEM)


def hbm():
    return pl.BlockSpec(memory_space=pl.ANY)


def params():
    return pltpu.CompilerParams(vmem_limit_bytes=VMEM_LIMIT)


def cost(flops, read):
    return pl.CostEstimate(flops=int(flops), bytes_accessed=int(read), transcendentals=0)


def eye(size):
    return lax.broadcasted_iota(jnp.int32, (size, size), 0) == lax.broadcasted_iota(
        jnp.int32, (size, size), 1
    )


def chunks(total, step=128):
    return [(start, min(step, total - start)) for start in range(0, total, step)]


def column_to_row(column):
    parts = []
    for start, size in chunks(column.shape[0]):
        parts.append(
            jnp.sum(jnp.where(eye(size), column[start : start + size], 0.0), axis=0, keepdims=True)
        )
    return parts[0] if len(parts) == 1 else jnp.concatenate(parts, axis=1)


def row_to_column(row):
    parts = []
    for start, size in chunks(row.shape[1]):
        parts.append(
            jnp.sum(jnp.where(eye(size), row[:, start : start + size], 0.0), axis=1, keepdims=True)
        )
    return parts[0] if len(parts) == 1 else jnp.concatenate(parts, axis=0)


def prepare_natural(base_ref, left_ref, right_ref, magnitude_ref, weight_ref, right_out, norm_ref):
    combined = base_ref[...].astype(f32) + ADAPTER_SCALE * dot_tn(left_ref[...], right_ref[...])
    norm = jnp.sqrt(jnp.sum(combined * combined, axis=0, keepdims=True))
    column = magnitude_ref[...] / norm
    weight_ref[...] = (combined * column).astype(bf16)
    right_out[...] = (ADAPTER_SCALE * column * right_ref[...].astype(f32)).astype(bf16)
    norm_ref[...] = norm


def prepare_turned(base_ref, left_ref, right_ref, magnitude_ref, weight_ref, right_out, norm_ref):
    combined = base_ref[...].astype(f32) + ADAPTER_SCALE * dot_tn(right_ref[...], left_ref[...])
    norm = jnp.sqrt(jnp.sum(combined * combined, axis=1, keepdims=True))
    norm_row = column_to_row(norm)
    column = magnitude_ref[...] / norm_row
    weight_ref[...] = (combined * row_to_column(column)).astype(bf16)
    right_out[...] = (ADAPTER_SCALE * column * right_ref[...].astype(f32)).astype(bf16)
    norm_ref[...] = norm_row


def prepare(base, left, right, magnitude, turned, step):
    out_size = right.shape[1]
    in_size = left.shape[1]
    if turned:
        base_spec = pl.BlockSpec((step, in_size), lambda i: (i, 0))
    else:
        base_spec = pl.BlockSpec((in_size, step), lambda i: (0, i))
    right_spec = pl.BlockSpec((RANK, step), lambda i: (0, i))
    row_spec = pl.BlockSpec((1, step), lambda i: (0, i))
    return pl.pallas_call(
        prepare_turned if turned else prepare_natural,
        grid=(pl.cdiv(out_size, step),),
        in_specs=[base_spec, full(left.shape), right_spec, row_spec],
        out_specs=[base_spec, right_spec, row_spec],
        out_shape=[
            jax.ShapeDtypeStruct(base.shape, bf16),
            jax.ShapeDtypeStruct(right.shape, bf16),
            jax.ShapeDtypeStruct(magnitude.shape, f32),
        ],
        compiler_params=params(),
        cost_estimate=cost(2 * RANK * base.size, 4 * base.size),
    )(base, left, right, magnitude)


def rms_factor(values):
    return lax.rsqrt(jnp.mean(values * values, axis=0, keepdims=True) + EPSILON)


def turn_heads(values, cosine, sine, heads, scale):
    half = HEAD // 2
    out = []
    for head in range(heads):
        first = values[head * HEAD : head * HEAD + half]
        second = values[head * HEAD + half : (head + 1) * HEAD]
        out.append((first * cosine - second * sine) * scale)
        out.append((second * cosine + first * sine) * scale)
    return jnp.concatenate(out, axis=0)


def turn_heads_back(values, cosine, sine, heads, scale):
    half = HEAD // 2
    out = []
    for head in range(heads):
        first = values[head * HEAD : head * HEAD + half]
        second = values[head * HEAD + half : (head + 1) * HEAD]
        out.append((first * cosine + second * sine) * scale)
        out.append((second * cosine - first * sine) * scale)
    return jnp.concatenate(out, axis=0)


def entry_kernel(
    x_ref, cos_ref, sin_ref, wq_ref, wk_ref, wv_ref, aq_ref, ak_ref, av_ref, q_ref, kv_ref, t_ref
):
    x = x_ref[...].astype(f32)
    normed = (x * rms_factor(x)).astype(bf16)
    cosine = cos_ref[...]
    sine = sin_ref[...]
    kv_size = KV_HEADS * HEAD
    query = dot_tn(wq_ref[...], normed)
    key = dot_nn(wk_ref[...], normed)
    kv_ref[kv_size:, :] = dot_nn(wv_ref[...], normed).astype(bf16)
    q_ref[...] = turn_heads(query, cosine, sine, HEADS, HEAD_SCALE).astype(bf16)
    kv_ref[:kv_size, :] = turn_heads(key, cosine, sine, KV_HEADS, 1.0).astype(bf16)
    for which, left in enumerate((aq_ref, ak_ref, av_ref)):
        t_ref[which * RANK : (which + 1) * RANK, :] = dot_nn(left[...], normed).astype(bf16)


def entry(row, x, cosine, sine, weights, lefts):
    _, width, tokens = x.shape
    q_size, kv_size = HEADS * HEAD, KV_HEADS * HEAD
    return pl.pallas_call(
        entry_kernel,
        in_specs=[
            lead((width, tokens), row),
            lead((HEAD // 2, tokens), row),
            lead((HEAD // 2, tokens), row),
        ]
        + [full(w.shape) for w in weights]
        + [full(a.shape) for a in lefts],
        out_specs=[full((q_size, tokens)), full((2 * kv_size, tokens)), full((3 * RANK, tokens))],
        out_shape=[
            jax.ShapeDtypeStruct((q_size, tokens), bf16),
            jax.ShapeDtypeStruct((2 * kv_size, tokens), bf16),
            jax.ShapeDtypeStruct((3 * RANK, tokens), bf16),
        ],
        grid=(1,),
        compiler_params=params(),
        cost_estimate=cost(2 * width * 1600 * tokens, 5e6),
    )(x, cosine, sine, *weights, *lefts)


def lower_back_kernel(dy_ref, wl_ref, cb_ref, dr_ref, dt_ref):
    dy = dy_ref[...]
    dr_ref[...] = dot_tn(wl_ref[...], dy).astype(bf16)
    dt_ref[...] = dot_nn(cb_ref[...], dy).astype(bf16)


def lower_back(dy, weight, right):
    rows, width, tokens = dy.shape
    hidden = weight.shape[1]
    return pl.pallas_call(
        lower_back_kernel,
        grid=(rows,),
        in_specs=[
            pl.BlockSpec((None, width, tokens), lambda i: (i, 0, 0)),
            full(weight.shape),
            full(right.shape),
        ],
        out_specs=[
            pl.BlockSpec((None, hidden, tokens), lambda i: (i, 0, 0)),
            pl.BlockSpec((None, RANK, tokens), lambda i: (i, 0, 0)),
        ],
        out_shape=[
            jax.ShapeDtypeStruct((rows, hidden, tokens), bf16),
            jax.ShapeDtypeStruct((rows, RANK, tokens), bf16),
        ],
        compiler_params=params(),
        cost_estimate=cost(2 * width * hidden * tokens * rows, 10e6),
    )(dy, weight, right)


def write_bias(bias_ref, position, distance):
    size = bias_ref.shape[0]
    key = lax.broadcasted_iota(jnp.int32, (size, size), 0)
    query = lax.broadcasted_iota(jnp.int32, (size, size), 1)
    start = query - position + distance * size
    bias_ref[...] = jnp.where((key >= start) & (key <= query + distance * size), 0.0, MASKED)


def block_distance(chip_ref, step, shards):
    return chip_ref[0] - block_source(chip_ref[0], step, shards)


def block_source(chip, step, shards):
    if shards & (shards - 1) == 0:
        return jnp.bitwise_xor(chip, step)
    return lax.rem(chip + step, shards)


def needed(chip_ref, first_ref, row, step, shards, size):
    distance = block_distance(chip_ref, step, shards)
    return (distance > 0) & (distance * size - first_ref[row] < size)


def attend_kernel(row, shards, chip_ref, first_ref, pos_ref, q_ref, *rest):
    kv_refs, (o_ref, lse_ref, bias_ref, max_ref, sum_ref, acc_ref) = rest[:shards], rest[shards:]
    size = q_ref.shape[-1]

    def visit(kv_ref, opening):
        def head_step(head, carry):
            key = kv_ref[head]
            value = kv_ref[head + KV_HEADS]
            for member in range(GROUP):
                rows = slice(member * HEAD, (member + 1) * HEAD)
                logits = dot_tn(key, q_ref[head, rows, :]) + bias_ref[...]
                top = jnp.max(logits, axis=0, keepdims=True)
                if not opening:
                    before = max_ref[head, member : member + 1, :]
                    top = jnp.maximum(top, before)
                weights = jnp.exp(logits - top)
                total = jnp.sum(weights, axis=0, keepdims=True)
                mixed = dot_nn(value, weights.astype(bf16))
                if not opening:
                    rescale = jnp.exp(before - top)
                    total = total + rescale * sum_ref[head, member : member + 1, :]
                    mixed = mixed + rescale * acc_ref[head, rows, :]
                max_ref[head, member : member + 1, :] = top
                sum_ref[head, member : member + 1, :] = total
                acc_ref[head, rows, :] = mixed
            return carry

        lax.fori_loop(0, KV_HEADS, head_step, 0)

    write_bias(bias_ref, pos_ref[...], 0)
    visit(kv_refs[0], True)
    for step in range(1, shards):

        @pl.when(needed(chip_ref, first_ref, row, step, shards, size))
        def _():
            write_bias(bias_ref, pos_ref[...], block_distance(chip_ref, step, shards))
            visit(kv_refs[step], False)

    for head in range(KV_HEADS):
        for member in range(GROUP):
            rows = slice(member * HEAD, (member + 1) * HEAD)
            total = sum_ref[head, member : member + 1, :]
            o_ref[head, rows, :] = (acc_ref[head, rows, :] / total).astype(bf16)
            lse_ref[head, member : member + 1, :] = max_ref[
                head, member : member + 1, :
            ] + jnp.log(total)


def attend(row, chip, first, position, query, blocks):
    shards = len(blocks)
    tokens = query.shape[-1]
    group = (KV_HEADS, GROUP * HEAD, tokens)
    stats = (KV_HEADS, 8, tokens)
    return pl.pallas_call(
        partial(attend_kernel, row, shards),
        grid=(1,),
        in_specs=[smem(), smem(), lead((1, tokens), row), full(group)]
        + [full(b.shape) for b in blocks],
        out_specs=[full(group), full(stats)],
        out_shape=[jax.ShapeDtypeStruct(group, bf16), jax.ShapeDtypeStruct(stats, f32)],
        scratch_shapes=[
            pltpu.VMEM((tokens, tokens), f32),
            pltpu.VMEM(stats, f32),
            pltpu.VMEM(stats, f32),
            pltpu.VMEM(group, f32),
        ],
        compiler_params=params(),
        cost_estimate=cost(6e9, 3e6),
    )(chip, first, position, query, *blocks)


def attend_back_kernel(
    row, shards, chip_ref, first_ref, pos_ref, q_ref, do_ref, lse_ref, delta_ref, *rest
):
    kv_refs, rest = rest[:shards], rest[shards:]
    dq_ref, dkv_refs, bias_ref = rest[0], rest[1 : 1 + shards], rest[1 + shards]
    size = q_ref.shape[-1]

    def visit(kv_ref, dkv_ref, opening):
        def head_step(head, carry):
            key = kv_ref[head]
            value = kv_ref[head + KV_HEADS]
            queries, upstreams, probs, score_grads = [], [], [], []
            for member in range(GROUP):
                rows = slice(member * HEAD, (member + 1) * HEAD)
                query = q_ref[head, rows, :]
                upstream = do_ref[head, rows, :]
                logits = dot_tn(key, query) + bias_ref[...]
                prob = jnp.exp(logits - lse_ref[head, member : member + 1, :])
                prob_grad = dot_tn(value, upstream)
                score_grad = prob * (prob_grad - delta_ref[head, member : member + 1, :])
                score_grad = score_grad.astype(bf16)
                query_grad = dot_nn(key, score_grad) * HEAD_SCALE
                if not opening:
                    query_grad = query_grad + dq_ref[head, rows, :]
                dq_ref[head, rows, :] = query_grad
                queries.append(query)
                upstreams.append(upstream)
                probs.append(prob.astype(bf16))
                score_grads.append(score_grad)
            dkv_ref[head] = dot_nt(
                jnp.concatenate(queries, axis=1), jnp.concatenate(score_grads, axis=1)
            ).astype(bf16)
            dkv_ref[head + KV_HEADS] = dot_nt(
                jnp.concatenate(upstreams, axis=1), jnp.concatenate(probs, axis=1)
            ).astype(bf16)
            return carry

        lax.fori_loop(0, KV_HEADS, head_step, 0)

    write_bias(bias_ref, pos_ref[...], 0)
    visit(kv_refs[0], dkv_refs[0], True)
    for step in range(1, shards):
        wanted = needed(chip_ref, first_ref, row, step, shards, size)

        @pl.when(wanted)
        def _():
            write_bias(bias_ref, pos_ref[...], block_distance(chip_ref, step, shards))
            visit(kv_refs[step], dkv_refs[step], False)

        @pl.when(jnp.logical_not(wanted))
        def _():
            dkv_refs[step][...] = jnp.zeros(dkv_refs[step].shape, bf16)


def attend_back(row, chip, first, position, query, upstream, lse, delta, blocks):
    shards = len(blocks)
    tokens = query.shape[-1]
    group = (KV_HEADS, GROUP * HEAD, tokens)
    stats = (KV_HEADS, 8, tokens)
    return pl.pallas_call(
        partial(attend_back_kernel, row, shards),
        grid=(1,),
        in_specs=[smem(), smem(), lead((1, tokens), row)]
        + [full(group), full(group), full(stats), full(stats)]
        + [full(b.shape) for b in blocks],
        out_specs=[full(group)] + [full(b.shape) for b in blocks],
        out_shape=[jax.ShapeDtypeStruct(group, f32)]
        + [jax.ShapeDtypeStruct(b.shape, bf16) for b in blocks],
        scratch_shapes=[pltpu.VMEM((tokens, tokens), f32)],
        compiler_params=params(),
        cost_estimate=cost(10e9, 5e6),
    )(chip, first, position, query, upstream, lse, delta, *blocks)


def middle_kernel(
    x_ref,
    dy_ref,
    dr_ref,
    dtl_ref,
    o_ref,
    ao_ref,
    ag_ref,
    au_ref,
    wo_hbm,
    cbo_hbm,
    wg_hbm,
    cbg_hbm,
    wu_hbm,
    cbu_hbm,
    wl_hbm,
    al_hbm,
    out_ref,
    dx1_ref,
    do_ref,
    delta_ref,
    dao_ref,
    dbo_ref,
    dag_ref,
    dau_ref,
    dbg_ref,
    dbu_ref,
    dal_ref,
    dbl_ref,
    so_ref,
    sg_ref,
    su_ref,
    sl_ref,
    wo,
    wg,
    wu,
    wl,
    act,
    dgate,
    dupper,
    sems,
):
    width, tokens = x_ref.shape
    hidden = act.shape[0]

    def fetch(slot, weight, extra, scratch):
        copies = [
            pltpu.make_async_copy(weight, scratch.at[pl.ds(0, width)], sems.at[2 * slot]),
            pltpu.make_async_copy(extra, scratch.at[pl.ds(width, RANK)], sems.at[2 * slot + 1]),
        ]
        for copy in copies:
            copy.start()
        return copies

    copies = [
        fetch(0, wo_hbm, cbo_hbm, wo),
        fetch(1, wg_hbm, cbg_hbm, wg),
        fetch(2, wu_hbm, cbu_hbm, wu),
        fetch(3, wl_hbm, al_hbm, wl),
    ]

    def arrive(slot):
        for copy in copies[slot]:
            copy.wait()

    mixed = o_ref[...]
    arrive(0)
    attn = dot_tn(wo[:width, :], mixed)
    x1 = x_ref[...].astype(f32) + attn
    rho = rms_factor(x1)
    normed = x1 * rho
    normed_low = normed.astype(bf16)
    t_output = dot_nn(ao_ref[...], mixed).astype(bf16)
    t_gate = dot_nn(ag_ref[...], normed_low).astype(bf16)
    t_upper = dot_nn(au_ref[...], normed_low).astype(bf16)
    arrive(1)
    arrive(2)
    step = 512
    for start in range(0, hidden, step):
        rows = slice(start, start + step)
        gate = dot_tn(wg[:width, rows], normed_low)
        upper = dot_tn(wu[:width, rows], normed_low)
        down = dr_ref[rows, :].astype(f32)
        sigmoid = jax.nn.sigmoid(gate)
        silu = gate * sigmoid
        act[rows, :] = (silu * upper).astype(bf16)
        gate_grad = down * upper * sigmoid * (1.0 + gate * (1.0 - sigmoid))
        upper_grad = down * silu
        dgate[rows, :] = gate_grad.astype(bf16)
        dupper[rows, :] = upper_grad.astype(bf16)
        sg_ref[:, rows] = column_to_row(jnp.sum(gate * gate_grad, axis=1, keepdims=True))
        su_ref[:, rows] = column_to_row(jnp.sum(upper * upper_grad, axis=1, keepdims=True))
    arrive(3)
    lower_all = dot_nn(wl[...], act[...])
    lower = lower_all[:width]
    t_lower = lower_all[width:].astype(bf16)
    out = (x1 + lower).astype(bf16)
    out_ref[0] = out[:, : tokens // 2]
    out_ref[1] = out[:, tokens // 2 :]
    dy_low = dy_ref[...]
    dy = dy_low.astype(f32)
    sl_ref[...] = column_to_row(jnp.sum(lower * dy, axis=1, keepdims=True))
    gate_back = dot_nn(wg[...], dgate[...])
    upper_back = dot_nn(wu[...], dupper[...])
    dt_gate = gate_back[width:].astype(bf16)
    dt_upper = upper_back[width:].astype(bf16)
    dnormed = gate_back[:width] + upper_back[:width]
    dx1 = dy + rho * (dnormed - normed * jnp.mean(dnormed * normed, axis=0, keepdims=True))
    dx1_ref[...] = dx1
    dx1_low = dx1.astype(bf16)
    so_ref[...] = column_to_row(jnp.sum(attn * dx1, axis=1, keepdims=True))
    output_back = dot_nn(wo[...], dx1_low)
    dt_output = output_back[width:].astype(bf16)
    dmixed = output_back[:width].astype(bf16)
    do_ref[...] = dmixed
    weighted = dmixed.astype(f32) * mixed.astype(f32)
    for head in range(HEADS):
        delta_ref[head // GROUP, head % GROUP : head % GROUP + 1, :] = jnp.sum(
            weighted[head * HEAD : (head + 1) * HEAD], axis=0, keepdims=True
        )
    dao_ref[...] = dot_nt(dt_output, mixed)
    dbo_ref[...] = dot_nt(t_output, dx1_low)
    dag_ref[...] = dot_nt(dt_gate, normed_low)
    dau_ref[...] = dot_nt(dt_upper, normed_low)
    dbg_ref[...] = dot_nt(t_gate, dgate[...])
    dbu_ref[...] = dot_nt(t_upper, dupper[...])
    dal_ref[...] = dot_nt(dtl_ref[...], act[...])
    dbl_ref[...] = dot_nt(t_lower, dy_low)


def middle(row, x, dy, dr, dt_lower, mixed, lefts, weights):
    _, width, tokens = x.shape
    hidden = dr.shape[1]
    shapes = [
        ((2, width, tokens // 2), bf16),
        ((width, tokens), f32),
        ((width, tokens), bf16),
        ((KV_HEADS, 8, tokens), f32),
        ((RANK, width), f32),
        ((RANK, width), f32),
        ((RANK, width), f32),
        ((RANK, width), f32),
        ((RANK, hidden), f32),
        ((RANK, hidden), f32),
        ((RANK, hidden), f32),
        ((RANK, width), f32),
        ((1, width), f32),
        ((1, hidden), f32),
        ((1, hidden), f32),
        ((1, width), f32),
    ]
    extended = width + RANK
    return pl.pallas_call(
        middle_kernel,
        grid=(1,),
        in_specs=[
            lead((width, tokens), row),
            lead((width, tokens), row),
            lead((hidden, tokens), row),
            lead((RANK, tokens), row),
            full((width, tokens)),
        ]
        + [full(a.shape) for a in lefts]
        + [hbm()] * 8,
        out_specs=[full(s) for s, _ in shapes],
        out_shape=[jax.ShapeDtypeStruct(s, d) for s, d in shapes],
        scratch_shapes=[
            pltpu.VMEM((extended, width), bf16),
            pltpu.VMEM((extended, hidden), bf16),
            pltpu.VMEM((extended, hidden), bf16),
            pltpu.VMEM((extended, hidden), bf16),
            pltpu.VMEM((hidden, tokens), bf16),
            pltpu.VMEM((hidden, tokens), bf16),
            pltpu.VMEM((hidden, tokens), bf16),
            pltpu.SemaphoreType.DMA((8,)),
        ],
        compiler_params=params(),
        cost_estimate=cost(2 * tokens * (2 * width * width + 5 * width * hidden), 20e6),
    )(x, dy, dr, dt_lower, mixed, *lefts, *weights)


def exit_kernel(
    shards,
    x_ref,
    cos_ref,
    sin_ref,
    dx1_ref,
    t_ref,
    q_ref,
    kv_ref,
    dq_ref,
    wq_ref,
    wk_ref,
    wv_ref,
    cbq_ref,
    cbk_ref,
    cbv_ref,
    *rest,
):
    dkv_refs, rest = rest[:shards], rest[shards:]
    dx_ref, da_ref, dbq_ref, dbkv_ref, sq_ref, skv_ref = rest
    tokens = x_ref.shape[1]
    kv_size = KV_HEADS * HEAD
    x = x_ref[...].astype(f32)
    rho = rms_factor(x)
    normed = x * rho
    normed_low = normed.astype(bf16)
    cosine = cos_ref[...]
    sine = sin_ref[...]
    dkv = dkv_refs[0][...].astype(f32)
    for ref in dkv_refs[1:]:
        dkv = dkv + ref[...].astype(f32)
    dquery = turn_heads_back(dq_ref[...], cosine, sine, HEADS, 1.0)
    dkey = turn_heads_back(dkv[:kv_size], cosine, sine, KV_HEADS, 1.0)
    dvalue = dkv[kv_size:]
    query = turn_heads_back(q_ref[...].astype(f32), cosine, sine, HEADS, 1.0 / HEAD_SCALE)
    key = turn_heads_back(kv_ref[:kv_size, :].astype(f32), cosine, sine, KV_HEADS, 1.0)
    value = kv_ref[kv_size:, :].astype(f32)
    sq_ref[...] = column_to_row(jnp.sum(query * dquery, axis=1, keepdims=True))
    skv_ref[0:1, :] = column_to_row(jnp.sum(key * dkey, axis=1, keepdims=True))
    skv_ref[1:2, :] = column_to_row(jnp.sum(value * dvalue, axis=1, keepdims=True))
    dquery = dquery.astype(bf16)
    dkey = dkey.astype(bf16)
    dvalue = dvalue.astype(bf16)
    dnormed = (
        dot_nn(wq_ref[...], dquery) + dot_tn(wk_ref[...], dkey) + dot_tn(wv_ref[...], dvalue)
    )
    dx = dx1_ref[...] + rho * (dnormed - normed * jnp.mean(dnormed * normed, axis=0, keepdims=True))
    dx_low = dx.astype(bf16)
    dx_ref[0] = dx_low[:, : tokens // 2]
    dx_ref[1] = dx_low[:, tokens // 2 :]
    dt = jnp.concatenate(
        [
            dot_nn(cbq_ref[...], dquery),
            dot_nn(cbk_ref[...], dkey),
            dot_nn(cbv_ref[...], dvalue),
        ],
        axis=0,
    ).astype(bf16)
    da_ref[...] = dot_nt(dt, normed_low)
    dbq_ref[...] = dot_nt(t_ref[:RANK, :], dquery)
    dbkv_ref[0] = dot_nt(t_ref[RANK : 2 * RANK, :], dkey)
    dbkv_ref[1] = dot_nt(t_ref[2 * RANK :, :], dvalue)


def leave(row, x, cosine, sine, dx1, inner, query, key_value, dquery, weights, rights, dkvs):
    _, width, tokens = x.shape
    q_size, kv_size = HEADS * HEAD, KV_HEADS * HEAD
    shapes = [
        ((2, width, tokens // 2), bf16),
        ((3 * RANK, width), f32),
        ((RANK, q_size), f32),
        ((2, RANK, kv_size), f32),
        ((1, q_size), f32),
        ((2, kv_size), f32),
    ]
    plain = (
        [dx1, inner, query, key_value, dquery]
        + list(weights)
        + list(rights)
        + [d.reshape(2 * kv_size, tokens) for d in dkvs]
    )
    return pl.pallas_call(
        partial(exit_kernel, len(dkvs)),
        grid=(1,),
        in_specs=[
            lead((width, tokens), row),
            lead((HEAD // 2, tokens), row),
            lead((HEAD // 2, tokens), row),
        ]
        + [full(a.shape) for a in plain],
        out_specs=[full(s) for s, _ in shapes],
        out_shape=[jax.ShapeDtypeStruct(s, d) for s, d in shapes],
        compiler_params=params(),
        cost_estimate=cost(2 * width * 1600 * tokens, 9e6),
    )(x, cosine, sine, *plain)


def settle(sums, weight, turned, left, right, norm, magnitude):
    left_sum, right_sum, stat = sums
    factor = -stat / (magnitude * norm)
    scaled = (ADAPTER_SCALE * factor * right.astype(f32)).astype(bf16)
    if turned:
        left_more = dot_nn(scaled, weight)
        product = dot_nt(left, weight)
    else:
        left_more = dot_nt(scaled, weight)
        product = dot_nn(left, weight)
    right_total = ADAPTER_SCALE * (right_sum * (magnitude / norm) + factor * product)
    return (left_sum + left_more, right_total, stat / magnitude)


STAT = 512


def put_stat(ref, half, row, lane, values):
    size = values.shape[1]
    for start in range(0, size, STAT):
        take = min(STAT, size - start)
        ref[half, row : row + 1, lane : lane + take] = values[:, start : start + take]
        row += 1
    return row


def stack_sum(refs):
    total = refs[0][...]
    for ref in refs[1:]:
        total = total + ref[...]
    return total


def settle_middle_kernel(rows, *refs):
    sums = [
        stack_sum([refs[row * 12 + which] for row in range(rows)]) for which in range(12)
    ]
    refs = refs[rows * 12 :]
    names = ("output", "gate", "upper", "lower")
    groups = {}
    for which, name in enumerate(names):
        groups[name] = [ref for ref in refs[which * 5 : which * 5 + 5]]
    pack = refs[20]
    dao, dbo, dag, dau, dbg, dbu, dal, dbl, so, sg, su, sl = sums
    pieces = {
        "output": (dao, dbo, so),
        "gate": (dag, dbg, sg),
        "upper": (dau, dbu, su),
        "lower": (dal, dbl, sl),
    }
    done = {}
    for name in names:
        weight, left, right, norm, magnitude = groups[name]
        done[name] = settle(
            pieces[name],
            weight[...],
            name == "lower",
            left[...],
            right[...],
            norm[...],
            magnitude[...],
        )
    width = dao.shape[1]
    slot, hidden = slots(width), dbg.shape[1]
    pack[...] = jnp.zeros(pack.shape, f32)
    pack[0, :, 0:hidden] = done["gate"][1]
    pack[0, :, hidden : 2 * hidden] = done["upper"][1]
    pack[0, :, 2 * hidden : 2 * hidden + width] = done["output"][0]
    row = 0
    for name in ("gate", "upper", "output", "lower"):
        row = put_stat(pack, 0, row, 2 * hidden + slot, done[name][2])
    pack[1, :, 0:hidden] = done["lower"][0]
    place = hidden
    for values in (done["output"][1], done["gate"][0], done["upper"][0], done["lower"][1]):
        pack[1, :, place : place + width] = values
        place += slot


def slots(width):
    return -(-width // 128) * 128


def settle_middle(partials, projections):
    hidden = partials[0][4].shape[1]
    width = partials[0][0].shape[1]
    half = 2 * hidden + slots(width) + STAT
    flat = [a for part in partials for a in part] + [a for group in projections for a in group]
    return pl.pallas_call(
        partial(settle_middle_kernel, len(partials)),
        grid=(1,),
        in_specs=[full(a.shape) for a in flat],
        out_specs=full((2, RANK, half)),
        out_shape=jax.ShapeDtypeStruct((2, RANK, half), f32),
        compiler_params=params(),
        cost_estimate=cost(4e9, 24e6),
    )(*flat)


def settle_entry_kernel(rows, *refs):
    sums = [stack_sum([refs[row * 5 + which] for row in range(rows)]) for which in range(5)]
    refs = refs[rows * 5 :]
    da, dbq, dbkv, sq, skv = sums
    pack = refs[15]
    pieces = (
        (da[:RANK], dbq, sq),
        (da[RANK : 2 * RANK], dbkv[0], skv[0:1]),
        (da[2 * RANK :], dbkv[1], skv[1:2]),
    )
    done = []
    for which in range(3):
        weight, left, right, norm, magnitude = refs[which * 5 : which * 5 + 5]
        done.append(
            settle(
                pieces[which],
                weight[...],
                which > 0,
                left[...],
                right[...],
                norm[...],
                magnitude[...],
            )
        )
    width = da.shape[1]
    slot = slots(width)
    kv_size = skv.shape[1]
    pack[...] = jnp.zeros(pack.shape, f32)
    pack[0, :, 0:width] = done[0][0]
    pack[0, :, slot : slot + width] = done[1][0]
    row = 0
    for which in range(3):
        row = put_stat(pack, 0, row, 2 * slot, done[which][2])
    pack[1, :, 0:width] = done[2][0]
    pack[1, :, slot : slot + sq.shape[1]] = done[0][1]
    pack[1, :, 2 * slot : 2 * slot + 2 * kv_size] = jnp.concatenate(
        [done[1][1], done[2][1]], axis=1
    )


def settle_entry(partials, projections):
    width = partials[0][0].shape[1]
    kv_size = partials[0][4].shape[1]
    half = 2 * slots(width) + max(STAT, slots(2 * kv_size))
    flat = [a for part in partials for a in part] + [a for group in projections for a in group]
    return pl.pallas_call(
        partial(settle_entry_kernel, len(partials)),
        grid=(1,),
        in_specs=[full(a.shape) for a in flat],
        out_specs=full((2, RANK, half)),
        out_shape=jax.ShapeDtypeStruct((2, RANK, half), f32),
        compiler_params=params(),
        cost_estimate=cost(1e9, 5e6),
    )(*flat)


def get_stat(value, row, lane, size):
    parts = []
    for start in range(0, size, STAT):
        take = min(STAT, size - start)
        parts.append(value[row : row + 1, lane : lane + take])
        row += 1
    return jnp.concatenate(parts, axis=1) if len(parts) > 1 else parts[0], row


def finish_kernel(width, hidden, kv_size, m0, m1, e0, e1, *outs):
    lefts, rights, stats = outs[:7], outs[7:14], outs[14:]
    slot = slots(width)
    m0, m1, e0, e1 = (ref[...].astype(f32) for ref in (m0, m1, e0, e1))
    rights[4][...] = m0[:, :hidden]
    rights[5][...] = m0[:, hidden : 2 * hidden]
    lefts[3][...] = m0[:, 2 * hidden : 2 * hidden + width]
    row = 0
    for which, size in ((4, hidden), (5, hidden), (3, width), (6, width)):
        stats[which][...], row = get_stat(m0, row, 2 * hidden + slot, size)
    lefts[6][...] = m1[:, :hidden]
    for place, ref in enumerate((rights[3], lefts[4], lefts[5], rights[6])):
        ref[...] = m1[:, hidden + place * slot : hidden + place * slot + width]
    lefts[0][...] = e0[:, :width]
    lefts[1][...] = e0[:, slot : slot + width]
    row = 0
    for which, size in ((0, width), (1, kv_size), (2, kv_size)):
        stats[which][...], row = get_stat(e0, row, 2 * slot, size)
    lefts[2][...] = e1[:, :width]
    rights[0][...] = e1[:, slot : slot + width]
    rights[1][...] = e1[:, 2 * slot : 2 * slot + kv_size]
    rights[2][...] = e1[:, 2 * slot + kv_size : 2 * slot + 2 * kv_size]


def finish(middle_sum, entry_sum, lefts, rights, magnitudes):
    arrays = list(middle_sum) + list(entry_sum)
    shapes = [a.shape for a in lefts] + [a.shape for a in rights] + [a.shape for a in magnitudes]
    return pl.pallas_call(
        partial(finish_kernel, lefts[0].shape[1], rights[4].shape[1], rights[1].shape[1]),
        grid=(1,),
        in_specs=[full(a.shape) for a in arrays],
        out_specs=[full(s) for s in shapes],
        out_shape=[jax.ShapeDtypeStruct(s, f32) for s in shapes],
        compiler_params=params(),
        cost_estimate=cost(0, 3e6),
    )(*arrays)


def to_other_core(value):
    size = lax.axis_size("seq")
    return lax.ppermute(value, "seq", [(i, i ^ 1) for i in range(size)])


def peer(index, step, count):
    return index ^ step if count & (count - 1) == 0 else (index + step) % count


def to_chip(value, step):
    size = lax.axis_size("seq")
    count = size // 2
    return lax.ppermute(
        value, "seq", [(2 * peer(c, step, count) + k, 2 * c + k) for c in range(count) for k in (0, 1)]
    )


def back_to_chip(value, step):
    size = lax.axis_size("seq")
    count = size // 2
    return lax.ppermute(
        value, "seq", [(2 * c + k, 2 * peer(c, step, count) + k) for c in range(count) for k in (0, 1)]
    )


def to_batch(value, step):
    count = lax.axis_size("batch")
    return lax.ppermute(value, "batch", [(b, peer(b, step, count)) for b in range(count)])


def sum_everywhere(pack, core):
    shards = lax.axis_size("seq") // 2
    batches = lax.axis_size("batch")
    low = pack.astype(bf16)
    own = lax.dynamic_index_in_dim(pack, core, 0, False)
    total = own + to_other_core(lax.dynamic_index_in_dim(low, 1 - core, 0, False)).astype(f32)
    low = total.astype(bf16)
    for step in range(1, shards):
        total = total + to_chip(low, step).astype(f32)
    low = total.astype(bf16)
    for step in range(1, batches):
        total = total + to_batch(low, step).astype(f32)
    mine = total.astype(bf16)
    other = to_other_core(mine)
    return (jnp.where(core == 0, mine, other), jnp.where(core == 0, other, mine))


def join_cores(value, core, axis):
    half = value.shape[0] // 2
    keep = lax.dynamic_slice_in_dim(value, core * half, half, 0)
    other = to_other_core(lax.dynamic_slice_in_dim(value, (1 - core) * half, half, 0))
    return jnp.where(
        core == 0,
        jnp.concatenate([keep, other], axis=axis),
        jnp.concatenate([other, keep], axis=axis),
    )


def part_cores(parts, core):
    value = jnp.stack(parts)
    keep = lax.dynamic_index_in_dim(value, core, 1, False)
    other = to_other_core(lax.dynamic_index_in_dim(value, 1 - core, 1, False))
    return jnp.where(core == 0, jnp.concatenate([keep, other]), jnp.concatenate([other, keep]))


def body(tokens, segment_ids, position_ids, cotangent, *weights):
    bases, lefts, rights, magnitudes = (
        weights[:7],
        [a.T for a in weights[7:14]],
        weights[14:21],
        [m[None, :] for m in weights[21:28]],
    )
    turned = (False, True, True, False, False, False, True)
    bases = [w.T if turn else w for w, turn in zip(bases, turned)]
    index = lax.axis_index("seq")
    core, chip = index % 2, index // 2
    shards = lax.axis_size("seq") // 2
    x = join_cores(jnp.swapaxes(tokens, 1, 2), core, 2)
    dy = join_cores(jnp.swapaxes(cotangent, 1, 2), core, 2)
    position = join_cores(position_ids, core, 1)
    rows, width, size = x.shape
    half_head = HEAD // 2
    frequency = ROTARY_BASE ** (-(jnp.arange(half_head, dtype=f32) * 2.0 / HEAD))
    phases = position.astype(f32)[:, None, :] * frequency[None, :, None]
    cosine, sine = jnp.cos(phases), jnp.sin(phases)
    first = position[:, 0]
    position = position[:, None, :]
    chip_array = chip.astype(jnp.int32)[None]

    steps = (256, 128, 128, 256, 512, 512, 128)
    ready = [None] * 7
    for which in (0, 1, 2):
        ready[which] = prepare(
            bases[which],
            lefts[which],
            rights[which],
            magnitudes[which],
            turned[which],
            steps[which],
        )
    effective = [ready[which][0] for which in range(3)]
    entries = [
        entry(row, x, cosine, sine, effective, lefts[:3]) for row in range(rows)
    ]
    gathered = []
    for row in range(rows):
        own = entries[row][1].reshape(2 * KV_HEADS, HEAD, size)
        gathered.append([own] + [to_chip(own, step) for step in range(1, shards)])
    for which in (3, 4, 5, 6):
        ready[which] = prepare(
            bases[which],
            lefts[which],
            rights[which],
            magnitudes[which],
            turned[which],
            steps[which],
        )
    dr, dt_lower = lower_back(dy, ready[6][0], ready[6][1])
    middle_weights = []
    for which in (3, 4, 5):
        middle_weights += [ready[which][0], ready[which][1]]
    middle_weights += [ready[6][0], lefts[6]]
    outs, middle_parts, backs = [], [], []
    for row in range(rows):
        query = entries[row][0].reshape(KV_HEADS, GROUP * HEAD, size)
        mixed, lse = attend(row, chip_array, first, position, query, gathered[row])
        results = middle(
            row,
            x,
            dy,
            dr,
            dt_lower,
            mixed.reshape(HEADS * HEAD, size),
            (lefts[3], lefts[4], lefts[5]),
            middle_weights,
        )
        outs.append(results[0])
        middle_parts.append(results[4:])
        dquery, *dkvs = attend_back(
            row,
            chip_array,
            first,
            position,
            query,
            results[2].reshape(KV_HEADS, GROUP * HEAD, size),
            lse,
            results[3],
            gathered[row],
        )
        dkvs = [dkvs[0]] + [back_to_chip(dkvs[step], step) for step in range(1, shards)]
        backs.append((results[1], dquery.reshape(HEADS * HEAD, size), dkvs))
    layer_out = part_cores(outs, core)

    def group(which):
        return (ready[which][0], lefts[which], rights[which], ready[which][2], magnitudes[which])

    middle_pack = settle_middle(middle_parts, [group(which) for which in (3, 4, 5, 6)])
    middle_sum = sum_everywhere(middle_pack, core)
    exits = []
    for row in range(rows):
        dx1, dquery, dkvs = backs[row]
        exits.append(
            leave(
                row,
                x,
                cosine,
                sine,
                dx1,
                entries[row][2],
                entries[row][0],
                entries[row][1],
                dquery,
                effective,
                [ready[which][1] for which in range(3)],
                dkvs,
            )
        )
    tokens_grad = part_cores([e[0] for e in exits], core)
    entry_pack = settle_entry([e[1:] for e in exits], [group(which) for which in (0, 1, 2)])
    entry_sum = sum_everywhere(entry_pack, core)
    finals = finish(middle_sum, entry_sum, lefts, rights, magnitudes)
    return (
        jnp.swapaxes(layer_out, 1, 2),
        jnp.swapaxes(tokens_grad, 1, 2),
        *[a.T for a in finals[:7]],
        *finals[7:14],
        *[m[0] for m in finals[14:]],
    )


def solution(mesh):
    split = P("batch", "seq", None)
    return jax.shard_map(
        body,
        mesh=mesh,
        in_specs=(split, P("batch", "seq"), P("batch", "seq"), split) + (P(),) * 28,
        out_specs=(split, split) + (P(),) * 21,
        check_vma=False,
    )
```

```python
from functools import partial

import jax
import jax.numpy as jnp
from jax import lax
from jax.experimental import pallas as pl
from jax.experimental.pallas import tpu as pltpu
from jax.sharding import PartitionSpec as P

HEADS = 15
KV_HEADS = 5
HEAD = 64
GROUP = 3
RANK = 16
EPSILON = 1e-05
ROTARY_BASE = 100000.0
MASKED = -1e30
ADAPTER_SCALE = 2.0
HEAD_SCALE = HEAD**-0.5

bf16 = jnp.bfloat16
f32 = jnp.float32


def dot_nn(a, b):
    return lax.dot_general(a, b, (((1,), (0,)), ((), ())), preferred_element_type=f32)


def dot_tn(a, b):
    return lax.dot_general(a, b, (((0,), (0,)), ((), ())), preferred_element_type=f32)


def dot_nt(a, b):
    return lax.dot_general(a, b, (((1,), (1,)), ((), ())), preferred_element_type=f32)


def vmem():
    return pl.BlockSpec(memory_space=pltpu.VMEM)


def smem():
    return pl.BlockSpec(memory_space=pltpu.SMEM)


def call(kernel, arrays, shapes, mebibytes, microseconds, scalars=(), scratch=(), after=()):
    skipped = len(after)
    return pl.pallas_call(
        (lambda *refs: kernel(*refs[skipped:])) if skipped else kernel,
        in_specs=[pl.BlockSpec(memory_space=pl.ANY)] * skipped
        + [smem()] * len(scalars)
        + [vmem()] * len(arrays),
        out_specs=[vmem()] * len(shapes),
        out_shape=[jax.ShapeDtypeStruct(shape, dtype) for shape, dtype in shapes],
        scratch_shapes=list(scratch),
        compiler_params=pltpu.CompilerParams(vmem_limit_bytes=mebibytes * 2**20),
        cost_estimate=pl.CostEstimate(
            flops=int(microseconds * 1.1e9), bytes_accessed=1, transcendentals=0
        ),
    )(*after, *scalars, *arrays)


def eye(size):
    return lax.broadcasted_iota(jnp.int32, (size, size), 0) == lax.broadcasted_iota(
        jnp.int32, (size, size), 1
    )


def chunks(total, step=128):
    return [(start, min(step, total - start)) for start in range(0, total, step)]


def column_to_row(column):
    parts = []
    for start, size in chunks(column.shape[0]):
        parts.append(
            jnp.sum(jnp.where(eye(size), column[start : start + size], 0.0), axis=0, keepdims=True)
        )
    return parts[0] if len(parts) == 1 else jnp.concatenate(parts, axis=1)


def row_to_column(row):
    parts = []
    for start, size in chunks(row.shape[1]):
        parts.append(
            jnp.sum(jnp.where(eye(size), row[:, start : start + size], 0.0), axis=1, keepdims=True)
        )
    return parts[0] if len(parts) == 1 else jnp.concatenate(parts, axis=0)


def prepare_natural(base_ref, left_ref, right_ref, magnitude_ref, weight_ref, norm_ref, held):
    inputs, outputs = base_ref.shape
    step = 96
    for at, lanes in chunks(outputs, 512):
        place = slice(at, at + lanes)
        right = right_ref[:, place]
        squares = jnp.zeros((8, lanes), f32)
        for start in range(0, inputs, step):
            rows = slice(start, start + step)
            combined = base_ref[rows, place].astype(f32) + dot_tn(
                left_ref[:, rows] * ADAPTER_SCALE, right
            )
            held[rows, :lanes] = combined
            squares = squares + jnp.sum(
                (combined * combined).reshape(step // 8, 8, lanes), axis=0
            )
        norm = jnp.sqrt(jnp.sum(squares, axis=0, keepdims=True))
        column = magnitude_ref[place].reshape(1, lanes) / norm
        for start in range(0, inputs, step):
            rows = slice(start, start + step)
            weight_ref[rows, place] = (held[rows, :lanes] * column).astype(bf16)
        weight_ref[inputs:, place] = (ADAPTER_SCALE * column * right.astype(f32)).astype(bf16)
        norm_ref[:, place] = norm


def prepare_turned(
    base_ref, left_ref, right_ref, magnitude_ref, weight_ref, norm_ref, scaled_ref
):
    outputs = base_ref.shape[0]
    left = left_ref[...]
    for at, size in chunks(outputs):
        rows = slice(at, at + size)
        right = right_ref[:, rows]
        combined = base_ref[rows, :].astype(f32) + dot_tn(right * ADAPTER_SCALE, left)
        norm = column_to_row(jnp.sqrt(jnp.sum(combined * combined, axis=1, keepdims=True)))
        column = magnitude_ref[rows].reshape(1, size) / norm
        weight_ref[rows, :] = (combined * row_to_column(column)).astype(bf16)
        scaled_ref[:, rows] = (ADAPTER_SCALE * column * right.astype(f32)).astype(bf16)
        norm_ref[:, rows] = norm
    weight_ref[outputs:, :] = left


def prepare(base, left, right, magnitude, turned, after=()):
    outputs = right.shape[1]
    shapes = [((base.shape[0] + RANK, base.shape[1]), bf16), ((1, outputs), f32)]
    if turned:
        shapes.append((right.shape, bf16))
    scratch = [] if turned else [pltpu.VMEM((base.shape[0], 512), f32)]
    return call(
        prepare_turned if turned else prepare_natural,
        (base, left, right, magnitude),
        shapes,
        4,
        1.3e-6 * base.size,
        scratch=scratch,
        after=after,
    )


def rms_factor(values):
    return lax.rsqrt(jnp.mean(values * values, axis=0, keepdims=True) + EPSILON)


def turn_heads(values, cosine, sine, heads, scale):
    half = HEAD // 2
    out = []
    for head in range(heads):
        first = values[head * HEAD : head * HEAD + half]
        second = values[head * HEAD + half : (head + 1) * HEAD]
        out.append((first * cosine - second * sine) * scale)
        out.append((second * cosine + first * sine) * scale)
    return jnp.concatenate(out, axis=0)


def turn_heads_back(values, cosine, sine, heads, scale):
    half = HEAD // 2
    out = []
    for head in range(heads):
        first = values[head * HEAD : head * HEAD + half]
        second = values[head * HEAD + half : (head + 1) * HEAD]
        out.append((first * cosine + second * sine) * scale)
        out.append((second * cosine - first * sine) * scale)
    return jnp.concatenate(out, axis=0)


def pair(place_ref, own, other, axis):
    here = place_ref[1] == 0
    return jnp.concatenate([jnp.where(here, own, other), jnp.where(here, other, own)], axis=axis)


def unpair(place_ref, value):
    size = value.shape[1] // 2
    here = place_ref[1] == 0
    first, second = value[:, :size], value[:, size:]
    return jnp.where(here, first, second), jnp.where(here, second, first)


def entry_kernel(
    rows,
    place_ref,
    own_ref,
    other_ref,
    pos_own_ref,
    pos_other_ref,
    freq_ref,
    aq_ref,
    wq_ref,
    wk_ref,
    wv_ref,
    x_ref,
    q_ref,
    kv_ref,
    t_ref,
    pos_ref,
    table_ref,
):
    kv_size = KV_HEADS * HEAD
    tokens = x_ref.shape[-1]
    width = x_ref.shape[-2]
    for at, row in enumerate(rows):
        mine = place_ref[1] * other_ref.shape[0] + row
        x_low = pair(place_ref, own_ref[mine], other_ref[row], 1)
        x_ref[at] = x_low
        position = pair(
            place_ref, pos_own_ref[pl.ds(mine, 1), :], pos_other_ref[row : row + 1, :], 1
        )
        pos_ref[at] = position
        phases = freq_ref[...] * position.astype(f32)
        cosine = jnp.cos(phases)
        sine = jnp.sin(phases)
        table_ref[at, 0] = cosine
        table_ref[at, 1] = sine
        x = x_low.astype(f32)
        normed = (x * rms_factor(x)).astype(bf16)
        key = dot_nn(wk_ref[...], normed)
        value = dot_nn(wv_ref[...], normed)
        query = dot_tn(wq_ref[:width, :], normed)
        turned = turn_heads(key, cosine, sine, KV_HEADS, 1.0).astype(bf16)
        value_low = value.astype(bf16)
        for head in range(KV_HEADS):
            kv_ref[at, head] = turned[head * HEAD : (head + 1) * HEAD]
            kv_ref[at, KV_HEADS + head] = value_low[head * HEAD : (head + 1) * HEAD]
        t_ref[at, :RANK] = dot_nn(aq_ref[...], normed).astype(bf16)
        t_ref[at, RANK : 2 * RANK] = key[kv_size:].astype(bf16)
        t_ref[at, 2 * RANK :] = value_low[kv_size:]
        turned = turn_heads(query, cosine, sine, HEADS, HEAD_SCALE).astype(bf16)
        for head in range(HEADS):
            lane = head % GROUP * tokens
            q_ref[at, head // GROUP, :, lane : lane + tokens] = turned[
                head * HEAD : (head + 1) * HEAD
            ]


def entry(rows, place, own, other, pos_own, pos_other, frequency, left, weights):
    width, size = own.shape[1], own.shape[2]
    tokens = 2 * size
    count = len(rows)
    shapes = [
        ((count, width, tokens), bf16),
        ((count, KV_HEADS, HEAD, GROUP * tokens), bf16),
        ((count, 2 * KV_HEADS, HEAD, tokens), bf16),
        ((count, 3 * RANK, tokens), bf16),
        ((count, 1, tokens), jnp.int32),
        ((count, 2, HEAD // 2, tokens), f32),
    ]
    return call(
        partial(entry_kernel, rows),
        (own, other, pos_own, pos_other, frequency, left, *weights),
        shapes,
        6,
        2.2 * count,
        scalars=(place,),
    )


def lower_back_kernel(
    place_ref, own_ref, other_ref, wl_ref, cb_ref, dy_ref, dr_ref, dt_ref
):
    rows = other_ref.shape[0]
    outputs = own_ref.shape[1]
    for row in range(rows):
        dy = pair(place_ref, own_ref[place_ref[1] * rows + row], other_ref[row], 1)
        dy_ref[row] = dy
        dr_ref[row] = dot_tn(wl_ref[:outputs, :], dy).astype(bf16)
        dt_ref[row] = dot_nn(cb_ref[...], dy).astype(bf16)


def lower_back(place, own, other, weight, scaled, after=()):
    rows, width, size = other.shape
    hidden = weight.shape[1]
    tokens = 2 * size
    shapes = [
        ((rows, width, tokens), bf16),
        ((rows, hidden, tokens), bf16),
        ((rows, RANK, tokens), bf16),
    ]
    return call(
        lower_back_kernel,
        (own, other, weight, scaled),
        shapes,
        8,
        1.9 * rows,
        scalars=(place,),
        after=after,
    )


def write_bias(bias_ref, position, distance):
    size = bias_ref.shape[0]
    key = lax.broadcasted_iota(jnp.int32, (size, size), 0)
    query = lax.broadcasted_iota(jnp.int32, (size, size), 1)
    start = query - position + distance * size
    bias_ref[...] = jnp.where((key >= start) & (key <= query + distance * size), 0.0, MASKED)


def block_distance(chip_ref, step, shards):
    return chip_ref[0] - block_source(chip_ref[0], step, shards)


def block_source(chip, step, shards):
    if shards & (shards - 1) == 0:
        return jnp.bitwise_xor(chip, step)
    return lax.rem(chip + step, shards)


def needed(place_ref, pos_own_ref, pos_other_ref, row, step, shards, size):
    rows = pos_other_ref.shape[0]
    first = jnp.where(
        place_ref[1] == 0, pos_own_ref[place_ref[1] * rows + row, 0], pos_other_ref[row, 0]
    )
    distance = block_distance(place_ref, step, shards)
    return (distance > 0) & (distance * size - first < size)


def attend_kernel(row, at, shards, place_ref, pos_own_ref, pos_other_ref, pos_ref, q_ref, *rest):
    kv_refs, (o_ref, lse_ref, bias_ref, max_ref, sum_ref, acc_ref) = rest[:shards], rest[shards:]
    size = pos_ref.shape[-1]

    def visit(kv_ref, opening):
        for head in range(KV_HEADS):
            bias = jnp.concatenate([bias_ref[...]] * GROUP, axis=1)
            logits = dot_tn(kv_ref[at, head], q_ref[at, head]) + bias
            top = jnp.max(logits, axis=0, keepdims=True)
            if not opening:
                before = max_ref[head]
                top = jnp.maximum(top, before)
            weights = jnp.exp(logits - top)
            total = jnp.sum(weights, axis=0, keepdims=True)
            mixed = dot_nn(kv_ref[at, head + KV_HEADS], weights.astype(bf16))
            if not opening:
                rescale = jnp.exp(before - top)
                total = total + rescale * sum_ref[head]
                mixed = mixed + rescale * acc_ref[head]
            max_ref[head] = top
            sum_ref[head] = total
            acc_ref[head] = mixed

    write_bias(bias_ref, pos_ref[at], 0)
    visit(kv_refs[0], True)
    for step in range(1, shards):

        @pl.when(needed(place_ref, pos_own_ref, pos_other_ref, row, step, shards, size))
        def _():
            write_bias(bias_ref, pos_ref[at], block_distance(place_ref, step, shards))
            visit(kv_refs[step], False)

    total = sum_ref[...]
    o_ref[...] = (acc_ref[...] / total).astype(bf16)
    lse_ref[...] = max_ref[...] + jnp.log(total)


def attend(row, at, place, pos_own, pos_other, position, query, blocks, after=()):
    tokens = position.shape[-1]
    stats = (KV_HEADS, 1, GROUP * tokens)
    return call(
        partial(attend_kernel, row, at, len(blocks)),
        (position, query, *blocks),
        [(query.shape[1:], bf16), (stats, f32)],
        4,
        6,
        scalars=(place, pos_own, pos_other),
        scratch=[
            pltpu.VMEM((tokens, tokens), f32),
            pltpu.VMEM(stats, f32),
            pltpu.VMEM(stats, f32),
            pltpu.VMEM(query.shape[1:], f32),
        ],
        after=after,
    )


def attend_back_kernel(
    row,
    at,
    shards,
    place_ref,
    pos_own_ref,
    pos_other_ref,
    pos_ref,
    q_ref,
    do_ref,
    lse_ref,
    delta_ref,
    *rest,
):
    kv_refs, rest = rest[:shards], rest[shards:]
    dq_ref, dkv_refs, bias_ref = rest[0], rest[1 : 1 + shards], rest[1 + shards]
    size = pos_ref.shape[-1]

    def visit(kv_ref, dkv_ref, opening):
        for head in range(KV_HEADS):
            key, value = kv_ref[at, head], kv_ref[at, head + KV_HEADS]
            query, upstream = q_ref[at, head], do_ref[head]
            bias = jnp.concatenate([bias_ref[...]] * GROUP, axis=1)
            probs = jnp.exp(dot_tn(key, query) + bias - lse_ref[head])
            score_grad = (probs * (dot_tn(value, upstream) - delta_ref[head])).astype(bf16)
            query_grad = dot_nn(key, score_grad) * HEAD_SCALE
            if not opening:
                query_grad = query_grad + dq_ref[head]
            dq_ref[head] = query_grad
            dkv_ref[head] = dot_nt(query, score_grad).astype(bf16)
            dkv_ref[head + KV_HEADS] = dot_nt(upstream, probs.astype(bf16)).astype(bf16)

    write_bias(bias_ref, pos_ref[at], 0)
    visit(kv_refs[0], dkv_refs[0], True)
    for step in range(1, shards):
        wanted = needed(place_ref, pos_own_ref, pos_other_ref, row, step, shards, size)

        @pl.when(wanted)
        def _():
            write_bias(bias_ref, pos_ref[at], block_distance(place_ref, step, shards))
            visit(kv_refs[step], dkv_refs[step], False)

        @pl.when(jnp.logical_not(wanted))
        def _():
            dkv_refs[step][...] = jnp.zeros(dkv_refs[step].shape, bf16)


def attend_back(
    row, at, place, pos_own, pos_other, position, query, upstream, lse, delta, blocks, after=()
):
    tokens = position.shape[-1]
    return call(
        partial(attend_back_kernel, row, at, len(blocks)),
        (position, query, upstream, lse, delta, *blocks),
        [(query.shape[1:], f32)] + [(b.shape[1:], bf16) for b in blocks],
        4,
        9,
        scalars=(place, pos_own, pos_other),
        scratch=[pltpu.VMEM((tokens, tokens), f32)],
        after=after,
    )


def spread_heads(ref):
    tokens = ref.shape[-1] // GROUP
    return jnp.concatenate(
        [
            ref[head // GROUP, :, head % GROUP * tokens : (head % GROUP + 1) * tokens]
            for head in range(HEADS)
        ],
        axis=0,
    )


def middle_kernel(
    row,
    at,
    place_ref,
    x_ref,
    dy_ref,
    dr_ref,
    dtl_ref,
    o_ref,
    ao_ref,
    ag_ref,
    au_ref,
    wo,
    wg,
    wu,
    wl,
    keep_ref,
    send_ref,
    dx1_ref,
    do_ref,
    delta_ref,
    dao_ref,
    dbo_ref,
    dag_ref,
    dau_ref,
    dbg_ref,
    dbu_ref,
    dal_ref,
    dbl_ref,
    so_ref,
    sg_ref,
    su_ref,
    sl_ref,
    act,
    dgate,
    dupper,
):
    _, width, tokens = x_ref.shape
    hidden = act.shape[0]
    mixed = spread_heads(o_ref)
    attn = dot_tn(wo[:width, :], mixed)
    x1 = x_ref[at].astype(f32) + attn
    rho = rms_factor(x1)
    normed = x1 * rho
    normed_low = normed.astype(bf16)
    t_output = dot_nn(ao_ref[...], mixed).astype(bf16)
    t_gate = dot_nn(ag_ref[...], normed_low).astype(bf16)
    t_upper = dot_nn(au_ref[...], normed_low).astype(bf16)
    step = 256
    for start in range(0, hidden, step):
        rows = slice(start, start + step)
        gate = dot_tn(wg[:width, rows], normed_low)
        upper = dot_tn(wu[:width, rows], normed_low)
        down = dr_ref[row, rows, :].astype(f32)
        sigmoid = jax.nn.sigmoid(gate)
        silu = gate * sigmoid
        act[rows, :] = (silu * upper).astype(bf16)
        gate_grad = down * upper * (sigmoid + silu * (1.0 - sigmoid))
        upper_grad = down * silu
        dgate[rows, :] = gate_grad.astype(bf16)
        dupper[rows, :] = upper_grad.astype(bf16)
        sg_ref[:, rows] = column_to_row(jnp.sum(gate * gate_grad, axis=1, keepdims=True))
        su_ref[:, rows] = column_to_row(jnp.sum(upper * upper_grad, axis=1, keepdims=True))
    lower_all = dot_nn(wl[...], act[...])
    lower = lower_all[:width]
    t_lower = lower_all[width:].astype(bf16)
    out = (x1 + lower).astype(bf16)
    keep_ref[...], send_ref[...] = unpair(place_ref, out)
    dy_low = dy_ref[row]
    dy = dy_low.astype(f32)
    sl_ref[...] = column_to_row(jnp.sum(lower * dy, axis=1, keepdims=True))
    gate_back = dot_nn(wg[...], dgate[...])
    upper_back = dot_nn(wu[...], dupper[...])
    dt_gate = gate_back[width:].astype(bf16)
    dt_upper = upper_back[width:].astype(bf16)
    dnormed = gate_back[:width] + upper_back[:width]
    dx1 = dy + rho * (dnormed - normed * jnp.mean(dnormed * normed, axis=0, keepdims=True))
    dx1_ref[...] = dx1
    dx1_low = dx1.astype(bf16)
    so_ref[...] = column_to_row(jnp.sum(attn * dx1, axis=1, keepdims=True))
    output_back = dot_nn(wo[...], dx1_low)
    dt_output = output_back[width:].astype(bf16)
    dmixed = output_back[:width].astype(bf16)
    weighted = dmixed.astype(f32) * mixed.astype(f32)
    for head in range(HEADS):
        rows = slice(head * HEAD, (head + 1) * HEAD)
        lanes = slice(head % GROUP * tokens, (head % GROUP + 1) * tokens)
        do_ref[head // GROUP, :, lanes] = dmixed[rows]
        delta_ref[head // GROUP, :, lanes] = jnp.sum(weighted[rows], axis=0, keepdims=True)
    dao_ref[...] = dot_nt(dt_output, mixed)
    dbo_ref[...] = dot_nt(t_output, dx1_low)
    dag_ref[...] = dot_nt(dt_gate, normed_low)
    dau_ref[...] = dot_nt(dt_upper, normed_low)
    dbg_ref[...] = dot_nt(t_gate, dgate[...])
    dbu_ref[...] = dot_nt(t_upper, dupper[...])
    dal_ref[...] = dot_nt(dtl_ref[row], act[...])
    dbl_ref[...] = dot_nt(t_lower, dy_low)


def middle(row, at, place, x, dy, dr, dt_lower, mixed, lefts, weights, after=()):
    _, width, tokens = x.shape
    hidden = dr.shape[1]
    shapes = [
        ((width, tokens // 2), bf16),
        ((width, tokens // 2), bf16),
        ((width, tokens), f32),
        (mixed.shape, bf16),
        ((KV_HEADS, 1, GROUP * tokens), f32),
        ((RANK, width), f32),
        ((RANK, width), f32),
        ((RANK, width), f32),
        ((RANK, width), f32),
        ((RANK, hidden), f32),
        ((RANK, hidden), f32),
        ((RANK, hidden), f32),
        ((RANK, width), f32),
        ((1, width), f32),
        ((1, hidden), f32),
        ((1, hidden), f32),
        ((1, width), f32),
    ]
    return call(
        partial(middle_kernel, row, at),
        (x, dy, dr, dt_lower, mixed, *lefts, *weights),
        shapes,
        14,
        13,
        scalars=(place,),
        scratch=[pltpu.VMEM((hidden, tokens), bf16)] * 3,
        after=after,
    )


def exit_kernel(at, shards, *refs):
    place_ref, *refs = refs
    (x_ref, table_ref, dx1_ref, t_ref, q_ref, kv_ref, dq_ref, wq_ref, wk_ref, wv_ref) = refs[:10]
    cbk_ref, cbv_ref = refs[10:12]
    dkv_refs = refs[12 : 12 + shards]
    keep_ref, send_ref, da_ref, dbq_ref, dbkv_ref, sq_ref, skv_ref = refs[12 + shards :]
    _, width, tokens = x_ref.shape
    kv_size = KV_HEADS * HEAD
    x = x_ref[at].astype(f32)
    rho = rms_factor(x)
    normed = x * rho
    normed_low = normed.astype(bf16)
    cosine = table_ref[at, 0]
    sine = table_ref[at, 1]
    dquery = turn_heads_back(spread_heads(dq_ref), cosine, sine, HEADS, 1.0)
    query = turn_heads_back(
        spread_heads(q_ref.at[at]).astype(f32), cosine, sine, HEADS, 1.0 / HEAD_SCALE
    )
    sq_ref[...] = column_to_row(jnp.sum(query * dquery, axis=1, keepdims=True))
    dquery = dquery.astype(bf16)
    query_back = dot_nn(wq_ref[...], dquery)
    dkv = dkv_refs[0][...].astype(f32)
    for ref in dkv_refs[1:]:
        dkv = dkv + ref[...].astype(f32)
    dkv = dkv.reshape(2 * kv_size, tokens)
    key_value = kv_ref[at].astype(f32).reshape(2 * kv_size, tokens)
    dkey = turn_heads_back(dkv[:kv_size], cosine, sine, KV_HEADS, 1.0)
    dvalue = dkv[kv_size:]
    key = turn_heads_back(key_value[:kv_size], cosine, sine, KV_HEADS, 1.0)
    value = key_value[kv_size:]
    skv_ref[0:1, :] = column_to_row(jnp.sum(key * dkey, axis=1, keepdims=True))
    skv_ref[1:2, :] = column_to_row(jnp.sum(value * dvalue, axis=1, keepdims=True))
    dkey = dkey.astype(bf16)
    dvalue = dvalue.astype(bf16)
    dnormed = (
        query_back[:width]
        + dot_tn(wk_ref[:kv_size, :], dkey)
        + dot_tn(wv_ref[:kv_size, :], dvalue)
    )
    dx = dx1_ref[...] + rho * (dnormed - normed * jnp.mean(dnormed * normed, axis=0, keepdims=True))
    keep_ref[...], send_ref[...] = unpair(place_ref, dx.astype(bf16))
    dt = jnp.concatenate(
        [query_back[width:], dot_nn(cbk_ref[...], dkey), dot_nn(cbv_ref[...], dvalue)], axis=0
    ).astype(bf16)
    da_ref[...] = dot_nt(dt, normed_low)
    dbq_ref[...] = dot_nt(t_ref[at, :RANK], dquery)
    dbkv_ref[0] = dot_nt(t_ref[at, RANK : 2 * RANK], dkey)
    dbkv_ref[1] = dot_nt(t_ref[at, 2 * RANK :], dvalue)


def leave(at, place, x, table, dx1, inner, query, key_value, dquery, weights, scaled, dkvs, after=()):
    _, width, tokens = x.shape
    q_size, kv_size = HEADS * HEAD, KV_HEADS * HEAD
    shapes = [
        ((width, tokens // 2), bf16),
        ((width, tokens // 2), bf16),
        ((3 * RANK, width), f32),
        ((RANK, q_size), f32),
        ((2, RANK, kv_size), f32),
        ((1, q_size), f32),
        ((2, kv_size), f32),
    ]
    return call(
        partial(exit_kernel, at, len(dkvs)),
        (x, table, dx1, inner, query, key_value, dquery, *weights, *scaled, *dkvs),
        shapes,
        7,
        3,
        scalars=(place,),
        after=after,
    )


def settle(sums, weight, turned, left, right, norm, magnitude):
    left_sum, right_sum, stat = sums
    magnitude = magnitude.reshape(1, -1)
    factor = -stat / (magnitude * norm)
    scaled = (ADAPTER_SCALE * factor * right.astype(f32)).astype(bf16)
    if turned:
        left_more = dot_nn(scaled, weight)
        product = dot_nt(left, weight)
    else:
        left_more = dot_nt(scaled, weight)
        product = dot_nn(left, weight)
    right_total = ADAPTER_SCALE * (right_sum * (magnitude / norm) + factor * product)
    return (left_sum + left_more, right_total, stat / magnitude)


STAT = 512


def put_stat(ref, half, row, lane, values):
    size = values.shape[1]
    for start in range(0, size, STAT):
        take = min(STAT, size - start)
        ref[half, row : row + 1, lane : lane + take] = values[:, start : start + take]
        row += 1
    return row


def stack_sum(refs):
    total = refs[0][...]
    for ref in refs[1:]:
        total = total + ref[...]
    return total


def settle_middle_kernel(rows, shards, *refs):
    sums = [
        stack_sum([refs[row * 12 + which] for row in range(rows)]) for which in range(12)
    ]
    refs = refs[rows * 12 :]
    names = ("output", "gate", "upper", "lower")
    groups = {}
    for which, name in enumerate(names):
        groups[name] = [ref for ref in refs[which * 5 : which * 5 + 5]]
    out, pack = refs[20:]
    dao, dbo, dag, dau, dbg, dbu, dal, dbl, so, sg, su, sl = sums
    pieces = {
        "output": (dao, dbo, so),
        "gate": (dag, dbg, sg),
        "upper": (dau, dbu, su),
        "lower": (dal, dbl, sl),
    }
    done = {}
    for name in names:
        weight, left, right, norm, magnitude = groups[name]
        done[name] = settle(
            pieces[name],
            weight[: weight.shape[0] - RANK, :],
            name == "lower",
            left[...],
            right[...],
            norm[...],
            magnitude[...],
        )
    width = dao.shape[1]
    slot, hidden = slots(width), dbg.shape[1]
    pack[...] = jnp.zeros(pack.shape, f32)
    pack[0, :, 0:hidden] = done["gate"][1]
    pack[0, :, hidden : 2 * hidden] = done["upper"][1]
    pack[0, :, 2 * hidden : 2 * hidden + width] = done["output"][0]
    row = 0
    for name in ("gate", "upper", "output", "lower"):
        row = put_stat(pack, 0, row, 2 * hidden + slot, done[name][2])
    pack[1, :, 0:hidden] = done["lower"][0]
    place = hidden
    for values in (done["output"][1], done["gate"][0], done["upper"][0], done["lower"][1]):
        pack[1, :, place : place + width] = values
        place += slot
    cut(out, pack, shards)


def slots(width):
    return -(-width // 128) * 128


def piece_of(half, shards):
    return slots(-(-half // shards))


def cut(out, pack, shards):
    piece = out.shape[-1]
    for half in range(2):
        for shard in range(shards):
            out[half, shard] = pack[half, :, shard * piece : (shard + 1) * piece]


def settle_middle(partials, projections, shards, after=()):
    hidden = partials[0][4].shape[1]
    width = partials[0][0].shape[1]
    piece = piece_of(2 * hidden + slots(width) + STAT, shards)
    flat = [a for part in partials for a in part] + [a for group in projections for a in group]
    return call(
        partial(settle_middle_kernel, len(partials), shards),
        flat,
        [((2, shards, RANK, piece), f32)],
        5,
        6,
        scratch=[pltpu.VMEM((2, RANK, shards * piece), f32)],
        after=after,
    )[0]


def settle_entry_kernel(rows, shards, place_ref, middle_ref, *refs):
    sums = [stack_sum([refs[row * 5 + which] for row in range(rows)]) for which in range(5)]
    refs = refs[rows * 5 :]
    da, dbq, dbkv, sq, skv = sums
    keep_ref, send_ref, pack = refs[15:]
    pieces = (
        (da[:RANK], dbq, sq),
        (da[RANK : 2 * RANK], dbkv[0], skv[0:1]),
        (da[2 * RANK :], dbkv[1], skv[1:2]),
    )
    done = []
    for which in range(3):
        weight, left, right, norm, magnitude = refs[which * 5 : which * 5 + 5]
        done.append(
            settle(
                pieces[which],
                weight[: weight.shape[0] - RANK, :],
                which > 0,
                left[...],
                right[...],
                norm[...],
                magnitude[...],
            )
        )
    width = da.shape[1]
    slot = slots(width)
    kv_size = skv.shape[1]
    pack[...] = jnp.zeros(pack.shape, f32)
    pack[0, :, 0:width] = done[0][0]
    pack[0, :, slot : slot + width] = done[1][0]
    row = 0
    for which in range(3):
        row = put_stat(pack, 0, row, 2 * slot, done[which][2])
    pack[1, :, 0:width] = done[2][0]
    pack[1, :, slot : slot + sq.shape[1]] = done[0][1]
    pack[1, :, 2 * slot : 2 * slot + 2 * kv_size] = jnp.concatenate(
        [done[1][1], done[2][1]], axis=1
    )
    here = place_ref[1] == 0
    middle_piece = middle_ref.shape[-1]
    piece = pack.shape[-1] // shards
    for shard in range(shards):
        place = slice(shard * piece, (shard + 1) * piece)
        parts = (
            (slice(0, middle_piece), middle_ref[0, shard], middle_ref[1, shard]),
            (slice(middle_piece, middle_piece + piece), pack[0, :, place], pack[1, :, place]),
        )
        for lanes, first, second in parts:
            keep_ref[shard, :, lanes] = jnp.where(here, first, second)
            send_ref[shard, :, lanes] = jnp.where(here, second, first).astype(bf16)


def settle_entry(place, middle_pack, partials, projections):
    shards = middle_pack.shape[1]
    width = partials[0][0].shape[1]
    kv_size = partials[0][4].shape[1]
    piece = piece_of(2 * slots(width) + max(STAT, slots(2 * kv_size)), shards)
    flat = [a for part in partials for a in part] + [a for group in projections for a in group]
    shape = (shards, RANK, middle_pack.shape[-1] + piece)
    return call(
        partial(settle_entry_kernel, len(partials), shards),
        [middle_pack] + flat,
        [(shape, f32), (shape, bf16)],
        5,
        2,
        scalars=(place,),
        scratch=[pltpu.VMEM((2, RANK, shards * piece), f32)],
    )


def get_stat(value, row, lane, size):
    parts = []
    for start in range(0, size, STAT):
        take = min(STAT, size - start)
        parts.append(value[row : row + 1, lane : lane + take])
        row += 1
    return jnp.concatenate(parts, axis=1) if len(parts) > 1 else parts[0], row


def finish_kernel(width, hidden, kv_size, shards, middle_piece, place_ref, *refs):
    mine_ref, other_ref = refs[:2]
    lefts, rights, stats = refs[2:9], refs[9:16], refs[16:23]
    middle_held, entry_held = refs[23:]
    chip, core = place_ref[0], place_ref[1]
    piece = mine_ref.shape[-1] - middle_piece
    for half in range(2):
        for step in range(shards):
            value = jnp.where(core == half, mine_ref[step], other_ref[step]).astype(f32)
            source = block_source(chip, step, shards)
            lane = pl.multiple_of(source * middle_piece, 128)
            middle_held[half, :, pl.ds(lane, middle_piece)] = value[:, :middle_piece]
            lane = pl.multiple_of(source * piece, 128)
            entry_held[half, :, pl.ds(lane, piece)] = value[:, middle_piece:]
    slot = slots(width)
    m0, m1, e0, e1 = middle_held.at[0], middle_held.at[1], entry_held.at[0], entry_held.at[1]
    rights[4][...] = m0[:, :hidden]
    rights[5][...] = m0[:, hidden : 2 * hidden]
    lefts[3][...] = m0[:, 2 * hidden : 2 * hidden + width]
    row = 0
    for which, size in ((4, hidden), (5, hidden), (3, width), (6, width)):
        value, row = get_stat(m0, row, 2 * hidden + slot, size)
        stats[which][...] = value[0]
    lefts[6][...] = m1[:, :hidden]
    for place, ref in enumerate((rights[3], lefts[4], lefts[5], rights[6])):
        ref[...] = m1[:, hidden + place * slot : hidden + place * slot + width]
    lefts[0][...] = e0[:, :width]
    lefts[1][...] = e0[:, slot : slot + width]
    row = 0
    for which, size in ((0, width), (1, kv_size), (2, kv_size)):
        value, row = get_stat(e0, row, 2 * slot, size)
        stats[which][...] = value[0]
    lefts[2][...] = e1[:, :width]
    rights[0][...] = e1[:, slot : slot + width]
    both = e1[:, 2 * slot : 2 * slot + 2 * kv_size]
    rights[1][...] = both[:, :kv_size]
    rights[2][...] = both[:, kv_size:]


def finish(place, middle_piece, sums, lefts, rights, magnitudes):
    shards = sums[0].shape[0]
    shapes = [a.shape for a in lefts] + [a.shape for a in rights] + [a.shape for a in magnitudes]
    sizes = (lefts[0].shape[1], rights[4].shape[1], rights[1].shape[1])
    return call(
        partial(finish_kernel, *sizes, shards, middle_piece),
        sums,
        [(shape, f32) for shape in shapes],
        5,
        2,
        scalars=(place,),
        scratch=[
            pltpu.VMEM((2, RANK, shards * piece), f32)
            for piece in (middle_piece, sums[0].shape[-1] - middle_piece)
        ],
    )


def to_other_core(value):
    size = lax.axis_size("seq")
    return lax.ppermute(value, "seq", [(i, i ^ 1) for i in range(size)])


def peer(index, step, count):
    return index ^ step if count & (count - 1) == 0 else (index + step) % count


def to_chip(value, step):
    size = lax.axis_size("seq")
    count = size // 2
    return lax.ppermute(
        value, "seq", [(2 * peer(c, step, count) + k, 2 * c + k) for c in range(count) for k in (0, 1)]
    )


def back_to_chip(value, step):
    size = lax.axis_size("seq")
    count = size // 2
    return lax.ppermute(
        value, "seq", [(2 * c + k, 2 * peer(c, step, count) + k) for c in range(count) for k in (0, 1)]
    )


def to_batch(value, step):
    count = lax.axis_size("batch")
    return lax.ppermute(value, "batch", [(b, peer(b, step, count)) for b in range(count)])


def share_kernel(place_ref, keep_ref, come_ref, own_ref, *out_refs):
    chip = place_ref[0]
    shards = come_ref.shape[0]
    own_ref[...] = keep_ref[chip] + come_ref[chip].astype(f32)
    for step, ref in enumerate(out_refs, start=1):
        other = block_source(chip, step, shards)
        ref[...] = (keep_ref[other] + come_ref[other].astype(f32)).astype(bf16)


def sum_kernel(own_ref, *refs):
    *come_refs, total_ref, low_ref = refs
    total = own_ref[...]
    for ref in come_refs:
        total = total + ref[...].astype(f32)
    total_ref[...] = total
    low_ref[...] = total.astype(bf16)


def cross_core(place, keep, send):
    shards = keep.shape[0]
    piece = keep.shape[1:]
    own, *parts = call(
        share_kernel,
        (keep, to_other_core(send)),
        [(piece, f32)] + [(piece, bf16)] * (shards - 1),
        4,
        1,
        scalars=(place,),
    )
    return own, parts


def add_up(own, come, after=()):
    return call(
        sum_kernel, (own, *come), [(own.shape, f32), (own.shape, bf16)], 4, 1, after=after
    )


def cross_chips(own, parts):
    return add_up(own, [back_to_chip(part, step) for step, part in enumerate(parts, start=1)])


def cross_batch(sums):
    own, low = sums
    count = lax.axis_size("batch")
    return add_up(own, [to_batch(low, step) for step in range(1, count)])


def spread(sums, shards):
    low = sums[1]
    mine = jnp.stack([low] + [to_chip(low, step) for step in range(1, shards)])
    return mine, to_other_core(mine)


def other_half(value, core):
    half = value.shape[0] // 2
    return to_other_core(lax.dynamic_slice_in_dim(value, (1 - core) * half, half, 0))


def assemble_kernel(rows, skipped, *refs):
    place_ref = refs[skipped]
    keep_refs = refs[skipped + 1 : skipped + 1 + rows]
    other_refs = refs[skipped + 1 + rows : skipped + 1 + 2 * rows]
    out_ref, sems = refs[-2:]
    core = place_ref[1]
    copies = []
    for row in range(rows):
        copies.append(
            pltpu.make_async_copy(keep_refs[row], out_ref.at[core * rows + row], sems.at[0, row])
        )
        copies.append(
            pltpu.make_async_copy(
                other_refs[row], out_ref.at[(1 - core) * rows + row], sems.at[1, row]
            )
        )
    for copy in copies:
        copy.start()
    for copy in copies:
        copy.wait()


def assemble(place, keeps, others, after=()):
    rows = len(keeps)
    anywhere = pl.BlockSpec(memory_space=pl.ANY)
    return pl.pallas_call(
        partial(assemble_kernel, rows, len(after)),
        in_specs=[anywhere] * len(after) + [smem()] + [anywhere] * (2 * rows),
        out_specs=anywhere,
        out_shape=jax.ShapeDtypeStruct((2 * rows,) + keeps[0].shape, keeps[0].dtype),
        scratch_shapes=[pltpu.SemaphoreType.DMA((2, rows))],
        compiler_params=pltpu.CompilerParams(vmem_limit_bytes=2**20),
        cost_estimate=pl.CostEstimate(flops=10**9, bytes_accessed=1, transcendentals=0),
    )(*after, place, *keeps, *others)


def body(tokens, segment_ids, position_ids, cotangent, *weights):
    bases, lefts, rights, magnitudes = (
        weights[:7],
        [a.T for a in weights[7:14]],
        weights[14:21],
        weights[21:28],
    )
    turned = (False, True, True, False, False, False, True)
    bases = [w.T if turn else w for w, turn in zip(bases, turned)]
    index = lax.axis_index("seq")
    core, chip = index % 2, index // 2
    shards = lax.axis_size("seq") // 2
    place = jnp.stack([chip, core]).astype(jnp.int32)
    x = jnp.swapaxes(tokens, 1, 2)
    dy = jnp.swapaxes(cotangent, 1, 2)
    x_other = other_half(x, core)
    pos_other = other_half(position_ids, core)
    dy_other = other_half(dy, core)
    rows = x_other.shape[0]
    half_head = HEAD // 2
    frequency = ROTARY_BASE ** (-(jnp.arange(half_head, dtype=f32) * 2.0 / HEAD))[:, None]

    def ready_for(which, after=()):
        return prepare(
            bases[which], lefts[which], rights[which], magnitudes[which], turned[which], after
        )

    ready = {which: ready_for(which) for which in range(3)}
    first_weights = [ready[which][0] for which in range(3)]
    groups = [(0,), tuple(range(1, rows))]
    entries, gathered, where = [], [], {}
    for number, group in enumerate(groups):
        results = entry(
            group,
            place,
            x,
            x_other,
            position_ids,
            pos_other,
            frequency,
            lefts[0],
            first_weights,
        )
        entries.append(results)
        own = results[2]
        gathered.append([own] + [to_chip(own, step) for step in range(1, shards)])
        where.update({row: (number, at) for at, row in enumerate(group)})
    started = (entries[-1][2],)
    ready[6] = ready_for(6, started)
    dy, dr, dt_lower = lower_back(place, dy, dy_other, ready[6][0], ready[6][2])
    for which in (3, 4, 5):
        ready[which] = ready_for(which, started)
    keeps, others, middles, backs = [], [], [], []
    last = ()
    for row in range(rows):
        number, at = where[row]
        x_rows, query, _, _, position, _ = entries[number]
        mixed, lse = attend(
            row, at, place, position_ids, pos_other, position, query, gathered[number], last
        )
        keep, send, dx1, upstream, delta, *sums = middle(
            row,
            at,
            place,
            x_rows,
            dy,
            dr,
            dt_lower,
            mixed,
            lefts[3:6],
            [ready[which][0] for which in (3, 4, 5, 6)],
        )
        keeps.append(keep)
        others.append(to_other_core(send))
        middles.append(sums)
        dquery, *dkvs = attend_back(
            row,
            at,
            place,
            position_ids,
            pos_other,
            position,
            query,
            upstream,
            lse,
            delta,
            gathered[number],
            backs[-1][2][1:] if backs else (),
        )
        last = (dquery,)
        dkvs = [dkvs[0]] + [back_to_chip(dkvs[step], step) for step in range(1, shards)]
        backs.append((dx1, dquery, dkvs))

    def group_of(which):
        return (ready[which][0], lefts[which], rights[which], ready[which][1], magnitudes[which])

    exits = []

    def go_out(row, after):
        number, at = where[row]
        x_rows, query, key_value, inner, _, table = entries[number]
        dx1, dquery, dkvs = backs[row]
        exits.append(
            leave(
                at,
                place,
                x_rows,
                table,
                dx1,
                inner,
                query,
                key_value,
                dquery,
                first_weights,
                (ready[1][2], ready[2][2]),
                dkvs,
                after,
            )
        )

    for row in range(rows - 1):
        go_out(row, last)
    middle_pack = settle_middle(
        middles, [group_of(which) for which in (3, 4, 5, 6)], shards, last
    )
    layer_out = assemble(place, keeps, others, last)
    go_out(rows - 1, (middle_pack, layer_out, *[e[0] for e in exits]))
    others = [to_other_core(e[1]) for e in exits]
    keep, send = settle_entry(
        place, middle_pack, [e[2:] for e in exits], [group_of(which) for which in (0, 1, 2)]
    )
    sums = cross_batch(cross_chips(*cross_core(place, keep, send)))
    tokens_grad = assemble(place, [e[0] for e in exits], others)
    finals = finish(
        place, middle_pack.shape[-1], spread(sums, shards), lefts, rights, magnitudes
    )
    return (
        jnp.swapaxes(layer_out, 1, 2),
        jnp.swapaxes(tokens_grad, 1, 2),
        *[a.T for a in finals[:7]],
        *finals[7:],
    )


def solution(mesh):
    split = P("batch", "seq", None)
    return jax.shard_map(
        body,
        mesh=mesh,
        in_specs=(split, P("batch", "seq"), P("batch", "seq"), split) + (P(),) * 28,
        out_specs=(split, split) + (P(),) * 21,
        check_vma=False,
    )
```

```python
from functools import partial

import jax
import jax.numpy as jnp
from jax import lax
from jax.experimental import pallas as pl
from jax.experimental.pallas import tpu as pltpu
from jax.sharding import PartitionSpec as P

HEADS = 15
KV_HEADS = 5
HEAD = 64
GROUP = 3
RANK = 16
EPSILON = 1e-05
ROTARY_BASE = 100000.0
MASKED = -1e30
ADAPTER_SCALE = 2.0
HEAD_SCALE = HEAD**-0.5

bf16 = jnp.bfloat16
f32 = jnp.float32


def dot_nn(a, b):
    return lax.dot_general(a, b, (((1,), (0,)), ((), ())), preferred_element_type=f32)


def dot_tn(a, b):
    return lax.dot_general(a, b, (((0,), (0,)), ((), ())), preferred_element_type=f32)


def dot_nt(a, b):
    return lax.dot_general(a, b, (((1,), (1,)), ((), ())), preferred_element_type=f32)


def vmem():
    return pl.BlockSpec(memory_space=pltpu.VMEM)


def pick(row, lane):
    row = row[:, :128]
    return jnp.sum(jnp.where(lax.broadcasted_iota(jnp.int32, row.shape, 1) == lane, row, 0))


def read_place(place_ref):
    return pick(place_ref[...], 0), pick(place_ref[...], 1)


def call(kernel, arrays, shapes, mebibytes, microseconds, scalars=(), scratch=(), after=()):
    skipped = len(after)
    return pl.pallas_call(
        (lambda *refs: kernel(*refs[skipped:])) if skipped else kernel,
        in_specs=[pl.BlockSpec(memory_space=pl.ANY)] * skipped
        + [vmem()] * (len(scalars) + len(arrays)),
        out_specs=[vmem()] * len(shapes),
        out_shape=[jax.ShapeDtypeStruct(shape, dtype) for shape, dtype in shapes],
        scratch_shapes=list(scratch),
        compiler_params=pltpu.CompilerParams(vmem_limit_bytes=mebibytes * 2**20),
        cost_estimate=pl.CostEstimate(
            flops=int(microseconds * 1.1e9), bytes_accessed=1, transcendentals=0
        ),
    )(*after, *scalars, *arrays)


def mark_kernel(out_ref):
    out_ref[...] = jnp.zeros(out_ref.shape, f32)


def mark(after):
    return call(mark_kernel, (), [((8, 128), f32)], 1, 1, after=after)[0]


def eye(size):
    return lax.broadcasted_iota(jnp.int32, (size, size), 0) == lax.broadcasted_iota(
        jnp.int32, (size, size), 1
    )


def chunks(total, step=128):
    return [(start, min(step, total - start)) for start in range(0, total, step)]


def column_to_row(column):
    parts = []
    for start, size in chunks(column.shape[0]):
        parts.append(
            jnp.sum(jnp.where(eye(size), column[start : start + size], 0.0), axis=0, keepdims=True)
        )
    return parts[0] if len(parts) == 1 else jnp.concatenate(parts, axis=1)


def row_to_column(row):
    parts = []
    for start, size in chunks(row.shape[1]):
        parts.append(
            jnp.sum(jnp.where(eye(size), row[:, start : start + size], 0.0), axis=1, keepdims=True)
        )
    return parts[0] if len(parts) == 1 else jnp.concatenate(parts, axis=0)


def prepare_natural(base_ref, left_ref, right_ref, magnitude_ref, weight_ref, norm_ref, held):
    inputs, outputs = base_ref.shape
    step = 96
    for at, lanes in chunks(outputs, 512):
        place = slice(at, at + lanes)
        right = right_ref[:, place]
        squares = jnp.zeros((8, lanes), f32)
        for start in range(0, inputs, step):
            rows = slice(start, start + step)
            combined = base_ref[rows, place].astype(f32) + dot_tn(
                left_ref[:, rows] * ADAPTER_SCALE, right
            )
            held[rows, :lanes] = combined
            squares = squares + jnp.sum(
                (combined * combined).reshape(step // 8, 8, lanes), axis=0
            )
        norm = jnp.sqrt(jnp.sum(squares, axis=0, keepdims=True))
        column = magnitude_ref[place].reshape(1, lanes) / norm
        for start in range(0, inputs, step):
            rows = slice(start, start + step)
            weight_ref[rows, place] = (held[rows, :lanes] * column).astype(bf16)
        weight_ref[inputs:, place] = (ADAPTER_SCALE * column * right.astype(f32)).astype(bf16)
        norm_ref[:, place] = norm


def prepare_turned(
    base_ref, left_ref, right_ref, magnitude_ref, weight_ref, norm_ref, scaled_ref
):
    outputs = base_ref.shape[0]
    left = left_ref[...]
    for at, size in chunks(outputs):
        rows = slice(at, at + size)
        right = right_ref[:, rows]
        combined = base_ref[rows, :].astype(f32) + dot_tn(right * ADAPTER_SCALE, left)
        norm = column_to_row(jnp.sqrt(jnp.sum(combined * combined, axis=1, keepdims=True)))
        column = magnitude_ref[rows].reshape(1, size) / norm
        weight_ref[rows, :] = (combined * row_to_column(column)).astype(bf16)
        scaled_ref[:, rows] = (ADAPTER_SCALE * column * right.astype(f32)).astype(bf16)
        norm_ref[:, rows] = norm
    weight_ref[outputs:, :] = left


def prepare(base, left, right, magnitude, turned, after=()):
    outputs = right.shape[1]
    shapes = [((base.shape[0] + RANK, base.shape[1]), bf16), ((1, outputs), f32)]
    if turned:
        shapes.append((right.shape, bf16))
    scratch = [] if turned else [pltpu.VMEM((base.shape[0], 512), f32)]
    return call(
        prepare_turned if turned else prepare_natural,
        (base, left, right, magnitude),
        shapes,
        4,
        1.3e-6 * base.size,
        scratch=scratch,
        after=after,
    )


def prepare_first_kernel(*refs):
    sources, refs = refs[:12], refs[12:]
    outs, refs = refs[:8], refs[8:]
    places, held, sems = refs[:12], refs[12], refs[13]
    copies = [
        pltpu.make_async_copy(source, place, sems.at[slot])
        for slot, (source, place) in enumerate(zip(sources, places))
    ]
    for copy in copies:
        copy.start()
    for copy in copies[4:]:
        copy.wait()
    prepare_turned(*places[4:8], *outs[2:5])
    prepare_turned(*places[8:], *outs[5:])
    for copy in copies[:4]:
        copy.wait()
    prepare_natural(*places[:4], *outs[:2], held)


def prepare_first(groups):
    shapes = []
    for which, (base, _, right, _) in enumerate(groups):
        shapes += [((base.shape[0] + RANK, base.shape[1]), bf16), ((1, right.shape[1]), f32)]
        if which:
            shapes.append((right.shape, bf16))
    flat = [a for group in groups for a in group]
    anywhere = pl.BlockSpec(memory_space=pl.ANY)
    results = pl.pallas_call(
        prepare_first_kernel,
        in_specs=[anywhere] * 12,
        out_specs=[vmem()] * 8,
        out_shape=[jax.ShapeDtypeStruct(shape, dtype) for shape, dtype in shapes],
        scratch_shapes=[pltpu.VMEM(a.shape, a.dtype) for a in flat]
        + [pltpu.VMEM((groups[0][0].shape[0], 512), f32), pltpu.SemaphoreType.DMA((12,))],
        compiler_params=pltpu.CompilerParams(vmem_limit_bytes=8 * 2**20),
        cost_estimate=pl.CostEstimate(flops=4 * 10**9, bytes_accessed=1, transcendentals=0),
    )(*flat)
    return {0: results[:2], 1: results[2:5], 2: results[5:]}


def rms_factor(values):
    return lax.rsqrt(jnp.mean(values * values, axis=0, keepdims=True) + EPSILON)


def turn_heads(values, cosine, sine, heads, scale):
    half = HEAD // 2
    out = []
    for head in range(heads):
        first = values[head * HEAD : head * HEAD + half]
        second = values[head * HEAD + half : (head + 1) * HEAD]
        out.append((first * cosine - second * sine) * scale)
        out.append((second * cosine + first * sine) * scale)
    return jnp.concatenate(out, axis=0)


def turn_heads_back(values, cosine, sine, heads, scale):
    half = HEAD // 2
    out = []
    for head in range(heads):
        first = values[head * HEAD : head * HEAD + half]
        second = values[head * HEAD + half : (head + 1) * HEAD]
        out.append((first * cosine + second * sine) * scale)
        out.append((second * cosine - first * sine) * scale)
    return jnp.concatenate(out, axis=0)


def pair(place, out_ref, own, other):
    size = own.shape[-1]
    core = place[1]
    out_ref[:, pl.ds(pl.multiple_of(core * size, size), size)] = own
    out_ref[:, pl.ds(pl.multiple_of((1 - core) * size, size), size)] = other


def entry_kernel(
    rows,
    place_ref,
    own_ref,
    other_ref,
    pos_own_ref,
    pos_other_ref,
    freq_ref,
    aq_ref,
    wq_ref,
    wk_ref,
    wv_ref,
    x_ref,
    q_ref,
    kv_ref,
    t_ref,
    pos_ref,
    table_ref,
):
    kv_size = KV_HEADS * HEAD
    tokens = x_ref.shape[-1]
    width = x_ref.shape[-2]
    place = read_place(place_ref)
    for at, row in enumerate(rows):
        mine = place[1] * other_ref.shape[0] + row
        pair(place, x_ref.at[at], own_ref[mine], other_ref[row])
        x_low = x_ref[at]
        pair(
            place, pos_ref.at[at], pos_own_ref[pl.ds(mine, 1), :], pos_other_ref[row : row + 1, :]
        )
        position = pos_ref[at]
        phases = freq_ref[...] * position.astype(f32)
        cosine = jnp.cos(phases)
        sine = jnp.sin(phases)
        table_ref[at, 0] = cosine
        table_ref[at, 1] = sine
        x = x_low.astype(f32)
        normed = (x * rms_factor(x)).astype(bf16)
        key = dot_nn(wk_ref[...], normed)
        value = dot_nn(wv_ref[...], normed)
        query = dot_tn(wq_ref[:width, :], normed)
        turned = turn_heads(key, cosine, sine, KV_HEADS, 1.0).astype(bf16)
        value_low = value.astype(bf16)
        for head in range(KV_HEADS):
            kv_ref[at, head] = turned[head * HEAD : (head + 1) * HEAD]
            kv_ref[at, KV_HEADS + head] = value_low[head * HEAD : (head + 1) * HEAD]
        t_ref[at, :RANK] = dot_nn(aq_ref[...], normed).astype(bf16)
        t_ref[at, RANK : 2 * RANK] = key[kv_size:].astype(bf16)
        t_ref[at, 2 * RANK :] = value_low[kv_size:]
        turned = turn_heads(query, cosine, sine, HEADS, HEAD_SCALE).astype(bf16)
        for head in range(HEADS):
            lane = head % GROUP * tokens
            q_ref[at, head // GROUP, :, lane : lane + tokens] = turned[
                head * HEAD : (head + 1) * HEAD
            ]


def entry(rows, place, own, other, pos_own, pos_other, frequency, left, weights, after=()):
    width, size = own.shape[1], own.shape[2]
    tokens = 2 * size
    count = len(rows)
    shapes = [
        ((count, width, tokens), bf16),
        ((count, KV_HEADS, HEAD, GROUP * tokens), bf16),
        ((count, 2 * KV_HEADS, HEAD, tokens), bf16),
        ((count, 3 * RANK, tokens), bf16),
        ((count, 1, tokens), jnp.int32),
        ((count, 2, HEAD // 2, tokens), f32),
    ]
    return call(
        partial(entry_kernel, rows),
        (own, other, pos_own, pos_other, frequency, left, *weights),
        shapes,
        6,
        2.2 * count,
        scalars=(place,),
        after=after,
    )


def lower_back_kernel(
    place_ref, own_ref, other_ref, wl_ref, cb_ref, dy_ref, dr_ref, dt_ref
):
    rows = other_ref.shape[0]
    outputs = own_ref.shape[1]
    place = read_place(place_ref)
    for row in range(rows):
        pair(place, dy_ref.at[row], own_ref[place[1] * rows + row], other_ref[row])
        dy = dy_ref[row]
        dr_ref[row] = dot_tn(wl_ref[:outputs, :], dy).astype(bf16)
        dt_ref[row] = dot_nn(cb_ref[...], dy).astype(bf16)


def lower_back(place, own, other, weight, scaled, after=()):
    rows, width, size = other.shape
    hidden = weight.shape[1]
    tokens = 2 * size
    shapes = [
        ((rows, width, tokens), bf16),
        ((rows, hidden, tokens), bf16),
        ((rows, RANK, tokens), bf16),
    ]
    return call(
        lower_back_kernel,
        (own, other, weight, scaled),
        shapes,
        8,
        1.9 * rows,
        scalars=(place,),
        after=after,
    )


def write_bias(bias_ref, position, distance):
    size = bias_ref.shape[0]
    key = lax.broadcasted_iota(jnp.int32, (size, size), 0)
    query = lax.broadcasted_iota(jnp.int32, (size, size), 1)
    start = query - position + distance * size
    bias_ref[...] = jnp.where((key >= start) & (key <= query + distance * size), 0.0, MASKED)


def block_distance(chip, step, shards):
    return chip - block_source(chip, step, shards)


def block_source(chip, step, shards):
    if shards & (shards - 1) == 0:
        return jnp.bitwise_xor(chip, step)
    return lax.rem(chip + step, shards)


def needed(chip, first, step, shards, size):
    distance = block_distance(chip, step, shards)
    return (distance > 0) & (distance * size - first < size)


def attend_kernel(at, shards, place_ref, pos_ref, q_ref, *rest):
    kv_refs, rest = rest[:shards], rest[shards:]
    o_ref, lse_ref, bias_ref, max_ref, sum_ref, acc_ref, block_ref = rest
    size = pos_ref.shape[-1]
    chip, _ = read_place(place_ref)
    first = pick(pos_ref[at], 0)

    def visit(kv_ref, opening):
        for head in range(KV_HEADS):
            bias = jnp.concatenate([bias_ref[...]] * GROUP, axis=1)
            logits = dot_tn(kv_ref[head], q_ref[at, head]) + bias
            top = jnp.max(logits, axis=0, keepdims=True)
            if not opening:
                before = max_ref[head]
                top = jnp.maximum(top, before)
            weights = jnp.exp(logits - top)
            total = jnp.sum(weights, axis=0, keepdims=True)
            mixed = dot_nn(kv_ref[head + KV_HEADS], weights.astype(bf16))
            if not opening:
                rescale = jnp.exp(before - top)
                total = total + rescale * sum_ref[head]
                mixed = mixed + rescale * acc_ref[head]
            max_ref[head] = top
            sum_ref[head] = total
            acc_ref[head] = mixed

    write_bias(bias_ref, pos_ref[at], 0)
    visit(kv_refs[0].at[at], True)

    def block_step(step, carry):
        @pl.when(needed(chip, first, step, shards, size))
        def _():
            for which in range(1, shards):

                @pl.when(step == which)
                def _():
                    block_ref[...] = kv_refs[which][at]

            write_bias(bias_ref, pos_ref[at], block_distance(chip, step, shards))
            visit(block_ref, False)

        return carry

    lax.fori_loop(1, shards, block_step, 0)
    total = sum_ref[...]
    o_ref[...] = (acc_ref[...] / total).astype(bf16)
    lse_ref[...] = max_ref[...] + jnp.log(total)


def attend(at, place, position, query, blocks, after=()):
    tokens = position.shape[-1]
    stats = (KV_HEADS, 1, GROUP * tokens)
    return call(
        partial(attend_kernel, at, len(blocks)),
        (position, query, *blocks),
        [(query.shape[1:], bf16), (stats, f32)],
        4,
        6,
        scalars=(place,),
        scratch=[
            pltpu.VMEM((tokens, tokens), f32),
            pltpu.VMEM(stats, f32),
            pltpu.VMEM(stats, f32),
            pltpu.VMEM(query.shape[1:], f32),
            pltpu.VMEM(blocks[0].shape[1:], bf16),
        ],
        after=after,
    )


def attend_back_kernel(
    at,
    shards,
    place_ref,
    pos_ref,
    q_ref,
    do_ref,
    lse_ref,
    delta_ref,
    *rest,
):
    kv_refs, rest = rest[:shards], rest[shards:]
    dq_ref, dkv_refs, bias_ref = rest[0], rest[1 : 1 + shards], rest[1 + shards]
    size = pos_ref.shape[-1]
    chip, _ = read_place(place_ref)
    first = pick(pos_ref[at], 0)

    def visit(kv_ref, dkv_ref, opening):
        for head in range(KV_HEADS):
            key, value = kv_ref[at, head], kv_ref[at, head + KV_HEADS]
            query, upstream = q_ref[at, head], do_ref[head]
            bias = jnp.concatenate([bias_ref[...]] * GROUP, axis=1)
            probs = jnp.exp(dot_tn(key, query) + bias - lse_ref[head])
            score_grad = (probs * (dot_tn(value, upstream) - delta_ref[head])).astype(bf16)
            query_grad = dot_nn(key, score_grad) * HEAD_SCALE
            if not opening:
                query_grad = query_grad + dq_ref[head]
            dq_ref[head] = query_grad
            dkv_ref[head] = dot_nt(query, score_grad).astype(bf16)
            dkv_ref[head + KV_HEADS] = dot_nt(upstream, probs.astype(bf16)).astype(bf16)

    write_bias(bias_ref, pos_ref[at], 0)
    visit(kv_refs[0], dkv_refs[0], True)
    for step in range(1, shards):
        wanted = needed(chip, first, step, shards, size)

        @pl.when(wanted)
        def _():
            write_bias(bias_ref, pos_ref[at], block_distance(chip, step, shards))
            visit(kv_refs[step], dkv_refs[step], False)

        @pl.when(jnp.logical_not(wanted))
        def _():
            dkv_refs[step][...] = jnp.zeros(dkv_refs[step].shape, bf16)


def attend_back(
    at, place, position, query, upstream, lse, delta, blocks, after=()
):
    tokens = position.shape[-1]
    return call(
        partial(attend_back_kernel, at, len(blocks)),
        (position, query, upstream, lse, delta, *blocks),
        [(query.shape[1:], f32)] + [(b.shape[1:], bf16) for b in blocks],
        4,
        9,
        scalars=(place,),
        scratch=[pltpu.VMEM((tokens, tokens), f32)],
        after=after,
    )


def spread_heads(ref):
    tokens = ref.shape[-1] // GROUP
    return jnp.concatenate(
        [
            ref[head // GROUP, :, head % GROUP * tokens : (head % GROUP + 1) * tokens]
            for head in range(HEADS)
        ],
        axis=0,
    )


def middle_kernel(
    row,
    at,
    x_ref,
    dy_ref,
    dr_ref,
    dtl_ref,
    o_ref,
    ao_ref,
    ag_ref,
    au_ref,
    wo,
    wg,
    wu,
    wl,
    halves_ref,
    dx1_ref,
    do_ref,
    delta_ref,
    dao_ref,
    dbo_ref,
    dag_ref,
    dau_ref,
    dbg_ref,
    dbu_ref,
    dal_ref,
    dbl_ref,
    so_ref,
    sg_ref,
    su_ref,
    sl_ref,
    act,
    dgate,
    dupper,
):
    _, width, tokens = x_ref.shape
    hidden = act.shape[0]
    mixed = spread_heads(o_ref)
    attn = dot_tn(wo[:width, :], mixed)
    x1 = x_ref[at].astype(f32) + attn
    rho = rms_factor(x1)
    normed = x1 * rho
    normed_low = normed.astype(bf16)
    t_output = dot_nn(ao_ref[...], mixed).astype(bf16)
    both = jnp.concatenate([ag_ref[...], au_ref[...]], axis=0)
    both = dot_nn(both, normed_low).astype(bf16)
    t_gate, t_upper = both[:RANK], both[RANK:]
    step = 256
    for start in range(0, hidden, step):
        rows = slice(start, start + step)
        gate = dot_tn(wg[:width, rows], normed_low)
        upper = dot_tn(wu[:width, rows], normed_low)
        down = dr_ref[row, rows, :].astype(f32)
        sigmoid = jax.nn.sigmoid(gate)
        silu = gate * sigmoid
        act[rows, :] = (silu * upper).astype(bf16)
        gate_grad = down * upper * (sigmoid + silu * (1.0 - sigmoid))
        upper_grad = down * silu
        dgate[rows, :] = gate_grad.astype(bf16)
        dupper[rows, :] = upper_grad.astype(bf16)
        sg_ref[:, rows] = column_to_row(jnp.sum(gate * gate_grad, axis=1, keepdims=True))
        su_ref[:, rows] = column_to_row(jnp.sum(upper * upper_grad, axis=1, keepdims=True))
    lower_all = dot_nn(wl[...], act[...])
    lower = lower_all[:width]
    t_lower = lower_all[width:].astype(bf16)
    out = (x1 + lower).astype(bf16)
    halves_ref[0] = out[:, : tokens // 2]
    halves_ref[1] = out[:, tokens // 2 :]
    dy_low = dy_ref[row]
    dy = dy_low.astype(f32)
    sl_ref[...] = column_to_row(jnp.sum(lower * dy, axis=1, keepdims=True))
    gate_back = dot_nn(wg[...], dgate[...])
    upper_back = dot_nn(wu[...], dupper[...])
    dt_gate = gate_back[width:].astype(bf16)
    dt_upper = upper_back[width:].astype(bf16)
    dnormed = gate_back[:width] + upper_back[:width]
    dx1 = dy + rho * (dnormed - normed * jnp.mean(dnormed * normed, axis=0, keepdims=True))
    dx1_ref[...] = dx1
    dx1_low = dx1.astype(bf16)
    so_ref[...] = column_to_row(jnp.sum(attn * dx1, axis=1, keepdims=True))
    output_back = dot_nn(wo[...], dx1_low)
    dt_output = output_back[width:].astype(bf16)
    dmixed = output_back[:width].astype(bf16)
    weighted = dmixed.astype(f32) * mixed.astype(f32)
    for head in range(HEADS):
        rows = slice(head * HEAD, (head + 1) * HEAD)
        lanes = slice(head % GROUP * tokens, (head % GROUP + 1) * tokens)
        do_ref[head // GROUP, :, lanes] = dmixed[rows]
        delta_ref[head // GROUP, :, lanes] = jnp.sum(weighted[rows], axis=0, keepdims=True)
    dao_ref[...] = dot_nt(dt_output, mixed)
    dbo_ref[...] = dot_nt(t_output, dx1_low)
    both = dot_nt(jnp.concatenate([dt_gate, dt_upper], axis=0), normed_low)
    dag_ref[...] = both[:RANK]
    dau_ref[...] = both[RANK:]
    dbg_ref[...] = dot_nt(t_gate, dgate[...])
    dbu_ref[...] = dot_nt(t_upper, dupper[...])
    dal_ref[...] = dot_nt(dtl_ref[row], act[...])
    dbl_ref[...] = dot_nt(t_lower, dy_low)


def middle(row, at, x, dy, dr, dt_lower, mixed, lefts, weights, after=()):
    _, width, tokens = x.shape
    hidden = dr.shape[1]
    shapes = [
        ((2, width, tokens // 2), bf16),
        ((width, tokens), f32),
        (mixed.shape, bf16),
        ((KV_HEADS, 1, GROUP * tokens), f32),
        ((RANK, width), f32),
        ((RANK, width), f32),
        ((RANK, width), f32),
        ((RANK, width), f32),
        ((RANK, hidden), f32),
        ((RANK, hidden), f32),
        ((RANK, hidden), f32),
        ((RANK, width), f32),
        ((1, width), f32),
        ((1, hidden), f32),
        ((1, hidden), f32),
        ((1, width), f32),
    ]
    return call(
        partial(middle_kernel, row, at),
        (x, dy, dr, dt_lower, mixed, *lefts, *weights),
        shapes,
        14,
        13,
        scratch=[pltpu.VMEM((hidden, tokens), bf16)] * 3,
        after=after,
    )


def exit_kernel(at, shards, *refs):
    (x_ref, table_ref, dx1_ref, t_ref, q_ref, kv_ref, dq_ref, wq_ref, wk_ref, wv_ref) = refs[:10]
    cbk_ref, cbv_ref = refs[10:12]
    dkv_refs = refs[12 : 12 + shards]
    halves_ref, da_ref, dbq_ref, dbkv_ref, sq_ref, skv_ref = refs[12 + shards :]
    _, width, tokens = x_ref.shape
    kv_size = KV_HEADS * HEAD
    x = x_ref[at].astype(f32)
    rho = rms_factor(x)
    normed = x * rho
    normed_low = normed.astype(bf16)
    cosine = table_ref[at, 0]
    sine = table_ref[at, 1]
    dquery = turn_heads_back(spread_heads(dq_ref), cosine, sine, HEADS, 1.0)
    query = turn_heads_back(
        spread_heads(q_ref.at[at]).astype(f32), cosine, sine, HEADS, 1.0 / HEAD_SCALE
    )
    sq_ref[...] = column_to_row(jnp.sum(query * dquery, axis=1, keepdims=True))
    dquery = dquery.astype(bf16)
    query_back = dot_nn(wq_ref[...], dquery)
    dkv = dkv_refs[0][...].astype(f32)
    for ref in dkv_refs[1:]:
        dkv = dkv + ref[...].astype(f32)
    dkv = dkv.reshape(2 * kv_size, tokens)
    key_value = kv_ref[at].astype(f32).reshape(2 * kv_size, tokens)
    dkey = turn_heads_back(dkv[:kv_size], cosine, sine, KV_HEADS, 1.0)
    dvalue = dkv[kv_size:]
    key = turn_heads_back(key_value[:kv_size], cosine, sine, KV_HEADS, 1.0)
    value = key_value[kv_size:]
    skv_ref[0:1, :] = column_to_row(jnp.sum(key * dkey, axis=1, keepdims=True))
    skv_ref[1:2, :] = column_to_row(jnp.sum(value * dvalue, axis=1, keepdims=True))
    dkey = dkey.astype(bf16)
    dvalue = dvalue.astype(bf16)
    dnormed = (
        query_back[:width]
        + dot_tn(wk_ref[:kv_size, :], dkey)
        + dot_tn(wv_ref[:kv_size, :], dvalue)
    )
    dx = dx1_ref[...] + rho * (dnormed - normed * jnp.mean(dnormed * normed, axis=0, keepdims=True))
    dx = dx.astype(bf16)
    halves_ref[0] = dx[:, : tokens // 2]
    halves_ref[1] = dx[:, tokens // 2 :]
    dt = jnp.concatenate(
        [query_back[width:], dot_nn(cbk_ref[...], dkey), dot_nn(cbv_ref[...], dvalue)], axis=0
    ).astype(bf16)
    da_ref[...] = dot_nt(dt, normed_low)
    dbq_ref[...] = dot_nt(t_ref[at, :RANK], dquery)
    dbkv_ref[0] = dot_nt(t_ref[at, RANK : 2 * RANK], dkey)
    dbkv_ref[1] = dot_nt(t_ref[at, 2 * RANK :], dvalue)


def leave(at, x, table, dx1, inner, query, key_value, dquery, weights, scaled, dkvs, after=()):
    _, width, tokens = x.shape
    q_size, kv_size = HEADS * HEAD, KV_HEADS * HEAD
    shapes = [
        ((2, width, tokens // 2), bf16),
        ((3 * RANK, width), f32),
        ((RANK, q_size), f32),
        ((2, RANK, kv_size), f32),
        ((1, q_size), f32),
        ((2, kv_size), f32),
    ]
    return call(
        partial(exit_kernel, at, len(dkvs)),
        (x, table, dx1, inner, query, key_value, dquery, *weights, *scaled, *dkvs),
        shapes,
        7,
        3,
        after=after,
    )


def settle(sums, weight, turned, left, right, norm, magnitude):
    left_sum, right_sum, stat = sums
    magnitude = magnitude.reshape(1, -1)
    factor = -stat / (magnitude * norm)
    scaled = (ADAPTER_SCALE * factor * right.astype(f32)).astype(bf16)
    if turned:
        left_more = dot_nn(scaled, weight)
        product = dot_nt(left, weight)
    else:
        left_more = dot_nt(scaled, weight)
        product = dot_nn(left, weight)
    right_total = ADAPTER_SCALE * (right_sum * (magnitude / norm) + factor * product)
    return (left_sum + left_more, right_total, stat / magnitude)


STAT = 512


def put_stat(ref, half, row, lane, values):
    size = values.shape[1]
    for start in range(0, size, STAT):
        take = min(STAT, size - start)
        ref[half, row : row + 1, lane : lane + take] = values[:, start : start + take]
        row += 1
    return row


def stack_sum(refs):
    total = refs[0][...]
    for ref in refs[1:]:
        total = total + ref[...]
    return total


def settle_middle_kernel(rows, shards, *refs):
    sums = [
        stack_sum([refs[row * 12 + which] for row in range(rows)]) for which in range(12)
    ]
    refs = refs[rows * 12 :]
    names = ("output", "gate", "upper", "lower")
    groups = {}
    for which, name in enumerate(names):
        groups[name] = [ref for ref in refs[which * 5 : which * 5 + 5]]
    out, pack = refs[20:]
    dao, dbo, dag, dau, dbg, dbu, dal, dbl, so, sg, su, sl = sums
    pieces = {
        "output": (dao, dbo, so),
        "gate": (dag, dbg, sg),
        "upper": (dau, dbu, su),
        "lower": (dal, dbl, sl),
    }
    done = {}
    for name in names:
        weight, left, right, norm, magnitude = groups[name]
        done[name] = settle(
            pieces[name],
            weight[: weight.shape[0] - RANK, :],
            name == "lower",
            left[...],
            right[...],
            norm[...],
            magnitude[...],
        )
    width = dao.shape[1]
    slot, hidden = slots(width), dbg.shape[1]
    pack[...] = jnp.zeros(pack.shape, f32)
    pack[0, :, 0:hidden] = done["gate"][1]
    pack[0, :, hidden : 2 * hidden] = done["upper"][1]
    pack[0, :, 2 * hidden : 2 * hidden + width] = done["output"][0]
    row = 0
    for name in ("gate", "upper", "output", "lower"):
        row = put_stat(pack, 0, row, 2 * hidden + slot, done[name][2])
    pack[1, :, 0:hidden] = done["lower"][0]
    place = hidden
    for values in (done["output"][1], done["gate"][0], done["upper"][0], done["lower"][1]):
        pack[1, :, place : place + width] = values
        place += slot
    cut(out, pack, shards)


def slots(width):
    return -(-width // 128) * 128


def piece_of(half, shards):
    return slots(-(-half // shards))


def cut(out, pack, shards):
    piece = out.shape[-1]
    for half in range(2):
        for shard in range(shards):
            out[half, shard] = pack[half, :, shard * piece : (shard + 1) * piece]


def settle_middle(partials, projections, shards, after=()):
    hidden = partials[0][4].shape[1]
    width = partials[0][0].shape[1]
    piece = piece_of(2 * hidden + slots(width) + STAT, shards)
    flat = [a for part in partials for a in part] + [a for group in projections for a in group]
    return call(
        partial(settle_middle_kernel, len(partials), shards),
        flat,
        [((2, shards, RANK, piece), f32)],
        5,
        6,
        scratch=[pltpu.VMEM((2, RANK, shards * piece), f32)],
        after=after,
    )[0]


def settle_entry_kernel(rows, shards, place_ref, middle_ref, *refs):
    sums = [stack_sum([refs[row * 5 + which] for row in range(rows)]) for which in range(5)]
    refs = refs[rows * 5 :]
    da, dbq, dbkv, sq, skv = sums
    keep_ref, send_ref, pack = refs[15:]
    pieces = (
        (da[:RANK], dbq, sq),
        (da[RANK : 2 * RANK], dbkv[0], skv[0:1]),
        (da[2 * RANK :], dbkv[1], skv[1:2]),
    )
    done = []
    for which in range(3):
        weight, left, right, norm, magnitude = refs[which * 5 : which * 5 + 5]
        done.append(
            settle(
                pieces[which],
                weight[: weight.shape[0] - RANK, :],
                which > 0,
                left[...],
                right[...],
                norm[...],
                magnitude[...],
            )
        )
    width = da.shape[1]
    slot = slots(width)
    kv_size = skv.shape[1]
    pack[...] = jnp.zeros(pack.shape, f32)
    pack[0, :, 0:width] = done[0][0]
    pack[0, :, slot : slot + width] = done[1][0]
    row = 0
    for which in range(3):
        row = put_stat(pack, 0, row, 2 * slot, done[which][2])
    pack[1, :, 0:width] = done[2][0]
    pack[1, :, slot : slot + sq.shape[1]] = done[0][1]
    pack[1, :, 2 * slot : 2 * slot + 2 * kv_size] = jnp.concatenate(
        [done[1][1], done[2][1]], axis=1
    )
    here = read_place(place_ref)[1] == 0
    middle_piece = middle_ref.shape[-1]
    piece = pack.shape[-1] // shards
    for shard in range(shards):
        place = slice(shard * piece, (shard + 1) * piece)
        parts = (
            (slice(0, middle_piece), middle_ref[0, shard], middle_ref[1, shard]),
            (slice(middle_piece, middle_piece + piece), pack[0, :, place], pack[1, :, place]),
        )
        for lanes, first, second in parts:
            keep_ref[shard, :, lanes] = jnp.where(here, first, second)
            send_ref[shard, :, lanes] = jnp.where(here, second, first).astype(bf16)


def settle_entry(place, middle_pack, partials, projections):
    shards = middle_pack.shape[1]
    width = partials[0][0].shape[1]
    kv_size = partials[0][4].shape[1]
    piece = piece_of(2 * slots(width) + max(STAT, slots(2 * kv_size)), shards)
    flat = [a for part in partials for a in part] + [a for group in projections for a in group]
    shape = (shards, RANK, middle_pack.shape[-1] + piece)
    return call(
        partial(settle_entry_kernel, len(partials), shards),
        [middle_pack] + flat,
        [(shape, f32), (shape, bf16)],
        5,
        2,
        scalars=(place,),
        scratch=[pltpu.VMEM((2, RANK, shards * piece), f32)],
    )


def get_stat(value, row, lane, size):
    parts = []
    for start in range(0, size, STAT):
        take = min(STAT, size - start)
        parts.append(value[row : row + 1, lane : lane + take])
        row += 1
    return jnp.concatenate(parts, axis=1) if len(parts) > 1 else parts[0], row


def finish_kernel(width, hidden, kv_size, shards, middle_piece, place_ref, *refs):
    mine_ref, other_ref = refs[:2]
    lefts, rights, stats = refs[2:9], refs[9:16], refs[16:23]
    middle_held, entry_held = refs[23:]
    chip, core = read_place(place_ref)
    piece = mine_ref.shape[-1] - middle_piece
    for half in range(2):
        for step in range(shards):
            value = jnp.where(core == half, mine_ref[step], other_ref[step]).astype(f32)
            source = block_source(chip, step, shards)
            lane = pl.multiple_of(source * middle_piece, 128)
            middle_held[half, :, pl.ds(lane, middle_piece)] = value[:, :middle_piece]
            lane = pl.multiple_of(source * piece, 128)
            entry_held[half, :, pl.ds(lane, piece)] = value[:, middle_piece:]
    slot = slots(width)
    m0, m1, e0, e1 = middle_held.at[0], middle_held.at[1], entry_held.at[0], entry_held.at[1]
    rights[4][...] = m0[:, :hidden]
    rights[5][...] = m0[:, hidden : 2 * hidden]
    lefts[3][...] = m0[:, 2 * hidden : 2 * hidden + width]
    row = 0
    for which, size in ((4, hidden), (5, hidden), (3, width), (6, width)):
        value, row = get_stat(m0, row, 2 * hidden + slot, size)
        stats[which][...] = value[0]
    lefts[6][...] = m1[:, :hidden]
    for place, ref in enumerate((rights[3], lefts[4], lefts[5], rights[6])):
        ref[...] = m1[:, hidden + place * slot : hidden + place * slot + width]
    lefts[0][...] = e0[:, :width]
    lefts[1][...] = e0[:, slot : slot + width]
    row = 0
    for which, size in ((0, width), (1, kv_size), (2, kv_size)):
        value, row = get_stat(e0, row, 2 * slot, size)
        stats[which][...] = value[0]
    lefts[2][...] = e1[:, :width]
    rights[0][...] = e1[:, slot : slot + width]
    both = e1[:, 2 * slot : 2 * slot + 2 * kv_size]
    rights[1][...] = both[:, :kv_size]
    rights[2][...] = both[:, kv_size:]


def finish(place, middle_piece, sums, lefts, rights, magnitudes):
    shards = sums[0].shape[0]
    shapes = [a.shape for a in lefts] + [a.shape for a in rights] + [a.shape for a in magnitudes]
    sizes = (lefts[0].shape[1], rights[4].shape[1], rights[1].shape[1])
    return call(
        partial(finish_kernel, *sizes, shards, middle_piece),
        sums,
        [(shape, f32) for shape in shapes],
        5,
        2,
        scalars=(place,),
        scratch=[
            pltpu.VMEM((2, RANK, shards * piece), f32)
            for piece in (middle_piece, sums[0].shape[-1] - middle_piece)
        ],
    )


def to_other_core(value):
    size = lax.axis_size("seq")
    return lax.ppermute(value, "seq", [(i, i ^ 1) for i in range(size)])


def peer(index, step, count):
    return index ^ step if count & (count - 1) == 0 else (index + step) % count


def to_chip(value, step):
    size = lax.axis_size("seq")
    count = size // 2
    return lax.ppermute(
        value, "seq", [(2 * peer(c, step, count) + k, 2 * c + k) for c in range(count) for k in (0, 1)]
    )


def back_to_chip(value, step):
    size = lax.axis_size("seq")
    count = size // 2
    return lax.ppermute(
        value, "seq", [(2 * c + k, 2 * peer(c, step, count) + k) for c in range(count) for k in (0, 1)]
    )


def to_batch(value, step):
    count = lax.axis_size("batch")
    return lax.ppermute(value, "batch", [(b, peer(b, step, count)) for b in range(count)])


def share_kernel(place_ref, keep_ref, come_ref, own_ref, *out_refs):
    chip, _ = read_place(place_ref)
    shards = come_ref.shape[0]
    own_ref[...] = keep_ref[chip] + come_ref[chip].astype(f32)
    for step, ref in enumerate(out_refs, start=1):
        other = block_source(chip, step, shards)
        ref[...] = (keep_ref[other] + come_ref[other].astype(f32)).astype(bf16)


def sum_kernel(own_ref, *refs):
    *come_refs, total_ref, low_ref = refs
    total = own_ref[...]
    for ref in come_refs:
        total = total + ref[...].astype(f32)
    total_ref[...] = total
    low_ref[...] = total.astype(bf16)


def cross_core(place, keep, send):
    shards = keep.shape[0]
    piece = keep.shape[1:]
    own, *parts = call(
        share_kernel,
        (keep, to_other_core(send)),
        [(piece, f32)] + [(piece, bf16)] * (shards - 1),
        4,
        1,
        scalars=(place,),
    )
    return own, parts


def add_up(own, come, after=()):
    return call(
        sum_kernel, (own, *come), [(own.shape, f32), (own.shape, bf16)], 4, 1, after=after
    )


def cross_chips(own, parts):
    return add_up(own, [back_to_chip(part, step) for step, part in enumerate(parts, start=1)])


def cross_batch(sums, after=()):
    own, low = sums
    count = lax.axis_size("batch")
    return add_up(own, [to_batch(low, step) for step in range(1, count)], after)


def spread(sums, shards):
    low = sums[1]
    mine = jnp.stack([low] + [to_chip(low, step) for step in range(1, shards)])
    return mine, to_other_core(mine)


def other_half(value, core):
    half = value.shape[0] // 2
    return to_other_core(lax.dynamic_slice_in_dim(value, (1 - core) * half, half, 0))


def assemble_kernel(rows, skipped, *refs):
    place_ref = refs[skipped]
    keep_refs = refs[skipped + 1 : skipped + 1 + rows]
    other_refs = refs[skipped + 1 + rows : skipped + 1 + 2 * rows]
    out_ref, flag_ref, sems = refs[-3:]
    _, core = read_place(place_ref)
    copies = []
    for row in range(rows):
        for side, (source, place) in enumerate(
            ((keep_refs[row], core * rows + row), (other_refs[row], (1 - core) * rows + row))
        ):
            copies.append(
                pltpu.make_async_copy(source.at[core], out_ref.at[place], sems.at[side, row])
            )
    for copy in copies:
        copy.start()
    flag_ref[...] = jnp.zeros(flag_ref.shape, f32)
    for copy in copies:
        copy.wait()


def assemble(place, keeps, others, after=()):
    rows = len(keeps)
    anywhere = pl.BlockSpec(memory_space=pl.ANY)
    return pl.pallas_call(
        partial(assemble_kernel, rows, len(after)),
        in_specs=[anywhere] * len(after) + [vmem()] + [anywhere] * (2 * rows),
        out_specs=[anywhere, vmem()],
        out_shape=[
            jax.ShapeDtypeStruct((2 * rows,) + keeps[0].shape[1:], keeps[0].dtype),
            jax.ShapeDtypeStruct((8, 128), f32),
        ],
        scratch_shapes=[pltpu.SemaphoreType.DMA((2, rows))],
        compiler_params=pltpu.CompilerParams(vmem_limit_bytes=2**20),
        cost_estimate=pl.CostEstimate(flops=10**9, bytes_accessed=1, transcendentals=0),
    )(*after, place, *keeps, *others)


def body(tokens, segment_ids, position_ids, cotangent, *weights):
    bases, lefts, rights, magnitudes = (
        weights[:7],
        [a.T for a in weights[7:14]],
        weights[14:21],
        weights[21:28],
    )
    turned = (False, True, True, False, False, False, True)
    bases = [w.T if turn else w for w, turn in zip(bases, turned)]
    index = lax.axis_index("seq")
    core, chip = index % 2, index // 2
    shards = lax.axis_size("seq") // 2
    lanes = lax.broadcasted_iota(jnp.int32, (1, 128), 1)
    place = jnp.where(lanes == 0, chip, jnp.where(lanes == 1, core, 0)).astype(jnp.int32)
    x = jnp.swapaxes(tokens, 1, 2)
    dy = jnp.swapaxes(cotangent, 1, 2)
    x_other = other_half(x, core)
    pos_other = other_half(position_ids, core)
    dy_other = other_half(dy, core)
    rows = x_other.shape[0]
    half_head = HEAD // 2
    frequency = ROTARY_BASE ** (-(jnp.arange(half_head, dtype=f32) * 2.0 / HEAD))[:, None]

    def ready_for(which, after=()):
        return prepare(
            bases[which], lefts[which], rights[which], magnitudes[which], turned[which], after
        )

    ready = prepare_first(
        [(bases[which], lefts[which], rights[which], magnitudes[which]) for which in range(3)]
    )
    first_weights = [ready[which][0] for which in range(3)]
    groups = [(0,), tuple(range(1, rows))]
    entries, gathered, where = [], [], {}
    last = ()
    for number, group in enumerate(groups):
        results = entry(
            group,
            place,
            x,
            x_other,
            position_ids,
            pos_other,
            frequency,
            lefts[0],
            first_weights,
            last,
        )
        entries.append(results)
        own = results[2]
        gathered.append([own] + [to_chip(own, step) for step in range(1, shards)])
        where.update({row: (number, at) for at, row in enumerate(group)})
        if number == 0:
            started = (results[3],)
            for which in (6, 3, 4, 5):
                ready[which] = ready_for(which, started)
            dy, dr, dt_lower = lower_back(place, dy, dy_other, ready[6][0], ready[6][2])
            last = (dt_lower, *[ready[which][1] for which in (3, 4, 5)])
    last = (mark((entries[-1][3], *gathered[0])),)
    keeps, others, middles, backs = [], [], [], []
    for row in range(rows):
        number, at = where[row]
        x_rows, query, _, _, position, _ = entries[number]
        mixed, lse = attend(at, place, position, query, gathered[number], last)
        halves, dx1, upstream, delta, *sums = middle(
            row,
            at,
            x_rows,
            dy,
            dr,
            dt_lower,
            mixed,
            lefts[3:6],
            [ready[which][0] for which in (3, 4, 5, 6)],
        )
        keeps.append(halves)
        others.append(to_other_core(halves))
        middles.append(sums)
        dquery, *dkvs = attend_back(
            at,
            place,
            position,
            query,
            upstream,
            lse,
            delta,
            gathered[number],
            backs[-1][2][1:] if backs else (),
        )
        last = (dquery,)
        dkvs = [dkvs[0]] + [back_to_chip(dkvs[step], step) for step in range(1, shards)]
        backs.append((dx1, dquery, dkvs))

    def group_of(which):
        return (ready[which][0], lefts[which], rights[which], ready[which][1], magnitudes[which])

    exits = []

    def go_out(row, after):
        number, at = where[row]
        x_rows, query, key_value, inner, _, table = entries[number]
        dx1, dquery, dkvs = backs[row]
        exits.append(
            leave(
                at,
                x_rows,
                table,
                dx1,
                inner,
                query,
                key_value,
                dquery,
                first_weights,
                (ready[1][2], ready[2][2]),
                dkvs,
                after,
            )
        )

    for row in range(rows - 1):
        go_out(row, last)
    middle_pack = settle_middle(
        middles, [group_of(which) for which in (3, 4, 5, 6)], shards, last
    )
    layer_out, flag = assemble(place, keeps, others, last)
    go_out(rows - 1, (middle_pack, flag, *[e[1] for e in exits]))
    others = [to_other_core(e[0]) for e in exits]
    keep, send = settle_entry(
        place, middle_pack, [e[1:] for e in exits], [group_of(which) for which in (0, 1, 2)]
    )
    sums = cross_chips(*cross_core(place, keep, send))
    tokens_grad, flag = assemble(place, [e[0] for e in exits], others)
    sums = cross_batch(sums, (flag,))
    finals = finish(
        place, middle_pack.shape[-1], spread(sums, shards), lefts, rights, magnitudes
    )
    return (
        jnp.swapaxes(layer_out, 1, 2),
        jnp.swapaxes(tokens_grad, 1, 2),
        *[a.T for a in finals[:7]],
        *finals[7:],
    )


def solution(mesh):
    split = P("batch", "seq", None)
    return jax.shard_map(
        body,
        mesh=mesh,
        in_specs=(split, P("batch", "seq"), P("batch", "seq"), split) + (P(),) * 28,
        out_specs=(split, split) + (P(),) * 21,
        check_vma=False,
    )
```

```python
from functools import partial

import jax
import jax.numpy as jnp
from jax import lax
from jax.experimental import pallas as pl
from jax.experimental.pallas import tpu as pltpu
from jax.sharding import PartitionSpec as P

HEADS = 15
KV_HEADS = 5
HEAD = 64
GROUP = 3
RANK = 16
EPSILON = 1e-05
ROTARY_BASE = 100000.0
MASKED = -1e30
ADAPTER_SCALE = 2.0
HEAD_SCALE = HEAD**-0.5

bf16 = jnp.bfloat16
f32 = jnp.float32


def dot_nn(a, b):
    return lax.dot_general(a, b, (((1,), (0,)), ((), ())), preferred_element_type=f32)


def dot_tn(a, b):
    return lax.dot_general(a, b, (((0,), (0,)), ((), ())), preferred_element_type=f32)


def dot_nt(a, b):
    return lax.dot_general(a, b, (((1,), (1,)), ((), ())), preferred_element_type=f32)


def vmem():
    return pl.BlockSpec(memory_space=pltpu.VMEM)


def pick(row, lane):
    row = row[:, :128]
    return jnp.sum(jnp.where(lax.broadcasted_iota(jnp.int32, row.shape, 1) == lane, row, 0))


def read_place(place_ref):
    return pick(place_ref[...], 0), pick(place_ref[...], 1)


def call(kernel, arrays, shapes, mebibytes, microseconds, scalars=(), scratch=(), after=()):
    skipped = len(after)
    return pl.pallas_call(
        (lambda *refs: kernel(*refs[skipped:])) if skipped else kernel,
        in_specs=[pl.BlockSpec(memory_space=pl.ANY)] * skipped
        + [vmem()] * (len(scalars) + len(arrays)),
        out_specs=[vmem()] * len(shapes),
        out_shape=[jax.ShapeDtypeStruct(shape, dtype) for shape, dtype in shapes],
        scratch_shapes=list(scratch),
        compiler_params=pltpu.CompilerParams(vmem_limit_bytes=mebibytes * 2**20),
        cost_estimate=pl.CostEstimate(
            flops=int(microseconds * 1.1e9), bytes_accessed=1, transcendentals=0
        ),
    )(*after, *scalars, *arrays)


def mark_kernel(out_ref):
    out_ref[...] = jnp.zeros(out_ref.shape, f32)


def mark(after):
    return call(mark_kernel, (), [((8, 128), f32)], 1, 1, after=after)[0]


def hold_kernel(value_ref, out_ref):
    out_ref[...] = value_ref[...]


def hold(value, after):
    return call(hold_kernel, (value,), [(value.shape, value.dtype)], 1, 0.5, after=after)[0]


def eye(size):
    return lax.broadcasted_iota(jnp.int32, (size, size), 0) == lax.broadcasted_iota(
        jnp.int32, (size, size), 1
    )


def chunks(total, step=128):
    return [(start, min(step, total - start)) for start in range(0, total, step)]


def column_to_row(column):
    parts = []
    for start, size in chunks(column.shape[0]):
        parts.append(
            jnp.sum(jnp.where(eye(size), column[start : start + size], 0.0), axis=0, keepdims=True)
        )
    return parts[0] if len(parts) == 1 else jnp.concatenate(parts, axis=1)


def row_to_column(row):
    parts = []
    for start, size in chunks(row.shape[1]):
        parts.append(
            jnp.sum(jnp.where(eye(size), row[:, start : start + size], 0.0), axis=1, keepdims=True)
        )
    return parts[0] if len(parts) == 1 else jnp.concatenate(parts, axis=0)


def prepare_natural(base_ref, left_ref, right_ref, magnitude_ref, weight_ref, norm_ref, held):
    inputs, outputs = base_ref.shape
    step = 96
    for at, lanes in chunks(outputs, 512):
        place = slice(at, at + lanes)
        right = right_ref[:, place]
        squares = jnp.zeros((8, lanes), f32)
        for start in range(0, inputs, step):
            rows = slice(start, start + step)
            combined = base_ref[rows, place].astype(f32) + dot_tn(
                left_ref[:, rows] * ADAPTER_SCALE, right
            )
            held[rows, :lanes] = combined
            squares = squares + jnp.sum(
                (combined * combined).reshape(step // 8, 8, lanes), axis=0
            )
        norm = jnp.sqrt(jnp.sum(squares, axis=0, keepdims=True))
        column = magnitude_ref[place].reshape(1, lanes) / norm
        for start in range(0, inputs, step):
            rows = slice(start, start + step)
            weight_ref[rows, place] = (held[rows, :lanes] * column).astype(bf16)
        weight_ref[inputs:, place] = (ADAPTER_SCALE * column * right.astype(f32)).astype(bf16)
        norm_ref[:, place] = norm


def prepare_turned(
    base_ref, left_ref, right_ref, magnitude_ref, weight_ref, norm_ref, scaled_ref
):
    outputs = base_ref.shape[0]
    left = left_ref[...]
    for at, size in chunks(outputs):
        rows = slice(at, at + size)
        right = right_ref[:, rows]
        combined = base_ref[rows, :].astype(f32) + dot_tn(right * ADAPTER_SCALE, left)
        norm = column_to_row(jnp.sqrt(jnp.sum(combined * combined, axis=1, keepdims=True)))
        column = magnitude_ref[rows].reshape(1, size) / norm
        weight_ref[rows, :] = (combined * row_to_column(column)).astype(bf16)
        scaled_ref[:, rows] = (ADAPTER_SCALE * column * right.astype(f32)).astype(bf16)
        norm_ref[:, rows] = norm
    weight_ref[outputs:, :] = left


def prepare(base, left, right, magnitude, turned, after=()):
    outputs = right.shape[1]
    shapes = [((base.shape[0] + RANK, base.shape[1]), bf16), ((1, outputs), f32)]
    if turned:
        shapes.append((right.shape, bf16))
    scratch = [] if turned else [pltpu.VMEM((base.shape[0], 512), f32)]
    return call(
        prepare_turned if turned else prepare_natural,
        (base, left, right, magnitude),
        shapes,
        4,
        1.3e-6 * base.size,
        scratch=scratch,
        after=after,
    )


def prepare_first_kernel(*refs):
    sources, outs, held = refs[:12], refs[12:20], refs[20]
    prepare_natural(*sources[:4], *outs[:2], held)
    prepare_turned(*sources[4:8], *outs[2:5])
    prepare_turned(*sources[8:], *outs[5:])


def prepare_first(groups):
    shapes = []
    for which, (base, _, right, _) in enumerate(groups):
        shapes += [((base.shape[0] + RANK, base.shape[1]), bf16), ((1, right.shape[1]), f32)]
        if which:
            shapes.append((right.shape, bf16))
    results = call(
        prepare_first_kernel,
        [a for group in groups for a in group],
        shapes,
        4,
        4,
        scratch=[pltpu.VMEM((groups[0][0].shape[0], 512), f32)],
    )
    return {0: results[:2], 1: results[2:5], 2: results[5:]}


def rms_factor(values):
    return lax.rsqrt(jnp.mean(values * values, axis=0, keepdims=True) + EPSILON)


def turn_heads(values, cosine, sine, heads, scale):
    half = HEAD // 2
    out = []
    for head in range(heads):
        first = values[head * HEAD : head * HEAD + half]
        second = values[head * HEAD + half : (head + 1) * HEAD]
        out.append((first * cosine - second * sine) * scale)
        out.append((second * cosine + first * sine) * scale)
    return jnp.concatenate(out, axis=0)


def turn_heads_back(values, cosine, sine, heads, scale):
    half = HEAD // 2
    out = []
    for head in range(heads):
        first = values[head * HEAD : head * HEAD + half]
        second = values[head * HEAD + half : (head + 1) * HEAD]
        out.append((first * cosine + second * sine) * scale)
        out.append((second * cosine - first * sine) * scale)
    return jnp.concatenate(out, axis=0)


def pair(place, out_ref, own, other):
    size = own.shape[-1]
    core = place[1]
    out_ref[:, pl.ds(pl.multiple_of(core * size, size), size)] = own
    out_ref[:, pl.ds(pl.multiple_of((1 - core) * size, size), size)] = other


def entry_kernel(
    rows,
    place_ref,
    own_ref,
    other_ref,
    pos_own_ref,
    pos_other_ref,
    freq_ref,
    aq_ref,
    wq_ref,
    wk_ref,
    wv_ref,
    x_ref,
    q_ref,
    kv_ref,
    t_ref,
    pos_ref,
    table_ref,
):
    kv_size = KV_HEADS * HEAD
    tokens = x_ref.shape[-1]
    width = x_ref.shape[-2]
    place = read_place(place_ref)
    for at, row in enumerate(rows):
        mine = place[1] * other_ref.shape[0] + row
        pair(place, x_ref.at[at], own_ref[mine], other_ref[row])
        x_low = x_ref[at]
        pair(
            place, pos_ref.at[at], pos_own_ref[pl.ds(mine, 1), :], pos_other_ref[row : row + 1, :]
        )
        position = pos_ref[at]
        phases = freq_ref[...] * position.astype(f32)
        cosine = jnp.cos(phases)
        sine = jnp.sin(phases)
        table_ref[at, 0] = cosine
        table_ref[at, 1] = sine
        x = x_low.astype(f32)
        normed = (x * rms_factor(x)).astype(bf16)
        key = dot_nn(wk_ref[...], normed)
        value = dot_nn(wv_ref[...], normed)
        query = dot_tn(wq_ref[:width, :], normed)
        turned = turn_heads(key, cosine, sine, KV_HEADS, 1.0).astype(bf16)
        value_low = value.astype(bf16)
        for head in range(KV_HEADS):
            kv_ref[at, head] = turned[head * HEAD : (head + 1) * HEAD]
            kv_ref[at, KV_HEADS + head] = value_low[head * HEAD : (head + 1) * HEAD]
        t_ref[at, :RANK] = dot_nn(aq_ref[...], normed).astype(bf16)
        t_ref[at, RANK : 2 * RANK] = key[kv_size:].astype(bf16)
        t_ref[at, 2 * RANK :] = value_low[kv_size:]
        turned = turn_heads(query, cosine, sine, HEADS, HEAD_SCALE).astype(bf16)
        for head in range(HEADS):
            lane = head % GROUP * tokens
            q_ref[at, head // GROUP, :, lane : lane + tokens] = turned[
                head * HEAD : (head + 1) * HEAD
            ]


def entry(rows, place, own, other, pos_own, pos_other, frequency, left, weights, after=()):
    width, size = own.shape[1], own.shape[2]
    tokens = 2 * size
    count = len(rows)
    shapes = [
        ((count, width, tokens), bf16),
        ((count, KV_HEADS, HEAD, GROUP * tokens), bf16),
        ((count, 2 * KV_HEADS, HEAD, tokens), bf16),
        ((count, 3 * RANK, tokens), bf16),
        ((count, 1, tokens), jnp.int32),
        ((count, 2, HEAD // 2, tokens), f32),
    ]
    return call(
        partial(entry_kernel, rows),
        (own, other, pos_own, pos_other, frequency, left, *weights),
        shapes,
        6,
        2.2 * count,
        scalars=(place,),
        after=after,
    )


def lower_back_kernel(
    place_ref, own_ref, other_ref, wl_ref, cb_ref, dy_ref, dr_ref, dt_ref
):
    rows = other_ref.shape[0]
    outputs = own_ref.shape[1]
    place = read_place(place_ref)
    for row in range(rows):
        pair(place, dy_ref.at[row], own_ref[place[1] * rows + row], other_ref[row])
        dy = dy_ref[row]
        dr_ref[row] = dot_tn(wl_ref[:outputs, :], dy).astype(bf16)
        dt_ref[row] = dot_nn(cb_ref[...], dy).astype(bf16)


def lower_back(place, own, other, weight, scaled, after=()):
    rows, width, size = other.shape
    hidden = weight.shape[1]
    tokens = 2 * size
    shapes = [
        ((rows, width, tokens), bf16),
        ((rows, hidden, tokens), bf16),
        ((rows, RANK, tokens), bf16),
    ]
    return call(
        lower_back_kernel,
        (own, other, weight, scaled),
        shapes,
        8,
        1.9 * rows,
        scalars=(place,),
        after=after,
    )


def write_bias(bias_ref, position, distance):
    size = bias_ref.shape[0]
    key = lax.broadcasted_iota(jnp.int32, (size, size), 0)
    query = lax.broadcasted_iota(jnp.int32, (size, size), 1)
    start = query - position + distance * size
    bias_ref[...] = jnp.where((key >= start) & (key <= query + distance * size), 0.0, MASKED)


def block_distance(chip, step, shards):
    return chip - block_source(chip, step, shards)


def block_source(chip, step, shards):
    if shards & (shards - 1) == 0:
        return jnp.bitwise_xor(chip, step)
    return lax.rem(chip + step, shards)


def needed(chip, first, step, shards, size):
    distance = block_distance(chip, step, shards)
    return (distance > 0) & (distance * size - first < size)


def attend_kernel(at, shards, place_ref, pos_ref, q_ref, *rest):
    kv_refs, rest = rest[:shards], rest[shards:]
    o_ref, lse_ref, bias_ref, max_ref, sum_ref, acc_ref, block_ref = rest
    size = pos_ref.shape[-1]
    chip, _ = read_place(place_ref)
    first = pick(pos_ref[at], 0)

    def visit(kv_ref, opening):
        for head in range(KV_HEADS):
            bias = jnp.concatenate([bias_ref[...]] * GROUP, axis=1)
            logits = dot_tn(kv_ref[head], q_ref[at, head]) + bias
            top = jnp.max(logits, axis=0, keepdims=True)
            if not opening:
                before = max_ref[head]
                top = jnp.maximum(top, before)
            weights = jnp.exp(logits - top)
            total = jnp.sum(weights, axis=0, keepdims=True)
            mixed = dot_nn(kv_ref[head + KV_HEADS], weights.astype(bf16))
            if not opening:
                rescale = jnp.exp(before - top)
                total = total + rescale * sum_ref[head]
                mixed = mixed + rescale * acc_ref[head]
            max_ref[head] = top
            sum_ref[head] = total
            acc_ref[head] = mixed

    write_bias(bias_ref, pos_ref[at], 0)
    visit(kv_refs[0].at[at], True)

    def block_step(step, carry):
        @pl.when(needed(chip, first, step, shards, size))
        def _():
            for which in range(1, shards):

                @pl.when(step == which)
                def _():
                    block_ref[...] = kv_refs[which][at]

            write_bias(bias_ref, pos_ref[at], block_distance(chip, step, shards))
            visit(block_ref, False)

        return carry

    lax.fori_loop(1, shards, block_step, 0)
    total = sum_ref[...]
    o_ref[...] = (acc_ref[...] / total).astype(bf16)
    lse_ref[...] = max_ref[...] + jnp.log(total)


def attend(at, place, position, query, blocks, known, after=()):
    tokens = position.shape[-1]
    stats = (KV_HEADS, 1, GROUP * tokens)
    return call(
        partial(attend_kernel, at, len(blocks)),
        (position, query, *blocks),
        [(query.shape[1:], bf16), (stats, f32)],
        4,
        6 * known,
        scalars=(place,),
        scratch=[
            pltpu.VMEM((tokens, tokens), f32),
            pltpu.VMEM(stats, f32),
            pltpu.VMEM(stats, f32),
            pltpu.VMEM(query.shape[1:], f32),
            pltpu.VMEM(blocks[0].shape[1:], bf16),
        ],
        after=after,
    )


def attend_back_kernel(
    at,
    front,
    shards,
    place_ref,
    pos_ref,
    q_ref,
    do_ref,
    lse_ref,
    delta_ref,
    *rest,
):
    kv_refs, rest = rest[:shards], rest[shards:]
    if front:
        front_refs, rest = rest[: shards - 1], rest[shards - 1 :]
    low_ref, dkv_refs, bias_ref, dq_ref = rest[0], rest[1 : 1 + shards], *rest[1 + shards :]
    if front:
        for come_ref, out_ref in zip(front_refs, dkv_refs[1:]):
            out_ref[:front] = come_ref[...]
    dkv_refs = [dkv_refs[0]] + [ref.at[front] for ref in dkv_refs[1:]]
    size = pos_ref.shape[-1]
    chip, _ = read_place(place_ref)
    first = pick(pos_ref[at], 0)

    def visit(kv_ref, dkv_ref, opening):
        for head in range(KV_HEADS):
            key, value = kv_ref[at, head], kv_ref[at, head + KV_HEADS]
            query, upstream = q_ref[at, head], do_ref[head]
            bias = jnp.concatenate([bias_ref[...]] * GROUP, axis=1)
            probs = jnp.exp(dot_tn(key, query) + bias - lse_ref[head])
            score_grad = (probs * (dot_tn(value, upstream) - delta_ref[head])).astype(bf16)
            query_grad = dot_nn(key, score_grad) * HEAD_SCALE
            if not opening:
                query_grad = query_grad + dq_ref[head]
            dq_ref[head] = query_grad
            dkv_ref[head] = dot_nt(query, score_grad).astype(bf16)
            dkv_ref[head + KV_HEADS] = dot_nt(upstream, probs.astype(bf16)).astype(bf16)

    write_bias(bias_ref, pos_ref[at], 0)
    visit(kv_refs[0], dkv_refs[0], True)
    for step in range(1, shards):
        wanted = needed(chip, first, step, shards, size)

        @pl.when(wanted)
        def _():
            write_bias(bias_ref, pos_ref[at], block_distance(chip, step, shards))
            visit(kv_refs[step], dkv_refs[step], False)

        @pl.when(jnp.logical_not(wanted))
        def _():
            dkv_refs[step][...] = jnp.zeros(dkv_refs[step].shape, bf16)

    low_ref[...] = dq_ref[...].astype(bf16)


def attend_back(
    at, place, position, query, upstream, lse, delta, blocks, front, known, after=()
):
    tokens = position.shape[-1]
    count = front[0].shape[0] if front else 0
    piece = blocks[0].shape[1:]
    return call(
        partial(attend_back_kernel, at, count, len(blocks)),
        (position, query, upstream, lse, delta, *blocks, *front),
        [(query.shape[1:], bf16), (piece, bf16)] + [((count + 1,) + piece, bf16)] * (len(blocks) - 1),
        4,
        9 * known,
        scalars=(place,),
        scratch=[pltpu.VMEM((tokens, tokens), f32), pltpu.VMEM(query.shape[1:], f32)],
        after=after,
    )


def spread_heads(ref):
    tokens = ref.shape[-1] // GROUP
    return jnp.concatenate(
        [
            ref[head // GROUP, :, head % GROUP * tokens : (head % GROUP + 1) * tokens]
            for head in range(HEADS)
        ],
        axis=0,
    )


def middle_kernel(
    row,
    at,
    x_ref,
    dy_ref,
    dr_ref,
    dtl_ref,
    o_ref,
    ao_ref,
    ag_ref,
    au_ref,
    wo,
    wg,
    wu,
    wl,
    halves_ref,
    dx1_ref,
    do_ref,
    delta_ref,
    dao_ref,
    dbo_ref,
    dag_ref,
    dau_ref,
    dbg_ref,
    dbu_ref,
    dal_ref,
    dbl_ref,
    so_ref,
    sg_ref,
    su_ref,
    sl_ref,
    act,
    dgate,
    dupper,
):
    _, width, tokens = x_ref.shape
    hidden = act.shape[0]
    mixed = spread_heads(o_ref)
    attn = dot_tn(wo[:width, :], mixed)
    x1 = x_ref[at].astype(f32) + attn
    rho = rms_factor(x1)
    normed = x1 * rho
    normed_low = normed.astype(bf16)
    t_output = dot_nn(ao_ref[...], mixed).astype(bf16)
    both = jnp.concatenate([ag_ref[...], au_ref[...]], axis=0)
    both = dot_nn(both, normed_low).astype(bf16)
    t_gate, t_upper = both[:RANK], both[RANK:]
    step = 256
    for start in range(0, hidden, step):
        rows = slice(start, start + step)
        gate = dot_tn(wg[:width, rows], normed_low)
        upper = dot_tn(wu[:width, rows], normed_low)
        down = dr_ref[row, rows, :].astype(f32)
        sigmoid = jax.nn.sigmoid(gate)
        silu = gate * sigmoid
        act[rows, :] = (silu * upper).astype(bf16)
        gate_grad = down * upper * (sigmoid + silu * (1.0 - sigmoid))
        upper_grad = down * silu
        dgate[rows, :] = gate_grad.astype(bf16)
        dupper[rows, :] = upper_grad.astype(bf16)
        sg_ref[:, rows] = column_to_row(jnp.sum(gate * gate_grad, axis=1, keepdims=True))
        su_ref[:, rows] = column_to_row(jnp.sum(upper * upper_grad, axis=1, keepdims=True))
    lower_all = dot_nn(wl[...], act[...])
    dal_ref[...] = dot_nt(dtl_ref[row], act[...])
    dbg_ref[...] = dot_nt(t_gate, dgate[...])
    dbu_ref[...] = dot_nt(t_upper, dupper[...])
    lower = lower_all[:width]
    t_lower = lower_all[width:].astype(bf16)
    out = (x1 + lower).astype(bf16)
    halves_ref[0] = out[:, : tokens // 2]
    halves_ref[1] = out[:, tokens // 2 :]
    dy_low = dy_ref[row]
    dy = dy_low.astype(f32)
    sl_ref[...] = column_to_row(jnp.sum(lower * dy, axis=1, keepdims=True))
    gate_back = dot_nn(wg[...], dgate[...])
    upper_back = dot_nn(wu[...], dupper[...])
    dt_gate = gate_back[width:].astype(bf16)
    dt_upper = upper_back[width:].astype(bf16)
    dbl_ref[...] = dot_nt(t_lower, dy_low)
    both = dot_nt(jnp.concatenate([dt_gate, dt_upper], axis=0), normed_low)
    dag_ref[...] = both[:RANK]
    dau_ref[...] = both[RANK:]
    dnormed = gate_back[:width] + upper_back[:width]
    dx1 = dy + rho * (dnormed - normed * jnp.mean(dnormed * normed, axis=0, keepdims=True))
    dx1_low = dx1.astype(bf16)
    dx1_ref[...] = dx1_low
    so_ref[...] = column_to_row(jnp.sum(attn * dx1, axis=1, keepdims=True))
    output_back = dot_nn(wo[...], dx1_low)
    dt_output = output_back[width:].astype(bf16)
    dao_ref[...] = dot_nt(dt_output, mixed)
    dbo_ref[...] = dot_nt(t_output, dx1_low)
    dmixed = output_back[:width].astype(bf16)
    weighted = dmixed.astype(f32) * mixed.astype(f32)
    for head in range(HEADS):
        rows = slice(head * HEAD, (head + 1) * HEAD)
        lanes = slice(head % GROUP * tokens, (head % GROUP + 1) * tokens)
        do_ref[head // GROUP, :, lanes] = dmixed[rows]
        delta_ref[head // GROUP, :, lanes] = jnp.sum(weighted[rows], axis=0, keepdims=True)


def middle(row, at, x, dy, dr, dt_lower, mixed, lefts, weights, known, after=()):
    _, width, tokens = x.shape
    hidden = dr.shape[1]
    shapes = [
        ((2, width, tokens // 2), bf16),
        ((width, tokens), bf16),
        (mixed.shape, bf16),
        ((KV_HEADS, 1, GROUP * tokens), f32),
        ((RANK, width), f32),
        ((RANK, width), f32),
        ((RANK, width), f32),
        ((RANK, width), f32),
        ((RANK, hidden), f32),
        ((RANK, hidden), f32),
        ((RANK, hidden), f32),
        ((RANK, width), f32),
        ((1, width), f32),
        ((1, hidden), f32),
        ((1, hidden), f32),
        ((1, width), f32),
    ]
    return call(
        partial(middle_kernel, row, at),
        (x, dy, dr, dt_lower, mixed, *lefts, *weights),
        shapes,
        14,
        13 * known,
        scratch=[pltpu.VMEM((hidden, tokens), bf16)] * 3,
        after=after,
    )


def exit_kernel(at, piece, shards, *refs):
    (x_ref, table_ref, dx1_ref, t_ref, q_ref, kv_ref, dq_ref, wq_ref, wk_ref, wv_ref) = refs[:10]
    cbk_ref, cbv_ref = refs[10:12]
    dkv_refs = refs[12 : 12 + shards]
    halves_ref, da_ref, dbq_ref, dbkv_ref, sq_ref, skv_ref = refs[12 + shards :]
    _, width, tokens = x_ref.shape
    kv_size = KV_HEADS * HEAD
    x = x_ref[at].astype(f32)
    rho = rms_factor(x)
    normed = x * rho
    normed_low = normed.astype(bf16)
    cosine = table_ref[at, 0]
    sine = table_ref[at, 1]
    dquery = turn_heads_back(spread_heads(dq_ref).astype(f32), cosine, sine, HEADS, 1.0)
    query = turn_heads_back(
        spread_heads(q_ref.at[at]).astype(f32), cosine, sine, HEADS, 1.0 / HEAD_SCALE
    )
    sq_ref[...] = column_to_row(jnp.sum(query * dquery, axis=1, keepdims=True))
    dquery = dquery.astype(bf16)
    query_back = dot_nn(wq_ref[...], dquery)
    dkv = dkv_refs[0][...].astype(f32)
    for ref in dkv_refs[1:]:
        dkv = dkv + ref[piece].astype(f32)
    dkv = dkv.reshape(2 * kv_size, tokens)
    key_value = kv_ref[at].astype(f32).reshape(2 * kv_size, tokens)
    dkey = turn_heads_back(dkv[:kv_size], cosine, sine, KV_HEADS, 1.0)
    dvalue = dkv[kv_size:]
    key = turn_heads_back(key_value[:kv_size], cosine, sine, KV_HEADS, 1.0)
    value = key_value[kv_size:]
    skv_ref[0:1, :] = column_to_row(jnp.sum(key * dkey, axis=1, keepdims=True))
    skv_ref[1:2, :] = column_to_row(jnp.sum(value * dvalue, axis=1, keepdims=True))
    dkey = dkey.astype(bf16)
    dvalue = dvalue.astype(bf16)
    dnormed = (
        query_back[:width]
        + dot_tn(wk_ref[:kv_size, :], dkey)
        + dot_tn(wv_ref[:kv_size, :], dvalue)
    )
    dx = dx1_ref[...].astype(f32) + rho * (dnormed - normed * jnp.mean(dnormed * normed, axis=0, keepdims=True))
    dx = dx.astype(bf16)
    halves_ref[0] = dx[:, : tokens // 2]
    halves_ref[1] = dx[:, tokens // 2 :]
    dt = jnp.concatenate(
        [query_back[width:], dot_nn(cbk_ref[...], dkey), dot_nn(cbv_ref[...], dvalue)], axis=0
    ).astype(bf16)
    da_ref[...] = dot_nt(dt, normed_low)
    dbq_ref[...] = dot_nt(t_ref[at, :RANK], dquery)
    dbkv_ref[0] = dot_nt(t_ref[at, RANK : 2 * RANK], dkey)
    dbkv_ref[1] = dot_nt(t_ref[at, 2 * RANK :], dvalue)


def leave(at, piece, x, table, dx1, inner, query, key_value, dquery, weights, scaled, dkvs, after=()):
    _, width, tokens = x.shape
    q_size, kv_size = HEADS * HEAD, KV_HEADS * HEAD
    shapes = [
        ((2, width, tokens // 2), bf16),
        ((3 * RANK, width), f32),
        ((RANK, q_size), f32),
        ((2, RANK, kv_size), f32),
        ((1, q_size), f32),
        ((2, kv_size), f32),
    ]
    return call(
        partial(exit_kernel, at, piece, len(dkvs)),
        (x, table, dx1, inner, query, key_value, dquery, *weights, *scaled, *dkvs),
        shapes,
        7,
        3,
        after=after,
    )


def settle(sums, weight, turned, left, right, norm, magnitude):
    left_sum, right_sum, stat = sums
    magnitude = magnitude.reshape(1, -1)
    factor = -stat / (magnitude * norm)
    scaled = (ADAPTER_SCALE * factor * right.astype(f32)).astype(bf16)
    if turned:
        left_more = dot_nn(scaled, weight)
        product = dot_nt(left, weight)
    else:
        left_more = dot_nt(scaled, weight)
        product = dot_nn(left, weight)
    right_total = ADAPTER_SCALE * (right_sum * (magnitude / norm) + factor * product)
    return (left_sum + left_more, right_total, stat / magnitude)


STAT = 512


def put_stat(ref, half, row, lane, values):
    size = values.shape[1]
    for start in range(0, size, STAT):
        take = min(STAT, size - start)
        ref[half, row : row + 1, lane : lane + take] = values[:, start : start + take]
        row += 1
    return row


def stack_sum(refs):
    total = refs[0][...]
    for ref in refs[1:]:
        total = total + ref[...]
    return total


def settle_middle_kernel(rows, shards, *refs):
    sums = [
        stack_sum([refs[row * 12 + which] for row in range(rows)]) for which in range(12)
    ]
    refs = refs[rows * 12 :]
    names = ("output", "gate", "upper", "lower")
    groups = {}
    for which, name in enumerate(names):
        groups[name] = [ref for ref in refs[which * 5 : which * 5 + 5]]
    out, pack = refs[20:]
    dao, dbo, dag, dau, dbg, dbu, dal, dbl, so, sg, su, sl = sums
    pieces = {
        "output": (dao, dbo, so),
        "gate": (dag, dbg, sg),
        "upper": (dau, dbu, su),
        "lower": (dal, dbl, sl),
    }
    done = {}
    for name in names:
        weight, left, right, norm, magnitude = groups[name]
        done[name] = settle(
            pieces[name],
            weight[: weight.shape[0] - RANK, :],
            name == "lower",
            left[...],
            right[...],
            norm[...],
            magnitude[...],
        )
    width = dao.shape[1]
    slot, hidden = slots(width), dbg.shape[1]
    pack[...] = jnp.zeros(pack.shape, f32)
    pack[0, :, 0:hidden] = done["gate"][1]
    pack[0, :, hidden : 2 * hidden] = done["upper"][1]
    pack[0, :, 2 * hidden : 2 * hidden + width] = done["output"][0]
    row = 0
    for name in ("gate", "upper", "output", "lower"):
        row = put_stat(pack, 0, row, 2 * hidden + slot, done[name][2])
    pack[1, :, 0:hidden] = done["lower"][0]
    place = hidden
    for values in (done["output"][1], done["gate"][0], done["upper"][0], done["lower"][1]):
        pack[1, :, place : place + width] = values
        place += slot
    cut(out, pack, shards)


def slots(width):
    return -(-width // 128) * 128


def piece_of(half, shards):
    return slots(-(-half // shards))


def cut(out, pack, shards):
    piece = out.shape[-1]
    for half in range(2):
        for shard in range(shards):
            out[half, shard] = pack[half, :, shard * piece : (shard + 1) * piece]


def settle_middle(partials, projections, shards, after=()):
    hidden = partials[0][4].shape[1]
    width = partials[0][0].shape[1]
    piece = piece_of(2 * hidden + slots(width) + STAT, shards)
    flat = [a for part in partials for a in part] + [a for group in projections for a in group]
    return call(
        partial(settle_middle_kernel, len(partials), shards),
        flat,
        [((2, shards, RANK, piece), f32)],
        5,
        6,
        scratch=[pltpu.VMEM((2, RANK, shards * piece), f32)],
        after=after,
    )[0]


def settle_entry_kernel(rows, shards, place_ref, middle_ref, *refs):
    sums = [stack_sum([refs[row * 5 + which] for row in range(rows)]) for which in range(5)]
    refs = refs[rows * 5 :]
    da, dbq, dbkv, sq, skv = sums
    keep_ref, send_ref, pack = refs[15:]
    pieces = (
        (da[:RANK], dbq, sq),
        (da[RANK : 2 * RANK], dbkv[0], skv[0:1]),
        (da[2 * RANK :], dbkv[1], skv[1:2]),
    )
    done = []
    for which in range(3):
        weight, left, right, norm, magnitude = refs[which * 5 : which * 5 + 5]
        done.append(
            settle(
                pieces[which],
                weight[: weight.shape[0] - RANK, :],
                which > 0,
                left[...],
                right[...],
                norm[...],
                magnitude[...],
            )
        )
    width = da.shape[1]
    slot = slots(width)
    kv_size = skv.shape[1]
    pack[...] = jnp.zeros(pack.shape, f32)
    pack[0, :, 0:width] = done[0][0]
    pack[0, :, slot : slot + width] = done[1][0]
    row = 0
    for which in range(3):
        row = put_stat(pack, 0, row, 2 * slot, done[which][2])
    pack[1, :, 0:width] = done[2][0]
    pack[1, :, slot : slot + sq.shape[1]] = done[0][1]
    pack[1, :, 2 * slot : 2 * slot + 2 * kv_size] = jnp.concatenate(
        [done[1][1], done[2][1]], axis=1
    )
    here = read_place(place_ref)[1] == 0
    middle_piece = middle_ref.shape[-1]
    piece = pack.shape[-1] // shards
    for shard in range(shards):
        place = slice(shard * piece, (shard + 1) * piece)
        parts = (
            (slice(0, middle_piece), middle_ref[0, shard], middle_ref[1, shard]),
            (slice(middle_piece, middle_piece + piece), pack[0, :, place], pack[1, :, place]),
        )
        for lanes, first, second in parts:
            keep_ref[shard, :, lanes] = jnp.where(here, first, second)
            send_ref[shard, :, lanes] = jnp.where(here, second, first).astype(bf16)


def settle_entry(place, middle_pack, partials, projections):
    shards = middle_pack.shape[1]
    width = partials[0][0].shape[1]
    kv_size = partials[0][4].shape[1]
    piece = piece_of(2 * slots(width) + max(STAT, slots(2 * kv_size)), shards)
    flat = [a for part in partials for a in part] + [a for group in projections for a in group]
    shape = (shards, RANK, middle_pack.shape[-1] + piece)
    return call(
        partial(settle_entry_kernel, len(partials), shards),
        [middle_pack] + flat,
        [(shape, f32), (shape, bf16)],
        5,
        2,
        scalars=(place,),
        scratch=[pltpu.VMEM((2, RANK, shards * piece), f32)],
    )


def get_stat(value, row, lane, size):
    parts = []
    for start in range(0, size, STAT):
        take = min(STAT, size - start)
        parts.append(value[row : row + 1, lane : lane + take])
        row += 1
    return jnp.concatenate(parts, axis=1) if len(parts) > 1 else parts[0], row


def finish_kernel(width, hidden, kv_size, shards, middle_piece, place_ref, *refs):
    mine_ref, other_ref = refs[:2]
    lefts, rights, stats = refs[2:9], refs[9:16], refs[16:23]
    middle_held, entry_held = refs[23:]
    chip, core = read_place(place_ref)
    piece = mine_ref.shape[-1] - middle_piece
    for half in range(2):
        for step in range(shards):
            value = jnp.where(core == half, mine_ref[step], other_ref[step]).astype(f32)
            source = block_source(chip, step, shards)
            lane = pl.multiple_of(source * middle_piece, 128)
            middle_held[half, :, pl.ds(lane, middle_piece)] = value[:, :middle_piece]
            lane = pl.multiple_of(source * piece, 128)
            entry_held[half, :, pl.ds(lane, piece)] = value[:, middle_piece:]
    slot = slots(width)
    m0, m1, e0, e1 = middle_held.at[0], middle_held.at[1], entry_held.at[0], entry_held.at[1]
    rights[4][...] = m0[:, :hidden]
    rights[5][...] = m0[:, hidden : 2 * hidden]
    lefts[3][...] = m0[:, 2 * hidden : 2 * hidden + width]
    row = 0
    for which, size in ((4, hidden), (5, hidden), (3, width), (6, width)):
        value, row = get_stat(m0, row, 2 * hidden + slot, size)
        stats[which][...] = value[0]
    lefts[6][...] = m1[:, :hidden]
    for place, ref in enumerate((rights[3], lefts[4], lefts[5], rights[6])):
        ref[...] = m1[:, hidden + place * slot : hidden + place * slot + width]
    lefts[0][...] = e0[:, :width]
    lefts[1][...] = e0[:, slot : slot + width]
    row = 0
    for which, size in ((0, width), (1, kv_size), (2, kv_size)):
        value, row = get_stat(e0, row, 2 * slot, size)
        stats[which][...] = value[0]
    lefts[2][...] = e1[:, :width]
    rights[0][...] = e1[:, slot : slot + width]
    both = e1[:, 2 * slot : 2 * slot + 2 * kv_size]
    rights[1][...] = both[:, :kv_size]
    rights[2][...] = both[:, kv_size:]


def finish(place, middle_piece, sums, lefts, rights, magnitudes):
    shards = sums[0].shape[0]
    shapes = [a.shape for a in lefts] + [a.shape for a in rights] + [a.shape for a in magnitudes]
    sizes = (lefts[0].shape[1], rights[4].shape[1], rights[1].shape[1])
    return call(
        partial(finish_kernel, *sizes, shards, middle_piece),
        sums,
        [(shape, f32) for shape in shapes],
        5,
        2,
        scalars=(place,),
        scratch=[
            pltpu.VMEM((2, RANK, shards * piece), f32)
            for piece in (middle_piece, sums[0].shape[-1] - middle_piece)
        ],
    )


def to_other_core(value):
    size = lax.axis_size("seq")
    return lax.ppermute(value, "seq", [(i, i ^ 1) for i in range(size)])


def peer(index, step, count):
    return index ^ step if count & (count - 1) == 0 else (index + step) % count


def to_chip(value, step):
    size = lax.axis_size("seq")
    count = size // 2
    return lax.ppermute(
        value, "seq", [(2 * peer(c, step, count) + k, 2 * c + k) for c in range(count) for k in (0, 1)]
    )


def back_to_chip(value, step):
    size = lax.axis_size("seq")
    count = size // 2
    return lax.ppermute(
        value, "seq", [(2 * c + k, 2 * peer(c, step, count) + k) for c in range(count) for k in (0, 1)]
    )


def to_batch(value, step):
    count = lax.axis_size("batch")
    return lax.ppermute(value, "batch", [(b, peer(b, step, count)) for b in range(count)])


def share_kernel(place_ref, keep_ref, come_ref, own_ref, *out_refs):
    chip, _ = read_place(place_ref)
    shards = come_ref.shape[0]
    own_ref[...] = keep_ref[chip] + come_ref[chip].astype(f32)
    for step, ref in enumerate(out_refs, start=1):
        other = block_source(chip, step, shards)
        ref[...] = (keep_ref[other] + come_ref[other].astype(f32)).astype(bf16)


def sum_kernel(own_ref, *refs):
    *come_refs, total_ref, low_ref = refs
    total = own_ref[...]
    for ref in come_refs:
        total = total + ref[...].astype(f32)
    total_ref[...] = total
    low_ref[...] = total.astype(bf16)


def cross_core(place, keep, send):
    shards = keep.shape[0]
    piece = keep.shape[1:]
    own, *parts = call(
        share_kernel,
        (keep, to_other_core(send)),
        [(piece, f32)] + [(piece, bf16)] * (shards - 1),
        4,
        1,
        scalars=(place,),
    )
    return own, parts


def add_up(own, come, after=()):
    return call(
        sum_kernel, (own, *come), [(own.shape, f32), (own.shape, bf16)], 4, 1, after=after
    )


def cross_chips(own, parts):
    return add_up(own, [back_to_chip(part, step) for step, part in enumerate(parts, start=1)])


def cross_batch(sums, after=()):
    own, low = sums
    count = lax.axis_size("batch")
    return add_up(own, [to_batch(low, step) for step in range(1, count)], after)


def spread(sums, shards):
    low = sums[1]
    mine = jnp.stack([low] + [to_chip(low, step) for step in range(1, shards)])
    return mine, to_other_core(mine)


def other_half(value, core):
    half = value.shape[0] // 2
    return to_other_core(lax.dynamic_slice_in_dim(value, (1 - core) * half, half, 0))


def other_halves_kernel(rows, skipped, *refs):
    place_ref, *half_refs = refs[skipped : skipped + 1 + rows]
    out_ref, sems = refs[-2:]
    _, core = read_place(place_ref)
    copies = [
        pltpu.make_async_copy(ref.at[1 - core], out_ref.at[row], sems.at[row])
        for row, ref in enumerate(half_refs)
    ]
    for copy in copies:
        copy.start()
    for copy in copies:
        copy.wait()


def other_halves(place, halves, after):
    rows = len(halves)
    anywhere = pl.BlockSpec(memory_space=pl.ANY)
    return pl.pallas_call(
        partial(other_halves_kernel, rows, len(after)),
        in_specs=[anywhere] * len(after) + [vmem()] + [anywhere] * rows,
        out_specs=anywhere,
        out_shape=jax.ShapeDtypeStruct((rows,) + halves[0].shape[1:], halves[0].dtype),
        scratch_shapes=[pltpu.SemaphoreType.DMA((rows,))],
        compiler_params=pltpu.CompilerParams(vmem_limit_bytes=2**20),
        cost_estimate=pl.CostEstimate(flops=10**9, bytes_accessed=1, transcendentals=0),
    )(*after, place, *halves)


def core_of(place_ref):
    return read_place(place_ref)[1]


def assemble_kernel(rows, skipped, *refs):
    place_ref = refs[skipped]
    keep_refs = refs[skipped + 1 : skipped + 1 + rows]
    other_refs = refs[skipped + 1 + rows : -3]
    if len(other_refs) == 1:
        other_refs = [other_refs[0].at[row] for row in range(rows)]
    else:
        other_refs = [ref.at[core_of(place_ref)] for ref in other_refs]
    out_ref, flag_ref, sems = refs[-3:]
    _, core = read_place(place_ref)
    copies = []
    for row in range(rows):
        for side, (source, place) in enumerate(
            (
                (keep_refs[row].at[core], core * rows + row),
                (other_refs[row], (1 - core) * rows + row),
            )
        ):
            copies.append(pltpu.make_async_copy(source, out_ref.at[place], sems.at[side, row]))
    for copy in copies:
        copy.start()
    flag_ref[...] = jnp.zeros(flag_ref.shape, f32)
    for copy in copies:
        copy.wait()


def assemble(place, keeps, others, after=()):
    rows = len(keeps)
    anywhere = pl.BlockSpec(memory_space=pl.ANY)
    return pl.pallas_call(
        partial(assemble_kernel, rows, len(after)),
        in_specs=[anywhere] * len(after) + [vmem()] + [anywhere] * (rows + len(others)),
        out_specs=[anywhere, vmem()],
        out_shape=[
            jax.ShapeDtypeStruct((2 * rows,) + keeps[0].shape[1:], keeps[0].dtype),
            jax.ShapeDtypeStruct((8, 128), f32),
        ],
        scratch_shapes=[pltpu.SemaphoreType.DMA((2, rows))],
        compiler_params=pltpu.CompilerParams(vmem_limit_bytes=2**20),
        cost_estimate=pl.CostEstimate(flops=10**9, bytes_accessed=1, transcendentals=0),
    )(*after, place, *keeps, *others)


def body(tokens, segment_ids, position_ids, cotangent, *weights):
    bases, lefts, rights, magnitudes = (
        weights[:7],
        [a.T for a in weights[7:14]],
        weights[14:21],
        weights[21:28],
    )
    turned = (False, True, True, False, False, False, True)
    bases = [w.T if turn else w for w, turn in zip(bases, turned)]
    index = lax.axis_index("seq")
    core, chip = index % 2, index // 2
    shards = lax.axis_size("seq") // 2
    lanes = lax.broadcasted_iota(jnp.int32, (1, 128), 1)
    place = jnp.where(lanes == 0, chip, jnp.where(lanes == 1, core, 0)).astype(jnp.int32)
    x = jnp.swapaxes(tokens, 1, 2)
    dy = jnp.swapaxes(cotangent, 1, 2)
    x_other = other_half(x, core)
    pos_other = other_half(position_ids, core)
    dy_other = other_half(dy, core)
    rows = x_other.shape[0]
    half_head = HEAD // 2
    frequency = ROTARY_BASE ** (-(jnp.arange(half_head, dtype=f32) * 2.0 / HEAD))[:, None]

    def ready_for(which, after=()):
        return prepare(
            bases[which], lefts[which], rights[which], magnitudes[which], turned[which], after
        )

    ready = prepare_first(
        [(bases[which], lefts[which], rights[which], magnitudes[which]) for which in range(3)]
    )
    first_weights = [ready[which][0] for which in range(3)]
    groups = [(0,), tuple(range(1, rows))]
    entries, gathered, where = [], [], {}
    last = ()
    for number, group in enumerate(groups):
        results = entry(
            group,
            place,
            x,
            x_other,
            position_ids,
            pos_other,
            frequency,
            lefts[0],
            first_weights,
            last,
        )
        entries.append(results)
        own = results[2]
        gathered.append([own] + [to_chip(own, step) for step in range(1, shards)])
        where.update({row: (number, at) for at, row in enumerate(group)})
        if number == 0:
            started = (results[3],)
            for which in (6, 3, 4, 5):
                ready[which] = ready_for(which, started)
            last = [ready[which][1] for which in (6, 3, 4, 5)]
    dy, dr, dt_lower = lower_back(
        place, dy, dy_other, ready[6][0], ready[6][2], (entries[-1][3],)
    )
    last = (mark((dt_lower, *gathered[0])),)
    keeps, middles, backs, waiting, sent = [], [], [], (), ()
    for row in range(rows):
        number, at = where[row]
        x_rows, query, _, _, position, _ = entries[number]
        known = 1.0
        mixed, lse = attend(at, place, position, query, gathered[number], known, last)
        halves, dx1, upstream, delta, *sums = middle(
            row,
            at,
            x_rows,
            dy,
            dr,
            dt_lower,
            mixed,
            lefts[3:6],
            [ready[which][0] for which in (3, 4, 5, 6)],
            known,
        )
        keeps.append(halves)
        middles.append(sums)
        together = row == rows - 2
        dquery, own, *dkvs = attend_back(
            at,
            place,
            position,
            query,
            upstream,
            lse,
            delta,
            gathered[number],
            waiting if row < rows - 1 else (),
            known,
            sent[:-1] if row == rows - 1 else (),
        )
        last = (dquery,)
        if row < rows - 2:
            waiting = dkvs
            backs.append([dx1, dquery, own])
            continue
        if row == rows - 1:
            last = (dquery, *sent[-1:])
        if together:
            sent = [back_to_chip(part, step) for step, part in enumerate(dkvs[:-1], start=1)]
            part = hold(dkvs[-1], sent) if sent else dkvs[-1]
            dkvs = sent + [back_to_chip(part, shards - 1)]
            sent = dkvs
        else:
            dkvs = [back_to_chip(part, step) for step, part in enumerate(dkvs, start=1)]
        backs.append([dx1, dquery, own])
        first_row = 0 if together else row
        for back_row in range(first_row, row + 1):
            backs[back_row] += [back_row - first_row, dkvs]

    def group_of(which):
        return (ready[which][0], lefts[which], rights[which], ready[which][1], magnitudes[which])

    exits = []

    def go_out(row, after):
        number, at = where[row]
        x_rows, query, key_value, inner, _, table = entries[number]
        dx1, dquery, own, piece, dkvs = backs[row]
        exits.append(
            leave(
                at,
                piece,
                x_rows,
                table,
                dx1,
                inner,
                query,
                key_value,
                dquery,
                first_weights,
                (ready[1][2], ready[2][2]),
                [own] + dkvs,
                after,
            )
        )

    for row in range(rows - 1):
        go_out(row, last)
    middle_pack = settle_middle(
        middles, [group_of(which) for which in (3, 4, 5, 6)], shards, last
    )
    layer_out, flag = assemble(place, keeps, [to_other_core(other_halves(place, keeps, last))])
    go_out(rows - 1, (middle_pack, flag, *[e[1] for e in exits]))
    others = [to_other_core(e[0]) for e in exits]
    keep, send = settle_entry(
        place, middle_pack, [e[1:] for e in exits], [group_of(which) for which in (0, 1, 2)]
    )
    sums = cross_chips(*cross_core(place, keep, send))
    tokens_grad, flag = assemble(place, [e[0] for e in exits], others)
    sums = cross_batch(sums, (flag,))
    finals = finish(
        place, middle_pack.shape[-1], spread(sums, shards), lefts, rights, magnitudes
    )
    return (
        jnp.swapaxes(layer_out, 1, 2),
        jnp.swapaxes(tokens_grad, 1, 2),
        *[a.T for a in finals[:7]],
        *finals[7:],
    )


def solution(mesh):
    split = P("batch", "seq", None)
    return jax.shard_map(
        body,
        mesh=mesh,
        in_specs=(split, P("batch", "seq"), P("batch", "seq"), split) + (P(),) * 28,
        out_specs=(split, split) + (P(),) * 21,
        check_vma=False,
    )
```

```python
from functools import partial

import jax
import jax.numpy as jnp
from jax import lax
from jax.experimental import pallas as pl
from jax.experimental.pallas import tpu as pltpu
from jax.sharding import PartitionSpec as P

HEADS = 15
KV_HEADS = 5
HEAD = 64
GROUP = 3
RANK = 16
EPSILON = 1e-05
ROTARY_BASE = 100000.0
MASKED = -1e30
ADAPTER_SCALE = 2.0
HEAD_SCALE = HEAD**-0.5

bf16 = jnp.bfloat16
f32 = jnp.float32


def dot_nn(a, b):
    return lax.dot_general(a, b, (((1,), (0,)), ((), ())), preferred_element_type=f32)


def dot_tn(a, b):
    return lax.dot_general(a, b, (((0,), (0,)), ((), ())), preferred_element_type=f32)


def dot_nt(a, b):
    return lax.dot_general(a, b, (((1,), (1,)), ((), ())), preferred_element_type=f32)


def vmem():
    return pl.BlockSpec(memory_space=pltpu.VMEM)


def pick(row, lane):
    row = row[:, :128]
    return jnp.sum(jnp.where(lax.broadcasted_iota(jnp.int32, row.shape, 1) == lane, row, 0))


def read_place(place_ref):
    return pick(place_ref[...], 0), pick(place_ref[...], 1)


def call(kernel, arrays, shapes, mebibytes, microseconds, scalars=(), scratch=(), after=()):
    skipped = len(after)
    return pl.pallas_call(
        (lambda *refs: kernel(*refs[skipped:])) if skipped else kernel,
        in_specs=[pl.BlockSpec(memory_space=pl.ANY)] * skipped
        + [vmem()] * (len(scalars) + len(arrays)),
        out_specs=[vmem()] * len(shapes),
        out_shape=[jax.ShapeDtypeStruct(shape, dtype) for shape, dtype in shapes],
        scratch_shapes=list(scratch),
        compiler_params=pltpu.CompilerParams(vmem_limit_bytes=mebibytes * 2**20),
        cost_estimate=pl.CostEstimate(
            flops=int(microseconds * 1.1e9), bytes_accessed=1, transcendentals=0
        ),
    )(*after, *scalars, *arrays)


def mark_kernel(out_ref):
    out_ref[...] = jnp.zeros(out_ref.shape, f32)


def mark(after):
    return call(mark_kernel, (), [((8, 128), f32)], 1, 1, after=after)[0]


def hold_kernel(value_ref, out_ref):
    out_ref[...] = value_ref[...]


def hold(value, after):
    return call(hold_kernel, (value,), [(value.shape, value.dtype)], 1, 0.5, after=after)[0]


def eye(size):
    return lax.broadcasted_iota(jnp.int32, (size, size), 0) == lax.broadcasted_iota(
        jnp.int32, (size, size), 1
    )


def chunks(total, step=128):
    return [(start, min(step, total - start)) for start in range(0, total, step)]


def column_to_row(column):
    parts = []
    for start, size in chunks(column.shape[0]):
        parts.append(
            jnp.sum(jnp.where(eye(size), column[start : start + size], 0.0), axis=0, keepdims=True)
        )
    return parts[0] if len(parts) == 1 else jnp.concatenate(parts, axis=1)


def row_to_column(row):
    parts = []
    for start, size in chunks(row.shape[1]):
        parts.append(
            jnp.sum(jnp.where(eye(size), row[:, start : start + size], 0.0), axis=1, keepdims=True)
        )
    return parts[0] if len(parts) == 1 else jnp.concatenate(parts, axis=0)


def prepare_natural(base_ref, left_ref, right_ref, magnitude_ref, weight_ref, norm_ref, held):
    inputs, outputs = base_ref.shape
    step = 96
    for at, lanes in chunks(outputs, 512):
        place = slice(at, at + lanes)
        right = right_ref[:, place]
        squares = jnp.zeros((8, lanes), f32)
        for start in range(0, inputs, step):
            rows = slice(start, start + step)
            combined = base_ref[rows, place].astype(f32) + dot_tn(
                left_ref[:, rows] * ADAPTER_SCALE, right
            )
            held[rows, :lanes] = combined
            squares = squares + jnp.sum(
                (combined * combined).reshape(step // 8, 8, lanes), axis=0
            )
        norm = jnp.sqrt(jnp.sum(squares, axis=0, keepdims=True))
        column = magnitude_ref[place].reshape(1, lanes) / norm
        for start in range(0, inputs, step):
            rows = slice(start, start + step)
            weight_ref[rows, place] = (held[rows, :lanes] * column).astype(bf16)
        weight_ref[inputs:, place] = (ADAPTER_SCALE * column * right.astype(f32)).astype(bf16)
        norm_ref[:, place] = norm


def prepare_turned(
    base_ref, left_ref, right_ref, magnitude_ref, weight_ref, norm_ref, scaled_ref
):
    outputs = base_ref.shape[0]
    left = left_ref[...]
    for at, size in chunks(outputs):
        rows = slice(at, at + size)
        right = right_ref[:, rows]
        combined = base_ref[rows, :].astype(f32) + dot_tn(right * ADAPTER_SCALE, left)
        norm = column_to_row(jnp.sqrt(jnp.sum(combined * combined, axis=1, keepdims=True)))
        column = magnitude_ref[rows].reshape(1, size) / norm
        weight_ref[rows, :] = (combined * row_to_column(column)).astype(bf16)
        scaled_ref[:, rows] = (ADAPTER_SCALE * column * right.astype(f32)).astype(bf16)
        norm_ref[:, rows] = norm
    weight_ref[outputs:, :] = left


def prepare(base, left, right, magnitude, turned, after=()):
    outputs = right.shape[1]
    shapes = [((base.shape[0] + RANK, base.shape[1]), bf16), ((1, outputs), f32)]
    if turned:
        shapes.append((right.shape, bf16))
    scratch = [] if turned else [pltpu.VMEM((base.shape[0], 512), f32)]
    return call(
        prepare_turned if turned else prepare_natural,
        (base, left, right, magnitude),
        shapes,
        4,
        1.3e-6 * base.size,
        scratch=scratch,
        after=after,
    )


def prepare_first_kernel(*refs):
    sources, outs, held = refs[:12], refs[12:20], refs[20]
    prepare_natural(*sources[:4], *outs[:2], held)
    prepare_turned(*sources[4:8], *outs[2:5])
    prepare_turned(*sources[8:], *outs[5:])


def prepare_first(groups):
    shapes = []
    for which, (base, _, right, _) in enumerate(groups):
        shapes += [((base.shape[0] + RANK, base.shape[1]), bf16), ((1, right.shape[1]), f32)]
        if which:
            shapes.append((right.shape, bf16))
    results = call(
        prepare_first_kernel,
        [a for group in groups for a in group],
        shapes,
        4,
        8,
        scratch=[pltpu.VMEM((groups[0][0].shape[0], 512), f32)],
    )
    return {0: results[:2], 1: results[2:5], 2: results[5:]}


def rms_factor(values):
    return lax.rsqrt(jnp.mean(values * values, axis=0, keepdims=True) + EPSILON)


def turn_heads(values, cosine, sine, heads, scale):
    half = HEAD // 2
    out = []
    for head in range(heads):
        first = values[head * HEAD : head * HEAD + half]
        second = values[head * HEAD + half : (head + 1) * HEAD]
        out.append((first * cosine - second * sine) * scale)
        out.append((second * cosine + first * sine) * scale)
    return jnp.concatenate(out, axis=0)


def turn_heads_back(values, cosine, sine, heads, scale):
    half = HEAD // 2
    out = []
    for head in range(heads):
        first = values[head * HEAD : head * HEAD + half]
        second = values[head * HEAD + half : (head + 1) * HEAD]
        out.append((first * cosine + second * sine) * scale)
        out.append((second * cosine - first * sine) * scale)
    return jnp.concatenate(out, axis=0)


def pair(place, out_ref, own, other):
    size = own.shape[-1]
    core = place[1]
    out_ref[:, pl.ds(pl.multiple_of(core * size, size), size)] = own
    out_ref[:, pl.ds(pl.multiple_of((1 - core) * size, size), size)] = other


def entry_kernel(
    rows,
    place_ref,
    own_ref,
    other_ref,
    pos_own_ref,
    pos_other_ref,
    freq_ref,
    aq_ref,
    wq_ref,
    wk_ref,
    wv_ref,
    x_ref,
    q_ref,
    kv_ref,
    t_ref,
    pos_ref,
    table_ref,
):
    kv_size = KV_HEADS * HEAD
    tokens = x_ref.shape[-1]
    width = x_ref.shape[-2]
    place = read_place(place_ref)
    for at, row in enumerate(rows):
        mine = place[1] * other_ref.shape[0] + row
        pair(place, x_ref.at[at], own_ref[mine], other_ref[row])
        x_low = x_ref[at]
        pair(
            place, pos_ref.at[at], pos_own_ref[pl.ds(mine, 1), :], pos_other_ref[row : row + 1, :]
        )
        position = pos_ref[at]
        phases = freq_ref[...] * position.astype(f32)
        cosine = jnp.cos(phases)
        sine = jnp.sin(phases)
        table_ref[at, 0] = cosine
        table_ref[at, 1] = sine
        x = x_low.astype(f32)
        normed = (x * rms_factor(x)).astype(bf16)
        key = dot_nn(wk_ref[...], normed)
        value = dot_nn(wv_ref[...], normed)
        query = dot_tn(wq_ref[:width, :], normed)
        turned = turn_heads(key, cosine, sine, KV_HEADS, 1.0).astype(bf16)
        value_low = value.astype(bf16)
        for head in range(KV_HEADS):
            kv_ref[at, head] = turned[head * HEAD : (head + 1) * HEAD]
            kv_ref[at, KV_HEADS + head] = value_low[head * HEAD : (head + 1) * HEAD]
        t_ref[at, :RANK] = dot_nn(aq_ref[...], normed).astype(bf16)
        t_ref[at, RANK : 2 * RANK] = key[kv_size:].astype(bf16)
        t_ref[at, 2 * RANK :] = value_low[kv_size:]
        turned = turn_heads(query, cosine, sine, HEADS, HEAD_SCALE).astype(bf16)
        for head in range(HEADS):
            lane = head % GROUP * tokens
            q_ref[at, head // GROUP, :, lane : lane + tokens] = turned[
                head * HEAD : (head + 1) * HEAD
            ]


def entry(rows, place, own, other, pos_own, pos_other, frequency, left, weights, after=()):
    width, size = own.shape[1], own.shape[2]
    tokens = 2 * size
    count = len(rows)
    shapes = [
        ((count, width, tokens), bf16),
        ((count, KV_HEADS, HEAD, GROUP * tokens), bf16),
        ((count, 2 * KV_HEADS, HEAD, tokens), bf16),
        ((count, 3 * RANK, tokens), bf16),
        ((count, 1, tokens), jnp.int32),
        ((count, 2, HEAD // 2, tokens), f32),
    ]
    return call(
        partial(entry_kernel, rows),
        (own, other, pos_own, pos_other, frequency, left, *weights),
        shapes,
        6,
        6 * count,
        scalars=(place,),
        after=after,
    )


def lower_back_kernel(
    place_ref, own_ref, other_ref, wl_ref, cb_ref, dy_ref, dr_ref, dt_ref
):
    rows = other_ref.shape[0]
    outputs = own_ref.shape[1]
    place = read_place(place_ref)
    for row in range(rows):
        pair(place, dy_ref.at[row], own_ref[place[1] * rows + row], other_ref[row])
        dy = dy_ref[row]
        dr_ref[row] = dot_tn(wl_ref[:outputs, :], dy).astype(bf16)
        dt_ref[row] = dot_nn(cb_ref[...], dy).astype(bf16)


def lower_back(place, own, other, weight, scaled, after=()):
    rows, width, size = other.shape
    hidden = weight.shape[1]
    tokens = 2 * size
    shapes = [
        ((rows, width, tokens), bf16),
        ((rows, hidden, tokens), bf16),
        ((rows, RANK, tokens), bf16),
    ]
    return call(
        lower_back_kernel,
        (own, other, weight, scaled),
        shapes,
        8,
        1.9 * rows,
        scalars=(place,),
        after=after,
    )


def write_bias(bias_ref, position, distance):
    size = bias_ref.shape[0]
    key = lax.broadcasted_iota(jnp.int32, (size, size), 0)
    query = lax.broadcasted_iota(jnp.int32, (size, size), 1)
    start = query - position + distance * size
    bias_ref[...] = jnp.where((key >= start) & (key <= query + distance * size), 0.0, MASKED)


def block_distance(chip, step, shards):
    return chip - block_source(chip, step, shards)


def block_source(chip, step, shards):
    if shards & (shards - 1) == 0:
        return jnp.bitwise_xor(chip, step)
    return lax.rem(chip + step, shards)


def needed(chip, first, step, shards, size):
    distance = block_distance(chip, step, shards)
    return (distance > 0) & (distance * size - first < size)


def attend_kernel(at, shards, place_ref, pos_ref, q_ref, *rest):
    kv_refs, rest = rest[:shards], rest[shards:]
    o_ref, lse_ref, bias_ref, max_ref, sum_ref, acc_ref, block_ref = rest
    size = pos_ref.shape[-1]
    chip, _ = read_place(place_ref)
    first = pick(pos_ref[at], 0)

    def visit(kv_ref, opening):
        for head in range(KV_HEADS):
            bias = jnp.concatenate([bias_ref[...]] * GROUP, axis=1)
            logits = dot_tn(kv_ref[head], q_ref[at, head]) + bias
            top = jnp.max(logits, axis=0, keepdims=True)
            if not opening:
                before = max_ref[head]
                top = jnp.maximum(top, before)
            weights = jnp.exp(logits - top)
            total = jnp.sum(weights, axis=0, keepdims=True)
            mixed = dot_nn(kv_ref[head + KV_HEADS], weights.astype(bf16))
            if not opening:
                rescale = jnp.exp(before - top)
                total = total + rescale * sum_ref[head]
                mixed = mixed + rescale * acc_ref[head]
            max_ref[head] = top
            sum_ref[head] = total
            acc_ref[head] = mixed

    write_bias(bias_ref, pos_ref[at], 0)
    visit(kv_refs[0].at[at], True)

    def block_step(step, carry):
        @pl.when(needed(chip, first, step, shards, size))
        def _():
            for which in range(1, shards):

                @pl.when(step == which)
                def _():
                    block_ref[...] = kv_refs[which][at]

            write_bias(bias_ref, pos_ref[at], block_distance(chip, step, shards))
            visit(block_ref, False)

        return carry

    lax.fori_loop(1, shards, block_step, 0)
    total = sum_ref[...]
    o_ref[...] = (acc_ref[...] / total).astype(bf16)
    lse_ref[...] = max_ref[...] + jnp.log(total)


def attend(at, place, position, query, blocks, known, after=()):
    tokens = position.shape[-1]
    stats = (KV_HEADS, 1, GROUP * tokens)
    return call(
        partial(attend_kernel, at, len(blocks)),
        (position, query, *blocks),
        [(query.shape[1:], bf16), (stats, f32)],
        4,
        6 * known,
        scalars=(place,),
        scratch=[
            pltpu.VMEM((tokens, tokens), f32),
            pltpu.VMEM(stats, f32),
            pltpu.VMEM(stats, f32),
            pltpu.VMEM(query.shape[1:], f32),
            pltpu.VMEM(blocks[0].shape[1:], bf16),
        ],
        after=after,
    )


def attend_back_kernel(
    at,
    front,
    shards,
    place_ref,
    pos_ref,
    q_ref,
    do_ref,
    lse_ref,
    delta_ref,
    *rest,
):
    kv_refs, rest = rest[:shards], rest[shards:]
    if front:
        front_refs, rest = rest[: shards - 1], rest[shards - 1 :]
    low_ref, dkv_refs, bias_ref, dq_ref = rest[0], rest[1 : 1 + shards], *rest[1 + shards :]
    if front:
        for come_ref, out_ref in zip(front_refs, dkv_refs[1:]):
            out_ref[:front] = come_ref[...]
    dkv_refs = [dkv_refs[0]] + [ref.at[front] for ref in dkv_refs[1:]]
    size = pos_ref.shape[-1]
    chip, _ = read_place(place_ref)
    first = pick(pos_ref[at], 0)

    def visit(kv_ref, dkv_ref, opening):
        for head in range(KV_HEADS):
            key, value = kv_ref[at, head], kv_ref[at, head + KV_HEADS]
            query, upstream = q_ref[at, head], do_ref[head]
            bias = jnp.concatenate([bias_ref[...]] * GROUP, axis=1)
            probs = jnp.exp(dot_tn(key, query) + bias - lse_ref[head])
            score_grad = (probs * (dot_tn(value, upstream) - delta_ref[head])).astype(bf16)
            query_grad = dot_nn(key, score_grad) * HEAD_SCALE
            if not opening:
                query_grad = query_grad + dq_ref[head]
            dq_ref[head] = query_grad
            dkv_ref[head] = dot_nt(query, score_grad).astype(bf16)
            dkv_ref[head + KV_HEADS] = dot_nt(upstream, probs.astype(bf16)).astype(bf16)

    write_bias(bias_ref, pos_ref[at], 0)
    visit(kv_refs[0], dkv_refs[0], True)
    for step in range(1, shards):
        wanted = needed(chip, first, step, shards, size)

        @pl.when(wanted)
        def _():
            write_bias(bias_ref, pos_ref[at], block_distance(chip, step, shards))
            visit(kv_refs[step], dkv_refs[step], False)

        @pl.when(jnp.logical_not(wanted))
        def _():
            dkv_refs[step][...] = jnp.zeros(dkv_refs[step].shape, bf16)

    low_ref[...] = dq_ref[...].astype(bf16)


def attend_back(
    at, place, position, query, upstream, lse, delta, blocks, front, known, after=()
):
    tokens = position.shape[-1]
    count = front[0].shape[0] if front else 0
    piece = blocks[0].shape[1:]
    return call(
        partial(attend_back_kernel, at, count, len(blocks)),
        (position, query, upstream, lse, delta, *blocks, *front),
        [(query.shape[1:], bf16), (piece, bf16)] + [((count + 1,) + piece, bf16)] * (len(blocks) - 1),
        4,
        9 * known,
        scalars=(place,),
        scratch=[pltpu.VMEM((tokens, tokens), f32), pltpu.VMEM(query.shape[1:], f32)],
        after=after,
    )


def spread_heads(ref):
    tokens = ref.shape[-1] // GROUP
    return jnp.concatenate(
        [
            ref[head // GROUP, :, head % GROUP * tokens : (head % GROUP + 1) * tokens]
            for head in range(HEADS)
        ],
        axis=0,
    )


def middle_kernel(
    row,
    at,
    x_ref,
    dy_ref,
    dr_ref,
    dtl_ref,
    o_ref,
    ao_ref,
    ag_ref,
    au_ref,
    wo,
    wg,
    wu,
    wl,
    halves_ref,
    dx1_ref,
    do_ref,
    delta_ref,
    dao_ref,
    dbo_ref,
    dag_ref,
    dau_ref,
    dbg_ref,
    dbu_ref,
    dal_ref,
    dbl_ref,
    so_ref,
    sg_ref,
    su_ref,
    sl_ref,
    act,
    dgate,
    dupper,
):
    _, width, tokens = x_ref.shape
    hidden = act.shape[0]
    mixed = spread_heads(o_ref)
    attn = dot_tn(wo[:width, :], mixed)
    x1 = x_ref[at].astype(f32) + attn
    rho = rms_factor(x1)
    normed = x1 * rho
    normed_low = normed.astype(bf16)
    t_output = dot_nn(ao_ref[...], mixed).astype(bf16)
    both = jnp.concatenate([ag_ref[...], au_ref[...]], axis=0)
    both = dot_nn(both, normed_low).astype(bf16)
    t_gate, t_upper = both[:RANK], both[RANK:]
    step = 256
    for start in range(0, hidden, step):
        rows = slice(start, start + step)
        gate = dot_tn(wg[:width, rows], normed_low)
        upper = dot_tn(wu[:width, rows], normed_low)
        down = dr_ref[row, rows, :].astype(f32)
        sigmoid = jax.nn.sigmoid(gate)
        silu = gate * sigmoid
        act[rows, :] = (silu * upper).astype(bf16)
        gate_grad = down * upper * (sigmoid + silu * (1.0 - sigmoid))
        upper_grad = down * silu
        dgate[rows, :] = gate_grad.astype(bf16)
        dupper[rows, :] = upper_grad.astype(bf16)
        sg_ref[:, rows] = column_to_row(jnp.sum(gate * gate_grad, axis=1, keepdims=True))
        su_ref[:, rows] = column_to_row(jnp.sum(upper * upper_grad, axis=1, keepdims=True))
    lower_all = dot_nn(wl[...], act[...])
    dal_ref[...] = dot_nt(dtl_ref[row], act[...])
    dbg_ref[...] = dot_nt(t_gate, dgate[...])
    dbu_ref[...] = dot_nt(t_upper, dupper[...])
    lower = lower_all[:width]
    t_lower = lower_all[width:].astype(bf16)
    out = (x1 + lower).astype(bf16)
    halves_ref[0] = out[:, : tokens // 2]
    halves_ref[1] = out[:, tokens // 2 :]
    dy_low = dy_ref[row]
    dy = dy_low.astype(f32)
    sl_ref[...] = column_to_row(jnp.sum(lower * dy, axis=1, keepdims=True))
    gate_back = dot_nn(wg[...], dgate[...])
    upper_back = dot_nn(wu[...], dupper[...])
    dt_gate = gate_back[width:].astype(bf16)
    dt_upper = upper_back[width:].astype(bf16)
    dbl_ref[...] = dot_nt(t_lower, dy_low)
    both = dot_nt(jnp.concatenate([dt_gate, dt_upper], axis=0), normed_low)
    dag_ref[...] = both[:RANK]
    dau_ref[...] = both[RANK:]
    dnormed = gate_back[:width] + upper_back[:width]
    dx1 = dy + rho * (dnormed - normed * jnp.mean(dnormed * normed, axis=0, keepdims=True))
    dx1_low = dx1.astype(bf16)
    dx1_ref[...] = dx1_low
    so_ref[...] = column_to_row(jnp.sum(attn * dx1, axis=1, keepdims=True))
    output_back = dot_nn(wo[...], dx1_low)
    dt_output = output_back[width:].astype(bf16)
    dao_ref[...] = dot_nt(dt_output, mixed)
    dbo_ref[...] = dot_nt(t_output, dx1_low)
    dmixed = output_back[:width].astype(bf16)
    weighted = dmixed.astype(f32) * mixed.astype(f32)
    for head in range(HEADS):
        rows = slice(head * HEAD, (head + 1) * HEAD)
        lanes = slice(head % GROUP * tokens, (head % GROUP + 1) * tokens)
        do_ref[head // GROUP, :, lanes] = dmixed[rows]
        delta_ref[head // GROUP, :, lanes] = jnp.sum(weighted[rows], axis=0, keepdims=True)


def middle(row, at, x, dy, dr, dt_lower, mixed, lefts, weights, known, after=()):
    _, width, tokens = x.shape
    hidden = dr.shape[1]
    shapes = [
        ((2, width, tokens // 2), bf16),
        ((width, tokens), bf16),
        (mixed.shape, bf16),
        ((KV_HEADS, 1, GROUP * tokens), f32),
        ((RANK, width), f32),
        ((RANK, width), f32),
        ((RANK, width), f32),
        ((RANK, width), f32),
        ((RANK, hidden), f32),
        ((RANK, hidden), f32),
        ((RANK, hidden), f32),
        ((RANK, width), f32),
        ((1, width), f32),
        ((1, hidden), f32),
        ((1, hidden), f32),
        ((1, width), f32),
    ]
    return call(
        partial(middle_kernel, row, at),
        (x, dy, dr, dt_lower, mixed, *lefts, *weights),
        shapes,
        14,
        13 * known,
        scratch=[pltpu.VMEM((hidden, tokens), bf16)] * 3,
        after=after,
    )


def exit_kernel(at, piece, shards, *refs):
    (x_ref, table_ref, dx1_ref, t_ref, q_ref, kv_ref, dq_ref, wq_ref, wk_ref, wv_ref) = refs[:10]
    cbk_ref, cbv_ref = refs[10:12]
    dkv_refs = refs[12 : 12 + shards]
    halves_ref, da_ref, dbq_ref, dbkv_ref, sq_ref, skv_ref = refs[12 + shards :]
    _, width, tokens = x_ref.shape
    kv_size = KV_HEADS * HEAD
    x = x_ref[at].astype(f32)
    rho = rms_factor(x)
    normed = x * rho
    normed_low = normed.astype(bf16)
    cosine = table_ref[at, 0]
    sine = table_ref[at, 1]
    dquery = turn_heads_back(spread_heads(dq_ref).astype(f32), cosine, sine, HEADS, 1.0)
    query = turn_heads_back(
        spread_heads(q_ref.at[at]).astype(f32), cosine, sine, HEADS, 1.0 / HEAD_SCALE
    )
    sq_ref[...] = column_to_row(jnp.sum(query * dquery, axis=1, keepdims=True))
    dquery = dquery.astype(bf16)
    query_back = dot_nn(wq_ref[...], dquery)
    dkv = dkv_refs[0][...].astype(f32)
    for ref in dkv_refs[1:]:
        dkv = dkv + ref[piece].astype(f32)
    dkv = dkv.reshape(2 * kv_size, tokens)
    key_value = kv_ref[at].astype(f32).reshape(2 * kv_size, tokens)
    dkey = turn_heads_back(dkv[:kv_size], cosine, sine, KV_HEADS, 1.0)
    dvalue = dkv[kv_size:]
    key = turn_heads_back(key_value[:kv_size], cosine, sine, KV_HEADS, 1.0)
    value = key_value[kv_size:]
    skv_ref[0:1, :] = column_to_row(jnp.sum(key * dkey, axis=1, keepdims=True))
    skv_ref[1:2, :] = column_to_row(jnp.sum(value * dvalue, axis=1, keepdims=True))
    dkey = dkey.astype(bf16)
    dvalue = dvalue.astype(bf16)
    dnormed = (
        query_back[:width]
        + dot_tn(wk_ref[:kv_size, :], dkey)
        + dot_tn(wv_ref[:kv_size, :], dvalue)
    )
    dx = dx1_ref[...].astype(f32) + rho * (dnormed - normed * jnp.mean(dnormed * normed, axis=0, keepdims=True))
    dx = dx.astype(bf16)
    halves_ref[0] = dx[:, : tokens // 2]
    halves_ref[1] = dx[:, tokens // 2 :]
    dt = jnp.concatenate(
        [query_back[width:], dot_nn(cbk_ref[...], dkey), dot_nn(cbv_ref[...], dvalue)], axis=0
    ).astype(bf16)
    da_ref[...] = dot_nt(dt, normed_low)
    dbq_ref[...] = dot_nt(t_ref[at, :RANK], dquery)
    dbkv_ref[0] = dot_nt(t_ref[at, RANK : 2 * RANK], dkey)
    dbkv_ref[1] = dot_nt(t_ref[at, 2 * RANK :], dvalue)


def leave(at, piece, x, table, dx1, inner, query, key_value, dquery, weights, scaled, dkvs, after=()):
    _, width, tokens = x.shape
    q_size, kv_size = HEADS * HEAD, KV_HEADS * HEAD
    shapes = [
        ((2, width, tokens // 2), bf16),
        ((3 * RANK, width), f32),
        ((RANK, q_size), f32),
        ((2, RANK, kv_size), f32),
        ((1, q_size), f32),
        ((2, kv_size), f32),
    ]
    return call(
        partial(exit_kernel, at, piece, len(dkvs)),
        (x, table, dx1, inner, query, key_value, dquery, *weights, *scaled, *dkvs),
        shapes,
        7,
        3,
        after=after,
    )


def settle(sums, weight, turned, left, right, norm, magnitude):
    left_sum, right_sum, stat = sums
    magnitude = magnitude.reshape(1, -1)
    factor = -stat / (magnitude * norm)
    scaled = (ADAPTER_SCALE * factor * right.astype(f32)).astype(bf16)
    if turned:
        left_more = dot_nn(scaled, weight)
        product = dot_nt(left, weight)
    else:
        left_more = dot_nt(scaled, weight)
        product = dot_nn(left, weight)
    right_total = ADAPTER_SCALE * (right_sum * (magnitude / norm) + factor * product)
    return (left_sum + left_more, right_total, stat / magnitude)


STAT = 512


def put_stat(ref, half, row, lane, values):
    size = values.shape[1]
    for start in range(0, size, STAT):
        take = min(STAT, size - start)
        ref[half, row : row + 1, lane : lane + take] = values[:, start : start + take]
        row += 1
    return row


def stack_sum(refs):
    total = refs[0][...]
    for ref in refs[1:]:
        total = total + ref[...]
    return total


def settle_middle_kernel(rows, shards, *refs):
    sums = [
        stack_sum([refs[row * 12 + which] for row in range(rows)]) for which in range(12)
    ]
    refs = refs[rows * 12 :]
    names = ("output", "gate", "upper", "lower")
    groups = {}
    for which, name in enumerate(names):
        groups[name] = [ref for ref in refs[which * 5 : which * 5 + 5]]
    out, pack = refs[20:]
    dao, dbo, dag, dau, dbg, dbu, dal, dbl, so, sg, su, sl = sums
    pieces = {
        "output": (dao, dbo, so),
        "gate": (dag, dbg, sg),
        "upper": (dau, dbu, su),
        "lower": (dal, dbl, sl),
    }
    done = {}
    for name in names:
        weight, left, right, norm, magnitude = groups[name]
        done[name] = settle(
            pieces[name],
            weight[: weight.shape[0] - RANK, :],
            name == "lower",
            left[...],
            right[...],
            norm[...],
            magnitude[...],
        )
    width = dao.shape[1]
    slot, hidden = slots(width), dbg.shape[1]
    pack[...] = jnp.zeros(pack.shape, f32)
    pack[0, :, 0:hidden] = done["gate"][1]
    pack[0, :, hidden : 2 * hidden] = done["upper"][1]
    pack[0, :, 2 * hidden : 2 * hidden + width] = done["output"][0]
    row = 0
    for name in ("gate", "upper", "output", "lower"):
        row = put_stat(pack, 0, row, 2 * hidden + slot, done[name][2])
    pack[1, :, 0:hidden] = done["lower"][0]
    place = hidden
    for values in (done["output"][1], done["gate"][0], done["upper"][0], done["lower"][1]):
        pack[1, :, place : place + width] = values
        place += slot
    cut(out, pack, shards)


def slots(width):
    return -(-width // 128) * 128


def piece_of(half, shards):
    return slots(-(-half // shards))


def cut(out, pack, shards):
    piece = out.shape[-1]
    for half in range(2):
        for shard in range(shards):
            out[half, shard] = pack[half, :, shard * piece : (shard + 1) * piece]


def settle_middle(partials, projections, shards, after=()):
    hidden = partials[0][4].shape[1]
    width = partials[0][0].shape[1]
    piece = piece_of(2 * hidden + slots(width) + STAT, shards)
    flat = [a for part in partials for a in part] + [a for group in projections for a in group]
    return call(
        partial(settle_middle_kernel, len(partials), shards),
        flat,
        [((2, shards, RANK, piece), f32)],
        5,
        6,
        scratch=[pltpu.VMEM((2, RANK, shards * piece), f32)],
        after=after,
    )[0]


def settle_entry_kernel(rows, shards, place_ref, middle_ref, *refs):
    sums = [stack_sum([refs[row * 5 + which] for row in range(rows)]) for which in range(5)]
    refs = refs[rows * 5 :]
    da, dbq, dbkv, sq, skv = sums
    keep_ref, send_ref, pack = refs[15:]
    pieces = (
        (da[:RANK], dbq, sq),
        (da[RANK : 2 * RANK], dbkv[0], skv[0:1]),
        (da[2 * RANK :], dbkv[1], skv[1:2]),
    )
    done = []
    for which in range(3):
        weight, left, right, norm, magnitude = refs[which * 5 : which * 5 + 5]
        done.append(
            settle(
                pieces[which],
                weight[: weight.shape[0] - RANK, :],
                which > 0,
                left[...],
                right[...],
                norm[...],
                magnitude[...],
            )
        )
    width = da.shape[1]
    slot = slots(width)
    kv_size = skv.shape[1]
    pack[...] = jnp.zeros(pack.shape, f32)
    pack[0, :, 0:width] = done[0][0]
    pack[0, :, slot : slot + width] = done[1][0]
    row = 0
    for which in range(3):
        row = put_stat(pack, 0, row, 2 * slot, done[which][2])
    pack[1, :, 0:width] = done[2][0]
    pack[1, :, slot : slot + sq.shape[1]] = done[0][1]
    pack[1, :, 2 * slot : 2 * slot + 2 * kv_size] = jnp.concatenate(
        [done[1][1], done[2][1]], axis=1
    )
    here = read_place(place_ref)[1] == 0
    middle_piece = middle_ref.shape[-1]
    piece = pack.shape[-1] // shards
    for shard in range(shards):
        place = slice(shard * piece, (shard + 1) * piece)
        parts = (
            (slice(0, middle_piece), middle_ref[0, shard], middle_ref[1, shard]),
            (slice(middle_piece, middle_piece + piece), pack[0, :, place], pack[1, :, place]),
        )
        for lanes, first, second in parts:
            keep_ref[shard, :, lanes] = jnp.where(here, first, second)
            send_ref[shard, :, lanes] = jnp.where(here, second, first).astype(bf16)


def settle_entry(place, middle_pack, partials, projections):
    shards = middle_pack.shape[1]
    width = partials[0][0].shape[1]
    kv_size = partials[0][4].shape[1]
    piece = piece_of(2 * slots(width) + max(STAT, slots(2 * kv_size)), shards)
    flat = [a for part in partials for a in part] + [a for group in projections for a in group]
    shape = (shards, RANK, middle_pack.shape[-1] + piece)
    return call(
        partial(settle_entry_kernel, len(partials), shards),
        [middle_pack] + flat,
        [(shape, f32), (shape, bf16)],
        5,
        2,
        scalars=(place,),
        scratch=[pltpu.VMEM((2, RANK, shards * piece), f32)],
    )


def get_stat(value, row, lane, size):
    parts = []
    for start in range(0, size, STAT):
        take = min(STAT, size - start)
        parts.append(value[row : row + 1, lane : lane + take])
        row += 1
    return jnp.concatenate(parts, axis=1) if len(parts) > 1 else parts[0], row


def finish_kernel(width, hidden, kv_size, shards, middle_piece, place_ref, *refs):
    mine_ref, other_ref = refs[:2]
    lefts, rights, stats = refs[2:9], refs[9:16], refs[16:23]
    middle_held, entry_held = refs[23:]
    chip, core = read_place(place_ref)
    piece = mine_ref.shape[-1] - middle_piece
    for half in range(2):
        for step in range(shards):
            value = jnp.where(core == half, mine_ref[step], other_ref[step]).astype(f32)
            source = block_source(chip, step, shards)
            lane = pl.multiple_of(source * middle_piece, 128)
            middle_held[half, :, pl.ds(lane, middle_piece)] = value[:, :middle_piece]
            lane = pl.multiple_of(source * piece, 128)
            entry_held[half, :, pl.ds(lane, piece)] = value[:, middle_piece:]
    slot = slots(width)
    m0, m1, e0, e1 = middle_held.at[0], middle_held.at[1], entry_held.at[0], entry_held.at[1]
    rights[4][...] = m0[:, :hidden]
    rights[5][...] = m0[:, hidden : 2 * hidden]
    lefts[3][...] = m0[:, 2 * hidden : 2 * hidden + width]
    row = 0
    for which, size in ((4, hidden), (5, hidden), (3, width), (6, width)):
        value, row = get_stat(m0, row, 2 * hidden + slot, size)
        stats[which][...] = value[0]
    lefts[6][...] = m1[:, :hidden]
    for place, ref in enumerate((rights[3], lefts[4], lefts[5], rights[6])):
        ref[...] = m1[:, hidden + place * slot : hidden + place * slot + width]
    lefts[0][...] = e0[:, :width]
    lefts[1][...] = e0[:, slot : slot + width]
    row = 0
    for which, size in ((0, width), (1, kv_size), (2, kv_size)):
        value, row = get_stat(e0, row, 2 * slot, size)
        stats[which][...] = value[0]
    lefts[2][...] = e1[:, :width]
    rights[0][...] = e1[:, slot : slot + width]
    both = e1[:, 2 * slot : 2 * slot + 2 * kv_size]
    rights[1][...] = both[:, :kv_size]
    rights[2][...] = both[:, kv_size:]


def finish(place, middle_piece, sums, lefts, rights, magnitudes):
    shards = sums[0].shape[0]
    shapes = [a.shape for a in lefts] + [a.shape for a in rights] + [a.shape for a in magnitudes]
    sizes = (lefts[0].shape[1], rights[4].shape[1], rights[1].shape[1])
    return call(
        partial(finish_kernel, *sizes, shards, middle_piece),
        sums,
        [(shape, f32) for shape in shapes],
        5,
        2,
        scalars=(place,),
        scratch=[
            pltpu.VMEM((2, RANK, shards * piece), f32)
            for piece in (middle_piece, sums[0].shape[-1] - middle_piece)
        ],
    )


def to_other_core(value):
    size = lax.axis_size("seq")
    return lax.ppermute(value, "seq", [(i, i ^ 1) for i in range(size)])


def peer(index, step, count):
    return index ^ step if count & (count - 1) == 0 else (index + step) % count


def to_chip(value, step, needed=False):
    size = lax.axis_size("seq")
    count = size // 2
    pairs = [(peer(c, step, count), c) for c in range(count)]
    pairs = [(a, c) for a, c in pairs if a < c or not needed]
    return lax.ppermute(value, "seq", [(2 * a + k, 2 * c + k) for a, c in pairs for k in (0, 1)])


def back_to_chip(value, step, needed=False):
    size = lax.axis_size("seq")
    count = size // 2
    pairs = [(c, peer(c, step, count)) for c in range(count)]
    pairs = [(c, a) for c, a in pairs if a < c or not needed]
    return lax.ppermute(value, "seq", [(2 * c + k, 2 * a + k) for c, a in pairs for k in (0, 1)])


def to_batch(value, step):
    count = lax.axis_size("batch")
    return lax.ppermute(value, "batch", [(b, peer(b, step, count)) for b in range(count)])


def share_kernel(place_ref, keep_ref, come_ref, own_ref, *out_refs):
    chip, _ = read_place(place_ref)
    shards = come_ref.shape[0]
    own_ref[...] = keep_ref[chip] + come_ref[chip].astype(f32)
    for step, ref in enumerate(out_refs, start=1):
        other = block_source(chip, step, shards)
        ref[...] = (keep_ref[other] + come_ref[other].astype(f32)).astype(bf16)


def sum_kernel(own_ref, *refs):
    *come_refs, total_ref, low_ref = refs
    total = own_ref[...]
    for ref in come_refs:
        total = total + ref[...].astype(f32)
    total_ref[...] = total
    low_ref[...] = total.astype(bf16)


def cross_core(place, keep, send):
    shards = keep.shape[0]
    piece = keep.shape[1:]
    own, *parts = call(
        share_kernel,
        (keep, to_other_core(send)),
        [(piece, f32)] + [(piece, bf16)] * (shards - 1),
        4,
        1,
        scalars=(place,),
    )
    return own, parts


def add_up(own, come, after=()):
    return call(
        sum_kernel, (own, *come), [(own.shape, f32), (own.shape, bf16)], 4, 1, after=after
    )


def cross_chips(own, parts, after=()):
    come = [back_to_chip(part, step) for step, part in enumerate(parts, start=1)]
    return add_up(own, come, after)


def cross_batch(sums, after=()):
    own, low = sums
    count = lax.axis_size("batch")
    return add_up(own, [to_batch(low, step) for step in range(1, count)], after)


def spread(sums, shards):
    low = sums[1]
    mine = jnp.stack([low] + [to_chip(low, step) for step in range(1, shards)])
    return mine, to_other_core(mine)


def leave_half_kernel(skipped, *refs):
    place_ref, value_ref, out_ref, sem = refs[skipped:]
    _, core = read_place(place_ref)
    half = out_ref.shape[0]
    copy = pltpu.make_async_copy(value_ref.at[pl.ds((1 - core) * half, half)], out_ref, sem)
    copy.start()
    copy.wait()


def leave_half(place, value, microseconds, after=()):
    half = value.shape[0] // 2
    anywhere = pl.BlockSpec(memory_space=pl.ANY)
    return pl.pallas_call(
        partial(leave_half_kernel, len(after)),
        in_specs=[anywhere] * len(after) + [vmem(), anywhere],
        out_specs=vmem(),
        out_shape=jax.ShapeDtypeStruct((half,) + value.shape[1:], value.dtype),
        scratch_shapes=[pltpu.SemaphoreType.DMA],
        compiler_params=pltpu.CompilerParams(vmem_limit_bytes=2**20),
        cost_estimate=pl.CostEstimate(
            flops=int(microseconds * 1.1e9), bytes_accessed=1, transcendentals=0
        ),
    )(*after, place, value)


def other_half(value, core):
    half = value.shape[0] // 2
    return to_other_core(lax.dynamic_slice_in_dim(value, (1 - core) * half, half, 0))


def other_halves_kernel(rows, skipped, *refs):
    place_ref, *half_refs = refs[skipped : skipped + 1 + rows]
    out_ref, sems = refs[-2:]
    _, core = read_place(place_ref)
    copies = [
        pltpu.make_async_copy(ref.at[1 - core], out_ref.at[row], sems.at[row])
        for row, ref in enumerate(half_refs)
    ]
    for copy in copies:
        copy.start()
    for copy in copies:
        copy.wait()


def other_halves(place, halves, after):
    rows = len(halves)
    anywhere = pl.BlockSpec(memory_space=pl.ANY)
    return pl.pallas_call(
        partial(other_halves_kernel, rows, len(after)),
        in_specs=[anywhere] * len(after) + [vmem()] + [anywhere] * rows,
        out_specs=anywhere,
        out_shape=jax.ShapeDtypeStruct((rows,) + halves[0].shape[1:], halves[0].dtype),
        scratch_shapes=[pltpu.SemaphoreType.DMA((rows,))],
        compiler_params=pltpu.CompilerParams(vmem_limit_bytes=2**20),
        cost_estimate=pl.CostEstimate(flops=10**9, bytes_accessed=1, transcendentals=0),
    )(*after, place, *halves)


def assemble_kernel(rows, offset, skipped, *refs):
    place_ref = refs[skipped]
    keep_refs = refs[skipped + 1 : skipped + 1 + rows]
    other_refs = refs[skipped + 1 + rows : -3]
    other_refs = [other_refs[0].at[offset + row] for row in range(rows)]
    out_ref, flag_ref, sems = refs[-3:]
    _, core = read_place(place_ref)
    copies = []
    for row in range(rows):
        for side, (source, place) in enumerate(
            (
                (keep_refs[row].at[core], core * rows + row),
                (other_refs[row], (1 - core) * rows + row),
            )
        ):
            copies.append(pltpu.make_async_copy(source, out_ref.at[place], sems.at[side, row]))
    for copy in copies:
        copy.start()
    flag_ref[...] = jnp.zeros(flag_ref.shape, f32)
    for copy in copies:
        copy.wait()


def assemble(place, keeps, others, offset, after=()):
    rows = len(keeps)
    anywhere = pl.BlockSpec(memory_space=pl.ANY)
    return pl.pallas_call(
        partial(assemble_kernel, rows, offset, len(after)),
        in_specs=[anywhere] * len(after) + [vmem()] + [anywhere] * (rows + 1),
        out_specs=[anywhere, vmem()],
        out_shape=[
            jax.ShapeDtypeStruct((2 * rows,) + keeps[0].shape[1:], keeps[0].dtype),
            jax.ShapeDtypeStruct((8, 128), f32),
        ],
        scratch_shapes=[pltpu.SemaphoreType.DMA((2, rows))],
        compiler_params=pltpu.CompilerParams(vmem_limit_bytes=2**20),
        cost_estimate=pl.CostEstimate(flops=10**9, bytes_accessed=1, transcendentals=0),
    )(*after, place, *keeps, others)


def body(tokens, segment_ids, position_ids, cotangent, *weights):
    bases, lefts, rights, magnitudes = (
        weights[:7],
        [a.T for a in weights[7:14]],
        weights[14:21],
        weights[21:28],
    )
    turned = (False, True, True, False, False, False, True)
    bases = [w.T if turn else w for w, turn in zip(bases, turned)]
    index = lax.axis_index("seq")
    core, chip = index % 2, index // 2
    shards = lax.axis_size("seq") // 2
    lanes = lax.broadcasted_iota(jnp.int32, (1, 128), 1)
    place = jnp.where(lanes == 0, chip, jnp.where(lanes == 1, core, 0)).astype(jnp.int32)
    x = jnp.swapaxes(tokens, 1, 2)
    dy = jnp.swapaxes(cotangent, 1, 2)
    pos_other = other_half(position_ids, core)
    x_other = to_other_core(leave_half(place, x, 12))
    rows = x_other.shape[0]
    half_head = HEAD // 2
    frequency = ROTARY_BASE ** (-(jnp.arange(half_head, dtype=f32) * 2.0 / HEAD))[:, None]

    def ready_for(which, after=()):
        return prepare(
            bases[which], lefts[which], rights[which], magnitudes[which], turned[which], after
        )

    ready = prepare_first(
        [(bases[which], lefts[which], rights[which], magnitudes[which]) for which in range(3)]
    )
    first_weights = [ready[which][0] for which in range(3)]
    groups = [(0,), tuple(range(1, rows))]
    entries, gathered, where = [], [], {}
    last = ()
    for number, group in enumerate(groups):
        results = entry(
            group,
            place,
            x,
            x_other,
            position_ids,
            pos_other,
            frequency,
            lefts[0],
            first_weights,
            last,
        )
        entries.append(results)
        own = results[2]
        gathered.append([own] + [to_chip(own, step) for step in range(1, shards)])
        where.update({row: (number, at) for at, row in enumerate(group)})
        if number == 0:
            started = (results[3],)
            for which in (6, 3, 4, 5):
                ready[which] = ready_for(which, started)
            last = [ready[which][1] for which in (6, 3, 4, 5)]
    dy_other = to_other_core(leave_half(place, dy, 1, (ready[0][1],)))
    dy, dr, dt_lower = lower_back(
        place, dy, dy_other, ready[6][0], ready[6][2], (entries[-1][3],)
    )
    last = (mark((dt_lower, *gathered[0])),)
    keeps, middles, backs, waiting, sent = [], [], [], (), ()
    for row in range(rows):
        number, at = where[row]
        x_rows, query, _, _, position, _ = entries[number]
        known = 1.0
        mixed, lse = attend(at, place, position, query, gathered[number], known, last)
        halves, dx1, upstream, delta, *sums = middle(
            row,
            at,
            x_rows,
            dy,
            dr,
            dt_lower,
            mixed,
            lefts[3:6],
            [ready[which][0] for which in (3, 4, 5, 6)],
            known,
        )
        keeps.append(halves)
        middles.append(sums)
        together = row == rows - 2
        dquery, own, *dkvs = attend_back(
            at,
            place,
            position,
            query,
            upstream,
            lse,
            delta,
            gathered[number],
            waiting if row < rows - 1 else (),
            known,
            sent[:-1] if row == rows - 1 else (),
        )
        last = (dquery,)
        if row < rows - 2:
            waiting = dkvs
            backs.append([dx1, dquery, own])
            continue
        if row == rows - 1:
            last = (dquery, *sent[-1:])
        if together:
            sent = [back_to_chip(part, step, True) for step, part in enumerate(dkvs[:-1], start=1)]
            part = hold(dkvs[-1], sent) if sent else dkvs[-1]
            dkvs = sent + [back_to_chip(part, shards - 1, True)]
            sent = dkvs
        else:
            dkvs = [back_to_chip(part, step, True) for step, part in enumerate(dkvs, start=1)]
        backs.append([dx1, dquery, own])
        first_row = 0 if together else row
        for back_row in range(first_row, row + 1):
            backs[back_row] += [back_row - first_row, dkvs]

    def group_of(which):
        return (ready[which][0], lefts[which], rights[which], ready[which][1], magnitudes[which])

    exits = []

    def go_out(row, after):
        number, at = where[row]
        x_rows, query, key_value, inner, _, table = entries[number]
        dx1, dquery, own, piece, dkvs = backs[row]
        exits.append(
            leave(
                at,
                piece,
                x_rows,
                table,
                dx1,
                inner,
                query,
                key_value,
                dquery,
                first_weights,
                (ready[1][2], ready[2][2]),
                [own] + dkvs,
                after,
            )
        )

    for row in range(rows - 1):
        go_out(row, last)
    middle_pack = settle_middle(
        middles, [group_of(which) for which in (3, 4, 5, 6)], shards, last
    )
    go_out(rows - 1, (middle_pack, *[e[1] for e in exits]))
    keep, send = settle_entry(
        place, middle_pack, [e[1:] for e in exits], [group_of(which) for which in (0, 1, 2)]
    )
    own, parts = cross_core(place, keep, send)
    sums = cross_chips(own, parts)
    ends = [e[0] for e in exits]
    others = to_other_core(other_halves(place, keeps + ends, (sums[1],)))
    layer_out, flag = assemble(place, keeps, others, 0)
    tokens_grad, more = assemble(place, ends, others, rows)
    sums = cross_batch(sums, (flag, more))
    finals = finish(
        place, middle_pack.shape[-1], spread(sums, shards), lefts, rights, magnitudes
    )
    return (
        jnp.swapaxes(layer_out, 1, 2),
        jnp.swapaxes(tokens_grad, 1, 2),
        *[a.T for a in finals[:7]],
        *finals[7:],
    )


def solution(mesh):
    split = P("batch", "seq", None)
    return jax.shard_map(
        body,
        mesh=mesh,
        in_specs=(split, P("batch", "seq"), P("batch", "seq"), split) + (P(),) * 28,
        out_specs=(split, split) + (P(),) * 21,
        check_vma=False,
    )
```

```python
from functools import partial

import jax
import jax.numpy as jnp
from jax import lax
from jax.experimental import pallas as pl
from jax.experimental.pallas import tpu as pltpu
from jax.sharding import PartitionSpec as P

HEADS = 15
KV_HEADS = 5
HEAD = 64
GROUP = 3
RANK = 16
EPSILON = 1e-05
ROTARY_BASE = 100000.0
MASKED = -1e30
ADAPTER_SCALE = 2.0
HEAD_SCALE = HEAD**-0.5

bf16 = jnp.bfloat16
f32 = jnp.float32


def dot_nn(a, b):
    return lax.dot_general(a, b, (((1,), (0,)), ((), ())), preferred_element_type=f32)


def dot_tn(a, b):
    return lax.dot_general(a, b, (((0,), (0,)), ((), ())), preferred_element_type=f32)


def dot_nt(a, b):
    return lax.dot_general(a, b, (((1,), (1,)), ((), ())), preferred_element_type=f32)


def vmem():
    return pl.BlockSpec(memory_space=pltpu.VMEM)


def pick(row, lane):
    row = row[:, :128]
    return jnp.sum(jnp.where(lax.broadcasted_iota(jnp.int32, row.shape, 1) == lane, row, 0))


def read_place(place_ref):
    return pick(place_ref[...], 0), pick(place_ref[...], 1)


def call(kernel, arrays, shapes, mebibytes, microseconds, scalars=(), scratch=(), after=()):
    skipped = len(after)
    return pl.pallas_call(
        (lambda *refs: kernel(*refs[skipped:])) if skipped else kernel,
        in_specs=[pl.BlockSpec(memory_space=pl.ANY)] * skipped
        + [vmem()] * (len(scalars) + len(arrays)),
        out_specs=[vmem()] * len(shapes),
        out_shape=[jax.ShapeDtypeStruct(shape, dtype) for shape, dtype in shapes],
        scratch_shapes=list(scratch),
        compiler_params=pltpu.CompilerParams(vmem_limit_bytes=mebibytes * 2**20),
        cost_estimate=pl.CostEstimate(
            flops=int(microseconds * 1.1e9), bytes_accessed=1, transcendentals=0
        ),
    )(*after, *scalars, *arrays)


def mark_kernel(out_ref):
    out_ref[...] = jnp.zeros(out_ref.shape, f32)


def mark(after):
    return call(mark_kernel, (), [((8, 128), f32)], 1, 1, after=after)[0]


def hold_kernel(value_ref, out_ref):
    out_ref[...] = value_ref[...]


def hold(value, after):
    return call(hold_kernel, (value,), [(value.shape, value.dtype)], 1, 0.5, after=after)[0]


def eye(size):
    return lax.broadcasted_iota(jnp.int32, (size, size), 0) == lax.broadcasted_iota(
        jnp.int32, (size, size), 1
    )


def chunks(total, step=128):
    return [(start, min(step, total - start)) for start in range(0, total, step)]


def column_to_row(column):
    parts = []
    for start, size in chunks(column.shape[0]):
        parts.append(
            jnp.sum(jnp.where(eye(size), column[start : start + size], 0.0), axis=0, keepdims=True)
        )
    return parts[0] if len(parts) == 1 else jnp.concatenate(parts, axis=1)


def row_to_column(row):
    parts = []
    for start, size in chunks(row.shape[1]):
        parts.append(
            jnp.sum(jnp.where(eye(size), row[:, start : start + size], 0.0), axis=1, keepdims=True)
        )
    return parts[0] if len(parts) == 1 else jnp.concatenate(parts, axis=0)


def prepare_natural(base_ref, left_ref, right_ref, magnitude_ref, weight_ref, norm_ref, held):
    inputs, outputs = base_ref.shape
    step = 96
    for at, lanes in chunks(outputs, 512):
        place = slice(at, at + lanes)
        right = right_ref[:, place]
        squares = jnp.zeros((8, lanes), f32)
        for start in range(0, inputs, step):
            rows = slice(start, start + step)
            combined = base_ref[rows, place].astype(f32) + dot_tn(
                left_ref[:, rows] * ADAPTER_SCALE, right
            )
            held[rows, :lanes] = combined
            squares = squares + jnp.sum(
                (combined * combined).reshape(step // 8, 8, lanes), axis=0
            )
        norm = jnp.sqrt(jnp.sum(squares, axis=0, keepdims=True))
        column = magnitude_ref[place].reshape(1, lanes) / norm
        for start in range(0, inputs, step):
            rows = slice(start, start + step)
            weight_ref[rows, place] = (held[rows, :lanes] * column).astype(bf16)
        weight_ref[inputs:, place] = (ADAPTER_SCALE * column * right.astype(f32)).astype(bf16)
        norm_ref[:, place] = norm


def prepare_turned(
    base_ref, left_ref, right_ref, magnitude_ref, weight_ref, norm_ref, scaled_ref
):
    outputs = base_ref.shape[0]
    left = left_ref[...]
    for at, size in chunks(outputs):
        rows = slice(at, at + size)
        right = right_ref[:, rows]
        combined = base_ref[rows, :].astype(f32) + dot_tn(right * ADAPTER_SCALE, left)
        norm = column_to_row(jnp.sqrt(jnp.sum(combined * combined, axis=1, keepdims=True)))
        column = magnitude_ref[rows].reshape(1, size) / norm
        weight_ref[rows, :] = (combined * row_to_column(column)).astype(bf16)
        scaled_ref[:, rows] = (ADAPTER_SCALE * column * right.astype(f32)).astype(bf16)
        norm_ref[:, rows] = norm
    weight_ref[outputs:, :] = left


def prepare(base, left, right, magnitude, turned, after=()):
    outputs = right.shape[1]
    shapes = [((base.shape[0] + RANK, base.shape[1]), bf16), ((1, outputs), f32)]
    if turned:
        shapes.append((right.shape, bf16))
    scratch = [] if turned else [pltpu.VMEM((base.shape[0], 512), f32)]
    return call(
        prepare_turned if turned else prepare_natural,
        (base, left, right, magnitude),
        shapes,
        4,
        1.3e-6 * base.size,
        scratch=scratch,
        after=after,
    )


def prepare_first_kernel(*refs):
    sources, outs, held = refs[:12], refs[12:20], refs[20]
    prepare_natural(*sources[:4], *outs[:2], held)
    prepare_turned(*sources[4:8], *outs[2:5])
    prepare_turned(*sources[8:], *outs[5:])


def prepare_first(groups):
    shapes = []
    for which, (base, _, right, _) in enumerate(groups):
        shapes += [((base.shape[0] + RANK, base.shape[1]), bf16), ((1, right.shape[1]), f32)]
        if which:
            shapes.append((right.shape, bf16))
    results = call(
        prepare_first_kernel,
        [a for group in groups for a in group],
        shapes,
        4,
        8,
        scratch=[pltpu.VMEM((groups[0][0].shape[0], 512), f32)],
    )
    return {0: results[:2], 1: results[2:5], 2: results[5:]}


def rms_factor(values):
    return lax.rsqrt(jnp.mean(values * values, axis=0, keepdims=True) + EPSILON)


def turn_heads(values, cosine, sine, heads, scale):
    half = HEAD // 2
    out = []
    for head in range(heads):
        first = values[head * HEAD : head * HEAD + half]
        second = values[head * HEAD + half : (head + 1) * HEAD]
        out.append((first * cosine - second * sine) * scale)
        out.append((second * cosine + first * sine) * scale)
    return jnp.concatenate(out, axis=0)


def turn_heads_back(values, cosine, sine, heads, scale):
    half = HEAD // 2
    out = []
    for head in range(heads):
        first = values[head * HEAD : head * HEAD + half]
        second = values[head * HEAD + half : (head + 1) * HEAD]
        out.append((first * cosine + second * sine) * scale)
        out.append((second * cosine - first * sine) * scale)
    return jnp.concatenate(out, axis=0)


def pair(place, out_ref, own, other):
    size = own.shape[-1]
    core = place[1]
    out_ref[:, pl.ds(pl.multiple_of(core * size, size), size)] = own
    out_ref[:, pl.ds(pl.multiple_of((1 - core) * size, size), size)] = other


def entry_kernel(
    rows,
    place_ref,
    own_ref,
    other_ref,
    pos_own_ref,
    pos_other_ref,
    freq_ref,
    aq_ref,
    wq_ref,
    wk_ref,
    wv_ref,
    x_ref,
    q_ref,
    kv_ref,
    t_ref,
    pos_ref,
    table_ref,
):
    kv_size = KV_HEADS * HEAD
    tokens = x_ref.shape[-1]
    width = x_ref.shape[-2]
    place = read_place(place_ref)
    for at, row in enumerate(rows):
        mine = place[1] * other_ref.shape[0] + row
        pair(place, x_ref.at[at], own_ref[mine], other_ref[row])
        x_low = x_ref[at]
        pair(
            place, pos_ref.at[at], pos_own_ref[pl.ds(mine, 1), :], pos_other_ref[row : row + 1, :]
        )
        position = pos_ref[at]
        phases = freq_ref[...] * position.astype(f32)
        cosine = jnp.cos(phases)
        sine = jnp.sin(phases)
        table_ref[at, 0] = cosine
        table_ref[at, 1] = sine
        x = x_low.astype(f32)
        normed = (x * rms_factor(x)).astype(bf16)
        key = dot_nn(wk_ref[...], normed)
        value = dot_nn(wv_ref[...], normed)
        query = dot_tn(wq_ref[:width, :], normed)
        turned = turn_heads(key, cosine, sine, KV_HEADS, 1.0).astype(bf16)
        value_low = value.astype(bf16)
        for head in range(KV_HEADS):
            kv_ref[at, head] = turned[head * HEAD : (head + 1) * HEAD]
            kv_ref[at, KV_HEADS + head] = value_low[head * HEAD : (head + 1) * HEAD]
        t_ref[at, :RANK] = dot_nn(aq_ref[...], normed).astype(bf16)
        t_ref[at, RANK : 2 * RANK] = key[kv_size:].astype(bf16)
        t_ref[at, 2 * RANK :] = value_low[kv_size:]
        turned = turn_heads(query, cosine, sine, HEADS, HEAD_SCALE).astype(bf16)
        for head in range(HEADS):
            lane = head % GROUP * tokens
            q_ref[at, head // GROUP, :, lane : lane + tokens] = turned[
                head * HEAD : (head + 1) * HEAD
            ]


def entry(rows, place, own, other, pos_own, pos_other, frequency, left, weights, after=()):
    width, size = own.shape[1], own.shape[2]
    tokens = 2 * size
    count = len(rows)
    shapes = [
        ((count, width, tokens), bf16),
        ((count, KV_HEADS, HEAD, GROUP * tokens), bf16),
        ((count, 2 * KV_HEADS, HEAD, tokens), bf16),
        ((count, 3 * RANK, tokens), bf16),
        ((count, 1, tokens), jnp.int32),
        ((count, 2, HEAD // 2, tokens), f32),
    ]
    return call(
        partial(entry_kernel, rows),
        (own, other, pos_own, pos_other, frequency, left, *weights),
        shapes,
        6,
        6 * count,
        scalars=(place,),
        after=after,
    )


def lower_back_kernel(
    place_ref, own_ref, other_ref, wl_ref, cb_ref, dy_ref, dr_ref, dt_ref
):
    rows = other_ref.shape[0]
    outputs = own_ref.shape[1]
    place = read_place(place_ref)
    for row in range(rows):
        pair(place, dy_ref.at[row], own_ref[place[1] * rows + row], other_ref[row])
        dy = dy_ref[row]
        dr_ref[row] = dot_tn(wl_ref[:outputs, :], dy).astype(bf16)
        dt_ref[row] = dot_nn(cb_ref[...], dy).astype(bf16)


def lower_back(place, own, other, weight, scaled, after=()):
    rows, width, size = other.shape
    hidden = weight.shape[1]
    tokens = 2 * size
    shapes = [
        ((rows, width, tokens), bf16),
        ((rows, hidden, tokens), bf16),
        ((rows, RANK, tokens), bf16),
    ]
    return call(
        lower_back_kernel,
        (own, other, weight, scaled),
        shapes,
        8,
        1.9 * rows,
        scalars=(place,),
        after=after,
    )


def write_bias(bias_ref, position, distance):
    size = bias_ref.shape[0]
    key = lax.broadcasted_iota(jnp.int32, (size, size), 0)
    query = lax.broadcasted_iota(jnp.int32, (size, size), 1)
    start = query - position + distance * size
    bias_ref[...] = jnp.where((key >= start) & (key <= query + distance * size), 0.0, MASKED)


def block_distance(chip, step, shards):
    return chip - block_source(chip, step, shards)


def block_source(chip, step, shards):
    if shards & (shards - 1) == 0:
        return jnp.bitwise_xor(chip, step)
    return lax.rem(chip + step, shards)


def needed(chip, first, step, shards, size):
    distance = block_distance(chip, step, shards)
    return (distance > 0) & (distance * size - first < size)


def attend_kernel(at, shards, place_ref, pos_ref, q_ref, *rest):
    kv_refs, rest = rest[:shards], rest[shards:]
    o_ref, lse_ref, bias_ref, max_ref, sum_ref, acc_ref, block_ref = rest
    size = pos_ref.shape[-1]
    chip, _ = read_place(place_ref)
    first = pick(pos_ref[at], 0)

    def visit(kv_ref, opening):
        for head in range(KV_HEADS):
            bias = jnp.concatenate([bias_ref[...]] * GROUP, axis=1)
            logits = dot_tn(kv_ref[head], q_ref[at, head]) + bias
            top = jnp.max(logits, axis=0, keepdims=True)
            if not opening:
                before = max_ref[head]
                top = jnp.maximum(top, before)
            weights = jnp.exp(logits - top)
            total = jnp.sum(weights, axis=0, keepdims=True)
            mixed = dot_nn(kv_ref[head + KV_HEADS], weights.astype(bf16))
            if not opening:
                rescale = jnp.exp(before - top)
                total = total + rescale * sum_ref[head]
                mixed = mixed + rescale * acc_ref[head]
            max_ref[head] = top
            sum_ref[head] = total
            acc_ref[head] = mixed

    write_bias(bias_ref, pos_ref[at], 0)
    visit(kv_refs[0].at[at], True)

    def block_step(step, carry):
        @pl.when(needed(chip, first, step, shards, size))
        def _():
            for which in range(1, shards):

                @pl.when(step == which)
                def _():
                    block_ref[...] = kv_refs[which][at]

            write_bias(bias_ref, pos_ref[at], block_distance(chip, step, shards))
            visit(block_ref, False)

        return carry

    lax.fori_loop(1, shards, block_step, 0)
    total = sum_ref[...]
    o_ref[...] = (acc_ref[...] / total).astype(bf16)
    lse_ref[...] = max_ref[...] + jnp.log(total)


def attend(at, place, position, query, blocks, known, after=()):
    tokens = position.shape[-1]
    stats = (KV_HEADS, 1, GROUP * tokens)
    return call(
        partial(attend_kernel, at, len(blocks)),
        (position, query, *blocks),
        [(query.shape[1:], bf16), (stats, f32)],
        4,
        6 * known,
        scalars=(place,),
        scratch=[
            pltpu.VMEM((tokens, tokens), f32),
            pltpu.VMEM(stats, f32),
            pltpu.VMEM(stats, f32),
            pltpu.VMEM(query.shape[1:], f32),
            pltpu.VMEM(blocks[0].shape[1:], bf16),
        ],
        after=after,
    )


def attend_back_kernel(
    at,
    front,
    shards,
    place_ref,
    pos_ref,
    q_ref,
    do_ref,
    lse_ref,
    delta_ref,
    *rest,
):
    kv_refs, rest = rest[:shards], rest[shards:]
    if front:
        front_refs, rest = rest[: shards - 1], rest[shards - 1 :]
    low_ref, dkv_refs, bias_ref, dq_ref = rest[0], rest[1 : 1 + shards], *rest[1 + shards :]
    if front:
        for come_ref, out_ref in zip(front_refs, dkv_refs[1:]):
            out_ref[:front] = come_ref[...]
    dkv_refs = [dkv_refs[0]] + [ref.at[front] for ref in dkv_refs[1:]]
    size = pos_ref.shape[-1]
    chip, _ = read_place(place_ref)
    first = pick(pos_ref[at], 0)

    def visit(kv_ref, dkv_ref, opening):
        for head in range(KV_HEADS):
            key, value = kv_ref[at, head], kv_ref[at, head + KV_HEADS]
            query, upstream = q_ref[at, head], do_ref[head]
            bias = jnp.concatenate([bias_ref[...]] * GROUP, axis=1)
            probs = jnp.exp(dot_tn(key, query) + bias - lse_ref[head])
            score_grad = (probs * (dot_tn(value, upstream) - delta_ref[head])).astype(bf16)
            query_grad = dot_nn(key, score_grad) * HEAD_SCALE
            if not opening:
                query_grad = query_grad + dq_ref[head]
            dq_ref[head] = query_grad
            dkv_ref[head] = dot_nt(query, score_grad).astype(bf16)
            dkv_ref[head + KV_HEADS] = dot_nt(upstream, probs.astype(bf16)).astype(bf16)

    write_bias(bias_ref, pos_ref[at], 0)
    visit(kv_refs[0], dkv_refs[0], True)
    for step in range(1, shards):
        wanted = needed(chip, first, step, shards, size)

        @pl.when(wanted)
        def _():
            write_bias(bias_ref, pos_ref[at], block_distance(chip, step, shards))
            visit(kv_refs[step], dkv_refs[step], False)

        @pl.when(jnp.logical_not(wanted))
        def _():
            dkv_refs[step][...] = jnp.zeros(dkv_refs[step].shape, bf16)

    low_ref[...] = dq_ref[...].astype(bf16)


def attend_back(
    at, place, position, query, upstream, lse, delta, blocks, front, known, after=()
):
    tokens = position.shape[-1]
    count = front[0].shape[0] if front else 0
    piece = blocks[0].shape[1:]
    return call(
        partial(attend_back_kernel, at, count, len(blocks)),
        (position, query, upstream, lse, delta, *blocks, *front),
        [(query.shape[1:], bf16), (piece, bf16)] + [((count + 1,) + piece, bf16)] * (len(blocks) - 1),
        4,
        9 * known,
        scalars=(place,),
        scratch=[pltpu.VMEM((tokens, tokens), f32), pltpu.VMEM(query.shape[1:], f32)],
        after=after,
    )


def spread_heads(ref):
    tokens = ref.shape[-1] // GROUP
    return jnp.concatenate(
        [
            ref[head // GROUP, :, head % GROUP * tokens : (head % GROUP + 1) * tokens]
            for head in range(HEADS)
        ],
        axis=0,
    )


def middle_kernel(
    row,
    at,
    x_ref,
    dy_ref,
    dr_ref,
    dtl_ref,
    o_ref,
    ao_ref,
    ag_ref,
    au_ref,
    wo,
    wg,
    wu,
    wl,
    halves_ref,
    dx1_ref,
    do_ref,
    delta_ref,
    dao_ref,
    dbo_ref,
    dag_ref,
    dau_ref,
    dbg_ref,
    dbu_ref,
    dal_ref,
    dbl_ref,
    so_ref,
    sg_ref,
    su_ref,
    sl_ref,
    act,
    dgate,
    dupper,
):
    _, width, tokens = x_ref.shape
    hidden = act.shape[0]
    mixed = spread_heads(o_ref)
    attn = dot_tn(wo[:width, :], mixed)
    x1 = x_ref[at].astype(f32) + attn
    rho = rms_factor(x1)
    normed = x1 * rho
    normed_low = normed.astype(bf16)
    t_output = dot_nn(ao_ref[...], mixed).astype(bf16)
    both = jnp.concatenate([ag_ref[...], au_ref[...]], axis=0)
    both = dot_nn(both, normed_low).astype(bf16)
    t_gate, t_upper = both[:RANK], both[RANK:]
    step = 256
    for start in range(0, hidden, step):
        rows = slice(start, start + step)
        gate = dot_tn(wg[:width, rows], normed_low)
        upper = dot_tn(wu[:width, rows], normed_low)
        down = dr_ref[row, rows, :].astype(f32)
        sigmoid = 0.5 + 0.5 * jnp.tanh(0.5 * gate)
        silu = gate * sigmoid
        act[rows, :] = (silu * upper).astype(bf16)
        gate_grad = down * upper * (sigmoid + silu * (1.0 - sigmoid))
        upper_grad = down * silu
        dgate[rows, :] = gate_grad.astype(bf16)
        dupper[rows, :] = upper_grad.astype(bf16)
        sg_ref[:, rows] = column_to_row(jnp.sum(gate * gate_grad, axis=1, keepdims=True))
        su_ref[:, rows] = column_to_row(jnp.sum(upper * upper_grad, axis=1, keepdims=True))
    lower_all = dot_nn(wl[...], act[...])
    dal_ref[...] = dot_nt(dtl_ref[row], act[...])
    dbg_ref[...] = dot_nt(t_gate, dgate[...])
    dbu_ref[...] = dot_nt(t_upper, dupper[...])
    lower = lower_all[:width]
    t_lower = lower_all[width:].astype(bf16)
    out = (x1 + lower).astype(bf16)
    halves_ref[0] = out[:, : tokens // 2]
    halves_ref[1] = out[:, tokens // 2 :]
    dy_low = dy_ref[row]
    dy = dy_low.astype(f32)
    sl_ref[...] = column_to_row(jnp.sum(lower * dy, axis=1, keepdims=True))
    gate_back = dot_nn(wg[...], dgate[...])
    upper_back = dot_nn(wu[...], dupper[...])
    dt_gate = gate_back[width:].astype(bf16)
    dt_upper = upper_back[width:].astype(bf16)
    dbl_ref[...] = dot_nt(t_lower, dy_low)
    both = dot_nt(jnp.concatenate([dt_gate, dt_upper], axis=0), normed_low)
    dag_ref[...] = both[:RANK]
    dau_ref[...] = both[RANK:]
    dnormed = gate_back[:width] + upper_back[:width]
    dx1 = dy + rho * (dnormed - normed * jnp.mean(dnormed * normed, axis=0, keepdims=True))
    dx1_low = dx1.astype(bf16)
    dx1_ref[...] = dx1_low
    so_ref[...] = column_to_row(jnp.sum(attn * dx1, axis=1, keepdims=True))
    output_back = dot_nn(wo[...], dx1_low)
    dt_output = output_back[width:].astype(bf16)
    dao_ref[...] = dot_nt(dt_output, mixed)
    dbo_ref[...] = dot_nt(t_output, dx1_low)
    dmixed = output_back[:width].astype(bf16)
    weighted = dmixed.astype(f32) * mixed.astype(f32)
    for head in range(HEADS):
        rows = slice(head * HEAD, (head + 1) * HEAD)
        lanes = slice(head % GROUP * tokens, (head % GROUP + 1) * tokens)
        do_ref[head // GROUP, :, lanes] = dmixed[rows]
        delta_ref[head // GROUP, :, lanes] = jnp.sum(weighted[rows], axis=0, keepdims=True)


def middle(row, at, x, dy, dr, dt_lower, mixed, lefts, weights, known, after=()):
    _, width, tokens = x.shape
    hidden = dr.shape[1]
    shapes = [
        ((2, width, tokens // 2), bf16),
        ((width, tokens), bf16),
        (mixed.shape, bf16),
        ((KV_HEADS, 1, GROUP * tokens), f32),
        ((RANK, width), f32),
        ((RANK, width), f32),
        ((RANK, width), f32),
        ((RANK, width), f32),
        ((RANK, hidden), f32),
        ((RANK, hidden), f32),
        ((RANK, hidden), f32),
        ((RANK, width), f32),
        ((1, width), f32),
        ((1, hidden), f32),
        ((1, hidden), f32),
        ((1, width), f32),
    ]
    return call(
        partial(middle_kernel, row, at),
        (x, dy, dr, dt_lower, mixed, *lefts, *weights),
        shapes,
        14,
        13 * known,
        scratch=[pltpu.VMEM((hidden, tokens), bf16)] * 3,
        after=after,
    )


def exit_kernel(at, piece, shards, *refs):
    (x_ref, table_ref, dx1_ref, t_ref, q_ref, kv_ref, dq_ref, wq_ref, wk_ref, wv_ref) = refs[:10]
    cbk_ref, cbv_ref = refs[10:12]
    dkv_refs = refs[12 : 12 + shards]
    halves_ref, da_ref, dbq_ref, dbkv_ref, sq_ref, skv_ref = refs[12 + shards :]
    _, width, tokens = x_ref.shape
    kv_size = KV_HEADS * HEAD
    x = x_ref[at].astype(f32)
    rho = rms_factor(x)
    normed = x * rho
    normed_low = normed.astype(bf16)
    cosine = table_ref[at, 0]
    sine = table_ref[at, 1]
    dquery = turn_heads_back(spread_heads(dq_ref).astype(f32), cosine, sine, HEADS, 1.0)
    query = turn_heads_back(
        spread_heads(q_ref.at[at]).astype(f32), cosine, sine, HEADS, 1.0 / HEAD_SCALE
    )
    sq_ref[...] = column_to_row(jnp.sum(query * dquery, axis=1, keepdims=True))
    dquery = dquery.astype(bf16)
    query_back = dot_nn(wq_ref[...], dquery)
    dkv = dkv_refs[0][...].astype(f32)
    for ref in dkv_refs[1:]:
        dkv = dkv + ref[piece].astype(f32)
    dkv = dkv.reshape(2 * kv_size, tokens)
    key_value = kv_ref[at].astype(f32).reshape(2 * kv_size, tokens)
    dkey = turn_heads_back(dkv[:kv_size], cosine, sine, KV_HEADS, 1.0)
    dvalue = dkv[kv_size:]
    key = turn_heads_back(key_value[:kv_size], cosine, sine, KV_HEADS, 1.0)
    value = key_value[kv_size:]
    skv_ref[0:1, :] = column_to_row(jnp.sum(key * dkey, axis=1, keepdims=True))
    skv_ref[1:2, :] = column_to_row(jnp.sum(value * dvalue, axis=1, keepdims=True))
    dkey = dkey.astype(bf16)
    dvalue = dvalue.astype(bf16)
    dnormed = (
        query_back[:width]
        + dot_tn(wk_ref[:kv_size, :], dkey)
        + dot_tn(wv_ref[:kv_size, :], dvalue)
    )
    dx = dx1_ref[...].astype(f32) + rho * (dnormed - normed * jnp.mean(dnormed * normed, axis=0, keepdims=True))
    dx = dx.astype(bf16)
    halves_ref[0] = dx[:, : tokens // 2]
    halves_ref[1] = dx[:, tokens // 2 :]
    dt = jnp.concatenate(
        [query_back[width:], dot_nn(cbk_ref[...], dkey), dot_nn(cbv_ref[...], dvalue)], axis=0
    ).astype(bf16)
    da_ref[...] = dot_nt(dt, normed_low)
    dbq_ref[...] = dot_nt(t_ref[at, :RANK], dquery)
    dbkv_ref[0] = dot_nt(t_ref[at, RANK : 2 * RANK], dkey)
    dbkv_ref[1] = dot_nt(t_ref[at, 2 * RANK :], dvalue)


def leave(at, piece, x, table, dx1, inner, query, key_value, dquery, weights, scaled, dkvs, after=()):
    _, width, tokens = x.shape
    q_size, kv_size = HEADS * HEAD, KV_HEADS * HEAD
    shapes = [
        ((2, width, tokens // 2), bf16),
        ((3 * RANK, width), f32),
        ((RANK, q_size), f32),
        ((2, RANK, kv_size), f32),
        ((1, q_size), f32),
        ((2, kv_size), f32),
    ]
    return call(
        partial(exit_kernel, at, piece, len(dkvs)),
        (x, table, dx1, inner, query, key_value, dquery, *weights, *scaled, *dkvs),
        shapes,
        7,
        3,
        after=after,
    )


def settle(sums, weight, turned, left, right, norm, magnitude):
    left_sum, right_sum, stat = sums
    magnitude = magnitude.reshape(1, -1)
    factor = -stat / (magnitude * norm)
    scaled = (ADAPTER_SCALE * factor * right.astype(f32)).astype(bf16)
    if turned:
        left_more = dot_nn(scaled, weight)
        product = dot_nt(left, weight)
    else:
        left_more = dot_nt(scaled, weight)
        product = dot_nn(left, weight)
    right_total = ADAPTER_SCALE * (right_sum * (magnitude / norm) + factor * product)
    return (left_sum + left_more, right_total, stat / magnitude)


STAT = 512


def put_stat(ref, half, row, lane, values):
    size = values.shape[1]
    for start in range(0, size, STAT):
        take = min(STAT, size - start)
        ref[half, row : row + 1, lane : lane + take] = values[:, start : start + take]
        row += 1
    return row


def stack_sum(refs):
    total = refs[0][...]
    for ref in refs[1:]:
        total = total + ref[...]
    return total


def settle_middle_kernel(rows, shards, *refs):
    sums = [
        stack_sum([refs[row * 12 + which] for row in range(rows)]) for which in range(12)
    ]
    refs = refs[rows * 12 :]
    names = ("output", "gate", "upper", "lower")
    groups = {}
    for which, name in enumerate(names):
        groups[name] = [ref for ref in refs[which * 5 : which * 5 + 5]]
    out, pack = refs[20:]
    dao, dbo, dag, dau, dbg, dbu, dal, dbl, so, sg, su, sl = sums
    pieces = {
        "output": (dao, dbo, so),
        "gate": (dag, dbg, sg),
        "upper": (dau, dbu, su),
        "lower": (dal, dbl, sl),
    }
    done = {}
    for name in names:
        weight, left, right, norm, magnitude = groups[name]
        done[name] = settle(
            pieces[name],
            weight[: weight.shape[0] - RANK, :],
            name == "lower",
            left[...],
            right[...],
            norm[...],
            magnitude[...],
        )
    width = dao.shape[1]
    slot, hidden = slots(width), dbg.shape[1]
    pack[...] = jnp.zeros(pack.shape, f32)
    pack[0, :, 0:hidden] = done["gate"][1]
    pack[0, :, hidden : 2 * hidden] = done["upper"][1]
    pack[0, :, 2 * hidden : 2 * hidden + width] = done["output"][0]
    row = 0
    for name in ("gate", "upper", "output", "lower"):
        row = put_stat(pack, 0, row, 2 * hidden + slot, done[name][2])
    pack[1, :, 0:hidden] = done["lower"][0]
    place = hidden
    for values in (done["output"][1], done["gate"][0], done["upper"][0], done["lower"][1]):
        pack[1, :, place : place + width] = values
        place += slot
    cut(out, pack, shards)


def slots(width):
    return -(-width // 128) * 128


def piece_of(half, shards):
    return slots(-(-half // shards))


def cut(out, pack, shards):
    piece = out.shape[-1]
    for half in range(2):
        for shard in range(shards):
            out[half, shard] = pack[half, :, shard * piece : (shard + 1) * piece]


def settle_middle(partials, projections, shards, after=()):
    hidden = partials[0][4].shape[1]
    width = partials[0][0].shape[1]
    piece = piece_of(2 * hidden + slots(width) + STAT, shards)
    flat = [a for part in partials for a in part] + [a for group in projections for a in group]
    return call(
        partial(settle_middle_kernel, len(partials), shards),
        flat,
        [((2, shards, RANK, piece), f32)],
        5,
        6,
        scratch=[pltpu.VMEM((2, RANK, shards * piece), f32)],
        after=after,
    )[0]


def settle_entry_kernel(rows, shards, place_ref, middle_ref, *refs):
    sums = [stack_sum([refs[row * 5 + which] for row in range(rows)]) for which in range(5)]
    refs = refs[rows * 5 :]
    da, dbq, dbkv, sq, skv = sums
    keep_ref, send_ref, pack = refs[15:]
    pieces = (
        (da[:RANK], dbq, sq),
        (da[RANK : 2 * RANK], dbkv[0], skv[0:1]),
        (da[2 * RANK :], dbkv[1], skv[1:2]),
    )
    done = []
    for which in range(3):
        weight, left, right, norm, magnitude = refs[which * 5 : which * 5 + 5]
        done.append(
            settle(
                pieces[which],
                weight[: weight.shape[0] - RANK, :],
                which > 0,
                left[...],
                right[...],
                norm[...],
                magnitude[...],
            )
        )
    width = da.shape[1]
    slot = slots(width)
    kv_size = skv.shape[1]
    pack[...] = jnp.zeros(pack.shape, f32)
    pack[0, :, 0:width] = done[0][0]
    pack[0, :, slot : slot + width] = done[1][0]
    row = 0
    for which in range(3):
        row = put_stat(pack, 0, row, 2 * slot, done[which][2])
    pack[1, :, 0:width] = done[2][0]
    pack[1, :, slot : slot + sq.shape[1]] = done[0][1]
    pack[1, :, 2 * slot : 2 * slot + 2 * kv_size] = jnp.concatenate(
        [done[1][1], done[2][1]], axis=1
    )
    here = read_place(place_ref)[1] == 0
    middle_piece = middle_ref.shape[-1]
    piece = pack.shape[-1] // shards
    for shard in range(shards):
        place = slice(shard * piece, (shard + 1) * piece)
        parts = (
            (slice(0, middle_piece), middle_ref[0, shard], middle_ref[1, shard]),
            (slice(middle_piece, middle_piece + piece), pack[0, :, place], pack[1, :, place]),
        )
        for lanes, first, second in parts:
            keep_ref[shard, :, lanes] = jnp.where(here, first, second)
            send_ref[shard, :, lanes] = jnp.where(here, second, first).astype(bf16)


def settle_entry(place, middle_pack, partials, projections):
    shards = middle_pack.shape[1]
    width = partials[0][0].shape[1]
    kv_size = partials[0][4].shape[1]
    piece = piece_of(2 * slots(width) + max(STAT, slots(2 * kv_size)), shards)
    flat = [a for part in partials for a in part] + [a for group in projections for a in group]
    shape = (shards, RANK, middle_pack.shape[-1] + piece)
    return call(
        partial(settle_entry_kernel, len(partials), shards),
        [middle_pack] + flat,
        [(shape, f32), (shape, bf16)],
        5,
        2,
        scalars=(place,),
        scratch=[pltpu.VMEM((2, RANK, shards * piece), f32)],
    )


def get_stat(value, row, lane, size):
    parts = []
    for start in range(0, size, STAT):
        take = min(STAT, size - start)
        parts.append(value[row : row + 1, lane : lane + take])
        row += 1
    return jnp.concatenate(parts, axis=1) if len(parts) > 1 else parts[0], row


def finish_kernel(width, hidden, kv_size, shards, middle_piece, place_ref, *refs):
    mine_ref, other_ref = refs[:2]
    lefts, rights, stats = refs[2:9], refs[9:16], refs[16:23]
    middle_held, entry_held = refs[23:]
    chip, core = read_place(place_ref)
    piece = mine_ref.shape[-1] - middle_piece
    for half in range(2):
        for step in range(shards):
            value = jnp.where(core == half, mine_ref[step], other_ref[step]).astype(f32)
            source = block_source(chip, step, shards)
            lane = pl.multiple_of(source * middle_piece, 128)
            middle_held[half, :, pl.ds(lane, middle_piece)] = value[:, :middle_piece]
            lane = pl.multiple_of(source * piece, 128)
            entry_held[half, :, pl.ds(lane, piece)] = value[:, middle_piece:]
    slot = slots(width)
    m0, m1, e0, e1 = middle_held.at[0], middle_held.at[1], entry_held.at[0], entry_held.at[1]
    rights[4][...] = m0[:, :hidden]
    rights[5][...] = m0[:, hidden : 2 * hidden]
    lefts[3][...] = m0[:, 2 * hidden : 2 * hidden + width]
    row = 0
    for which, size in ((4, hidden), (5, hidden), (3, width), (6, width)):
        value, row = get_stat(m0, row, 2 * hidden + slot, size)
        stats[which][...] = value[0]
    lefts[6][...] = m1[:, :hidden]
    for place, ref in enumerate((rights[3], lefts[4], lefts[5], rights[6])):
        ref[...] = m1[:, hidden + place * slot : hidden + place * slot + width]
    lefts[0][...] = e0[:, :width]
    lefts[1][...] = e0[:, slot : slot + width]
    row = 0
    for which, size in ((0, width), (1, kv_size), (2, kv_size)):
        value, row = get_stat(e0, row, 2 * slot, size)
        stats[which][...] = value[0]
    lefts[2][...] = e1[:, :width]
    rights[0][...] = e1[:, slot : slot + width]
    both = e1[:, 2 * slot : 2 * slot + 2 * kv_size]
    rights[1][...] = both[:, :kv_size]
    rights[2][...] = both[:, kv_size:]


def finish(place, middle_piece, sums, lefts, rights, magnitudes):
    shards = sums[0].shape[0]
    shapes = [a.shape for a in lefts] + [a.shape for a in rights] + [a.shape for a in magnitudes]
    sizes = (lefts[0].shape[1], rights[4].shape[1], rights[1].shape[1])
    return call(
        partial(finish_kernel, *sizes, shards, middle_piece),
        sums,
        [(shape, f32) for shape in shapes],
        5,
        2,
        scalars=(place,),
        scratch=[
            pltpu.VMEM((2, RANK, shards * piece), f32)
            for piece in (middle_piece, sums[0].shape[-1] - middle_piece)
        ],
    )


def to_other_core(value):
    size = lax.axis_size("seq")
    return lax.ppermute(value, "seq", [(i, i ^ 1) for i in range(size)])


def peer(index, step, count):
    return index ^ step if count & (count - 1) == 0 else (index + step) % count


def to_chip(value, step, needed=False):
    size = lax.axis_size("seq")
    count = size // 2
    pairs = [(peer(c, step, count), c) for c in range(count)]
    pairs = [(a, c) for a, c in pairs if a < c or not needed]
    return lax.ppermute(value, "seq", [(2 * a + k, 2 * c + k) for a, c in pairs for k in (0, 1)])


def back_to_chip(value, step, needed=False):
    size = lax.axis_size("seq")
    count = size // 2
    pairs = [(c, peer(c, step, count)) for c in range(count)]
    pairs = [(c, a) for c, a in pairs if a < c or not needed]
    return lax.ppermute(value, "seq", [(2 * c + k, 2 * a + k) for c, a in pairs for k in (0, 1)])


def to_batch(value, step):
    count = lax.axis_size("batch")
    return lax.ppermute(value, "batch", [(b, peer(b, step, count)) for b in range(count)])


def share_kernel(place_ref, keep_ref, come_ref, own_ref, *out_refs):
    chip, _ = read_place(place_ref)
    shards = come_ref.shape[0]
    own_ref[...] = keep_ref[chip] + come_ref[chip].astype(f32)
    for step, ref in enumerate(out_refs, start=1):
        other = block_source(chip, step, shards)
        ref[...] = (keep_ref[other] + come_ref[other].astype(f32)).astype(bf16)


def sum_kernel(own_ref, *refs):
    *come_refs, total_ref, low_ref = refs
    total = own_ref[...]
    for ref in come_refs:
        total = total + ref[...].astype(f32)
    total_ref[...] = total
    low_ref[...] = total.astype(bf16)


def cross_core(place, keep, send):
    shards = keep.shape[0]
    piece = keep.shape[1:]
    own, *parts = call(
        share_kernel,
        (keep, to_other_core(send)),
        [(piece, f32)] + [(piece, bf16)] * (shards - 1),
        4,
        1,
        scalars=(place,),
    )
    return own, parts


def add_up(own, come, after=()):
    return call(
        sum_kernel, (own, *come), [(own.shape, f32), (own.shape, bf16)], 4, 1, after=after
    )


def cross_chips(own, parts, after=()):
    come = [back_to_chip(part, step) for step, part in enumerate(parts, start=1)]
    return add_up(own, come, after)


def cross_batch(sums, after=()):
    own, low = sums
    count = lax.axis_size("batch")
    return add_up(own, [to_batch(low, step) for step in range(1, count)], after)


def spread(sums, shards):
    low = sums[1]
    mine = jnp.stack([low] + [to_chip(low, step) for step in range(1, shards)])
    return mine, to_other_core(mine)


def leave_half_kernel(skipped, *refs):
    place_ref, value_ref, out_ref, sem = refs[skipped:]
    _, core = read_place(place_ref)
    half = out_ref.shape[0]
    copy = pltpu.make_async_copy(value_ref.at[pl.ds((1 - core) * half, half)], out_ref, sem)
    copy.start()
    copy.wait()


def leave_half(place, value, microseconds, after=()):
    half = value.shape[0] // 2
    anywhere = pl.BlockSpec(memory_space=pl.ANY)
    return pl.pallas_call(
        partial(leave_half_kernel, len(after)),
        in_specs=[anywhere] * len(after) + [vmem(), anywhere],
        out_specs=vmem(),
        out_shape=jax.ShapeDtypeStruct((half,) + value.shape[1:], value.dtype),
        scratch_shapes=[pltpu.SemaphoreType.DMA],
        compiler_params=pltpu.CompilerParams(vmem_limit_bytes=2**20),
        cost_estimate=pl.CostEstimate(
            flops=int(microseconds * 1.1e9), bytes_accessed=1, transcendentals=0
        ),
    )(*after, place, value)


def other_half(value, core):
    half = value.shape[0] // 2
    return to_other_core(lax.dynamic_slice_in_dim(value, (1 - core) * half, half, 0))


def other_halves_kernel(rows, skipped, *refs):
    place_ref, *half_refs = refs[skipped : skipped + 1 + rows]
    out_ref, sems = refs[-2:]
    _, core = read_place(place_ref)
    copies = [
        pltpu.make_async_copy(ref.at[1 - core], out_ref.at[row], sems.at[row])
        for row, ref in enumerate(half_refs)
    ]
    for copy in copies:
        copy.start()
    for copy in copies:
        copy.wait()


def other_halves(place, halves, after):
    rows = len(halves)
    anywhere = pl.BlockSpec(memory_space=pl.ANY)
    return pl.pallas_call(
        partial(other_halves_kernel, rows, len(after)),
        in_specs=[anywhere] * len(after) + [vmem()] + [anywhere] * rows,
        out_specs=anywhere,
        out_shape=jax.ShapeDtypeStruct((rows,) + halves[0].shape[1:], halves[0].dtype),
        scratch_shapes=[pltpu.SemaphoreType.DMA((rows,))],
        compiler_params=pltpu.CompilerParams(vmem_limit_bytes=2**20),
        cost_estimate=pl.CostEstimate(flops=10**9, bytes_accessed=1, transcendentals=0),
    )(*after, place, *halves)


def assemble_kernel(rows, offset, skipped, *refs):
    place_ref = refs[skipped]
    keep_refs = refs[skipped + 1 : skipped + 1 + rows]
    other_refs = refs[skipped + 1 + rows : -3]
    other_refs = [other_refs[0].at[offset + row] for row in range(rows)]
    out_ref, flag_ref, sems = refs[-3:]
    _, core = read_place(place_ref)
    copies = []
    for row in range(rows):
        for side, (source, place) in enumerate(
            (
                (keep_refs[row].at[core], core * rows + row),
                (other_refs[row], (1 - core) * rows + row),
            )
        ):
            copies.append(pltpu.make_async_copy(source, out_ref.at[place], sems.at[side, row]))
    for copy in copies:
        copy.start()
    flag_ref[...] = jnp.zeros(flag_ref.shape, f32)
    for copy in copies:
        copy.wait()


def assemble(place, keeps, others, offset, after=()):
    rows = len(keeps)
    anywhere = pl.BlockSpec(memory_space=pl.ANY)
    return pl.pallas_call(
        partial(assemble_kernel, rows, offset, len(after)),
        in_specs=[anywhere] * len(after) + [vmem()] + [anywhere] * (rows + 1),
        out_specs=[anywhere, vmem()],
        out_shape=[
            jax.ShapeDtypeStruct((2 * rows,) + keeps[0].shape[1:], keeps[0].dtype),
            jax.ShapeDtypeStruct((8, 128), f32),
        ],
        scratch_shapes=[pltpu.SemaphoreType.DMA((2, rows))],
        compiler_params=pltpu.CompilerParams(vmem_limit_bytes=2**20),
        cost_estimate=pl.CostEstimate(flops=10**9, bytes_accessed=1, transcendentals=0),
    )(*after, place, *keeps, others)


def body(tokens, segment_ids, position_ids, cotangent, *weights):
    bases, lefts, rights, magnitudes = (
        weights[:7],
        [a.T for a in weights[7:14]],
        weights[14:21],
        weights[21:28],
    )
    turned = (False, True, True, False, False, False, True)
    bases = [w.T if turn else w for w, turn in zip(bases, turned)]
    index = lax.axis_index("seq")
    core, chip = index % 2, index // 2
    shards = lax.axis_size("seq") // 2
    lanes = lax.broadcasted_iota(jnp.int32, (1, 128), 1)
    place = jnp.where(lanes == 0, chip, jnp.where(lanes == 1, core, 0)).astype(jnp.int32)
    x = jnp.swapaxes(tokens, 1, 2)
    dy = jnp.swapaxes(cotangent, 1, 2)
    pos_other = other_half(position_ids, core)
    x_other = to_other_core(leave_half(place, x, 12))
    rows = x_other.shape[0]
    half_head = HEAD // 2
    frequency = ROTARY_BASE ** (-(jnp.arange(half_head, dtype=f32) * 2.0 / HEAD))[:, None]

    def ready_for(which, after=()):
        return prepare(
            bases[which], lefts[which], rights[which], magnitudes[which], turned[which], after
        )

    ready = prepare_first(
        [(bases[which], lefts[which], rights[which], magnitudes[which]) for which in range(3)]
    )
    first_weights = [ready[which][0] for which in range(3)]
    groups = [(0,), tuple(range(1, rows))]
    entries, gathered, where = [], [], {}
    last = ()
    for number, group in enumerate(groups):
        results = entry(
            group,
            place,
            x,
            x_other,
            position_ids,
            pos_other,
            frequency,
            lefts[0],
            first_weights,
            last,
        )
        entries.append(results)
        own = results[2]
        gathered.append([own] + [to_chip(own, step) for step in range(1, shards)])
        where.update({row: (number, at) for at, row in enumerate(group)})
        if number == 0:
            started = (results[3],)
            for which in (6, 3, 4, 5):
                ready[which] = ready_for(which, started)
            last = [ready[which][1] for which in (6, 3, 4, 5)]
    dy_other = to_other_core(leave_half(place, dy, 1, (ready[0][1],)))
    dy, dr, dt_lower = lower_back(
        place, dy, dy_other, ready[6][0], ready[6][2], (entries[-1][3],)
    )
    last = (mark((dt_lower, *gathered[0])),)
    keeps, middles, backs, waiting, sent = [], [], [], (), ()
    for row in range(rows):
        number, at = where[row]
        x_rows, query, _, _, position, _ = entries[number]
        known = 1.0
        mixed, lse = attend(at, place, position, query, gathered[number], known, last)
        halves, dx1, upstream, delta, *sums = middle(
            row,
            at,
            x_rows,
            dy,
            dr,
            dt_lower,
            mixed,
            lefts[3:6],
            [ready[which][0] for which in (3, 4, 5, 6)],
            known,
        )
        keeps.append(halves)
        middles.append(sums)
        together = row == rows - 2
        dquery, own, *dkvs = attend_back(
            at,
            place,
            position,
            query,
            upstream,
            lse,
            delta,
            gathered[number],
            waiting if row < rows - 1 else (),
            known,
            sent[:-1] if row == rows - 1 else (),
        )
        last = (dquery,)
        if row < rows - 2:
            waiting = dkvs
            backs.append([dx1, dquery, own])
            continue
        if row == rows - 1:
            last = (dquery, *sent[-1:])
        if together:
            sent = [back_to_chip(part, step, True) for step, part in enumerate(dkvs[:-1], start=1)]
            part = hold(dkvs[-1], sent) if sent else dkvs[-1]
            dkvs = sent + [back_to_chip(part, shards - 1, True)]
            sent = dkvs
        else:
            dkvs = [back_to_chip(part, step, True) for step, part in enumerate(dkvs, start=1)]
        backs.append([dx1, dquery, own])
        first_row = 0 if together else row
        for back_row in range(first_row, row + 1):
            backs[back_row] += [back_row - first_row, dkvs]

    def group_of(which):
        return (ready[which][0], lefts[which], rights[which], ready[which][1], magnitudes[which])

    exits = []

    def go_out(row, after):
        number, at = where[row]
        x_rows, query, key_value, inner, _, table = entries[number]
        dx1, dquery, own, piece, dkvs = backs[row]
        exits.append(
            leave(
                at,
                piece,
                x_rows,
                table,
                dx1,
                inner,
                query,
                key_value,
                dquery,
                first_weights,
                (ready[1][2], ready[2][2]),
                [own] + dkvs,
                after,
            )
        )

    for row in range(rows - 1):
        go_out(row, last)
    middle_pack = settle_middle(
        middles, [group_of(which) for which in (3, 4, 5, 6)], shards, last
    )
    go_out(rows - 1, (middle_pack, *[e[1] for e in exits]))
    keep, send = settle_entry(
        place, middle_pack, [e[1:] for e in exits], [group_of(which) for which in (0, 1, 2)]
    )
    own, parts = cross_core(place, keep, send)
    sums = cross_chips(own, parts)
    ends = [e[0] for e in exits]
    others = to_other_core(other_halves(place, keeps + ends, (sums[1],)))
    layer_out, flag = assemble(place, keeps, others, 0)
    tokens_grad, more = assemble(place, ends, others, rows)
    sums = cross_batch(sums, (flag, more))
    finals = finish(
        place, middle_pack.shape[-1], spread(sums, shards), lefts, rights, magnitudes
    )
    return (
        jnp.swapaxes(layer_out, 1, 2),
        jnp.swapaxes(tokens_grad, 1, 2),
        *[a.T for a in finals[:7]],
        *finals[7:],
    )


def solution(mesh):
    split = P("batch", "seq", None)
    return jax.shard_map(
        body,
        mesh=mesh,
        in_specs=(split, P("batch", "seq"), P("batch", "seq"), split) + (P(),) * 28,
        out_specs=(split, split) + (P(),) * 21,
        check_vma=False,
    )
```
